256 devices in a mesh: off: 32 (over x_lo, z, core), mid: 8 (over y, x_hi).
Axes of the slice: x: 4 (x_hi: 2, x_lo: 2; x = x_hi * 2 + x_lo), y: 4, z: 8, core: 2. Of those that a mesh axis runs over, the one named last changes fastest.
Arguments:
- tokens: bfloat16 [256, 256, 768], P('off', 'mid'), may hold values from -6 to 6
- cotangent: bfloat16 [256, 256, 768], P('off', 'mid'), may hold values from -6 to 6
- mask: int32 [256, 256], replicated, may hold values 0 or 1
- w_offset: bfloat16 [768, 3072], replicated, may hold values from -0.21875 to 0.21875
- w_midpoint: bfloat16 [768, 3072], replicated, may hold values from -0.21875 to 0.21875
Outputs:
- grad_tokens: bfloat16 [256, 256, 768], P('off', 'mid')
- grad_offset_weights: float32 [768, 3072], P(None, ('off', 'mid'))
- grad_midpoint_weights: float32 [768, 3072], P(None, ('off', 'mid'))
The draws below stay inside these ranges and needn't reach their ends.
All inputs are finite; a program needn't handle non-finite values.
Results may differ from the reference program's by a relative error of at most 0.02.
Values may be sent and summed in bfloat16 or wider, within the bound.
No kernel may reach another device: no remote copies, remote signals or barrier semaphores. Data moves between devices by JAX's collectives and lax.ppermute only.
A program may use at most 128 MiB of HBM per device.

```python
import math
import jax
import jax.numpy as jnp
from jax import lax

D = 768
HEADS = 12
OFFSETS = 256
MIDPOINTS = 256


def plant(entries, rng, smallest, largest):
    spot = [jax.random.randint(jax.random.fold_in(rng, axis), (), 0, length) for axis, length in enumerate(entries.shape)]
    widest = entries.shape.index(max(entries.shape))
    neighbour = spot[:widest] + [(spot[widest] + 1) % entries.shape[widest]] + spot[widest + 1:]
    return entries.at[tuple(spot)].set(smallest).at[tuple(neighbour)].set(largest)


def shard_levels(key, extent, cuts, smallest, largest):
    def one(position, parts):
        steps = jax.random.uniform(jax.random.fold_in(jax.random.fold_in(key, 6), position), (parts,), jnp.float32, smallest / len(cuts), largest / len(cuts))
        return jnp.repeat(jnp.exp(steps), extent[position] // parts).reshape((-1,) + (1,) * (len(extent) - position - 1))

    factor_of = one(*cuts[0])
    for cut in cuts[1:]:
        factor_of = factor_of * one(*cut)
    return factor_of


def centred(rng, extent, scale, limit, pieces=(), held_as=jnp.bfloat16):
    values = scale * jax.random.normal(rng, extent, jnp.float32)
    if pieces:
        values = values * shard_levels(rng, extent, pieces, -0.22, 0.18)
    return jnp.clip(values, -limit, limit).astype(held_as)


def setup_inputs(seed: int = 0) -> dict:
    splits = jax.random.split(jax.random.key(seed), 6)
    tokens = centred(splits[0], (OFFSETS, MIDPOINTS, D), 1.0, 6.0, ((0, 32), (1, 8)))
    cotangent = centred(splits[1], (OFFSETS, MIDPOINTS, D), 1.0, 6.0, ((0, 32), (1, 8)))
    mask = plant((jax.random.randint(splits[2], (OFFSETS, MIDPOINTS), 0, 4) < 3).astype(jnp.int32), jax.random.fold_in(splits[2], 1), 0, 1)
    w_offset = centred(splits[3], (D, 4 * D), D ** -0.5, 0.21875)
    w_midpoint = centred(splits[4], (D, 4 * D), D ** -0.5, 0.21875)
    return dict(tokens=tokens, cotangent=cotangent, mask=mask, w_offset=w_offset, w_midpoint=w_midpoint)


EPSILON = 1e-05
NEGATIVE = -1e+30

def lower(tensor):
    return lax.optimization_barrier(tensor.astype(jnp.bfloat16))

def normalize(values):
    widened = values.astype(jnp.float32)
    center = lax.optimization_barrier(jnp.mean(widened, axis=-1, keepdims=True))
    spread = lax.optimization_barrier(jnp.mean(jnp.square(widened - center), axis=-1, keepdims=True))
    return lower((widened - center) * lax.rsqrt(spread + EPSILON))

def normalize_grad(values, upstream):
    widened = values.astype(jnp.float32)
    center = lax.optimization_barrier(jnp.mean(widened, axis=-1, keepdims=True))
    spread = lax.optimization_barrier(jnp.mean(jnp.square(widened - center), axis=-1, keepdims=True))
    inverse = lax.rsqrt(spread + EPSILON)
    scaled = (widened - center) * inverse
    incoming = upstream.astype(jnp.float32)
    return inverse * (incoming - lax.optimization_barrier(jnp.mean(incoming, axis=-1, keepdims=True)) - scaled * lax.optimization_barrier(jnp.mean(incoming * scaled, axis=-1, keepdims=True)))

def split_heads(tensor):
    sequences, length, features = tensor.shape
    return tensor.reshape(sequences, length, HEADS, features // HEADS).astype(jnp.float32)

def attention_state(normed, weight, live):
    sequences, length, features = normed.shape
    projected = lower(jnp.dot(normed.reshape(sequences * length, features), weight[:, :3 * features], preferred_element_type=jnp.float32)).reshape(sequences, length, 3 * features)
    queries = split_heads(projected[..., :features])
    key_rows = split_heads(projected[..., features:2 * features])
    value_rows = split_heads(projected[..., 2 * features:])
    scaling = 1.0 / math.sqrt(features // HEADS)
    scores = jnp.einsum('slhd,smhd->shlm', queries, key_rows) * scaling
    allowed = jnp.logical_or(live[:, None, None, :], jnp.eye(length, dtype=bool)[None, None])
    scores = jnp.where(allowed, scores, NEGATIVE)
    highest = lax.optimization_barrier(jnp.max(scores, axis=-1, keepdims=True))
    expanded = jnp.exp(scores - highest)
    probabilities = expanded / lax.optimization_barrier(jnp.sum(expanded, axis=-1, keepdims=True))
    low_weights = lower(probabilities).astype(jnp.float32)
    attended = lower(jnp.einsum('shlm,smhd->slhd', low_weights, value_rows)).reshape(sequences, length, features)
    return (queries, key_rows, value_rows, probabilities, attended)

def project_out(attended, weight):
    sequences, length, features = attended.shape
    return lower(jnp.dot(attended.reshape(sequences * length, features), weight[:, 3 * features:], preferred_element_type=jnp.float32)).reshape(sequences, length, features)

def attention_grad(state, normed, upstream, weight):
    queries, key_rows, value_rows, probabilities, attended = state
    sequences, length, features = normed.shape
    rows_total = sequences * length
    scaling = 1.0 / math.sqrt(features // HEADS)
    flat_up = upstream.reshape(rows_total, features)
    grad_attended = lower(jnp.dot(flat_up, weight[:, 3 * features:].T, preferred_element_type=jnp.float32))
    grad_heads = grad_attended.reshape(sequences, length, HEADS, features // HEADS).astype(jnp.float32)
    low_weights = lower(probabilities).astype(jnp.float32)
    grad_values = lower(jnp.einsum('shlm,slhd->smhd', low_weights, grad_heads))
    grad_probs = jnp.einsum('slhd,smhd->shlm', grad_heads, value_rows)
    grad_scores = lower(probabilities * (grad_probs - lax.optimization_barrier(jnp.sum(probabilities * grad_probs, axis=-1, keepdims=True))) * scaling).astype(jnp.float32)
    grad_queries = lower(jnp.einsum('shlm,smhd->slhd', grad_scores, key_rows))
    grad_keys = lower(jnp.einsum('shlm,slhd->smhd', grad_scores, queries))
    grad_project = jnp.concatenate([grad_queries.reshape(rows_total, features), grad_keys.reshape(rows_total, features), grad_values.reshape(rows_total, features)], axis=1)
    grad_normed = lower(jnp.dot(grad_project, weight[:, :3 * features].T, preferred_element_type=jnp.float32)).reshape(sequences, length, features)
    flat_normed = normed.reshape(rows_total, features)
    flat_attended = attended.reshape(rows_total, features)
    term = jnp.concatenate([jnp.dot(flat_normed.T, grad_project, preferred_element_type=jnp.float32), jnp.dot(flat_attended.T, flat_up, preferred_element_type=jnp.float32)], axis=1)
    return (grad_normed, term)

def run_forward(normed, weight, live):
    sequences, length, features = normed.shape
    block_size = 8

    def one_block(inputs_pair):
        block_normed, block_live = inputs_pair
        state = attention_state(block_normed, weight, block_live)
        return project_out(state[4], weight)
    result = lax.map(one_block, (normed.reshape(sequences // block_size, block_size, length, features), live.reshape(sequences // block_size, block_size, length)))
    return result.reshape(sequences, length, features)

def run_backward(normed, upstream, weight, live):
    sequences, length, features = normed.shape
    block_size = 8

    def accumulate(total, triple):
        block_normed, block_up, block_live = triple
        state = attention_state(block_normed, weight, block_live)
        grad_normed, term = attention_grad(state, block_normed, block_up, weight)
        return (total + term, grad_normed)
    total, grads = lax.scan(accumulate, jnp.zeros((features, 4 * features), jnp.float32), (normed.reshape(sequences // block_size, block_size, length, features), upstream.reshape(sequences // block_size, block_size, length, features), live.reshape(sequences // block_size, block_size, length)))
    return (grads.reshape(sequences, length, features), total)

def reference(tokens, cotangent, mask, w_offset, w_midpoint):
    live = mask == 1
    normed = normalize(tokens)
    column_normed = jnp.swapaxes(normed, 0, 1)
    column_live = jnp.swapaxes(live, 0, 1)
    offset_out = jnp.swapaxes(run_forward(column_normed, w_offset, column_live), 0, 1)
    middle = lower(tokens.astype(jnp.float32) + offset_out.astype(jnp.float32))
    normed_mid = normalize(middle)
    grad_mid_normed, term_mid = run_backward(normed_mid, cotangent, w_midpoint, live)
    upstream = lower(cotangent.astype(jnp.float32) + normalize_grad(middle, grad_mid_normed))
    grad_column, term_off = run_backward(column_normed, jnp.swapaxes(upstream, 0, 1), w_offset, column_live)
    grad_tokens = (upstream.astype(jnp.float32) + normalize_grad(tokens, jnp.swapaxes(grad_column, 0, 1))).astype(jnp.bfloat16)
    return (grad_tokens, term_off, term_mid)
```

```python
import math

import jax
import jax.numpy as jnp
from jax import lax
from jax.sharding import Mesh
from jax.sharding import PartitionSpec as P

HEADS = 12
EPSILON = 1e-05
NEGATIVE = -1e30
OFF = ("xl", "z", "core")
MID = ("y", "xh")


def statistics(widened):
    center = jnp.mean(widened, axis=-1, keepdims=True)
    spread = jnp.mean(jnp.square(widened - center), axis=-1, keepdims=True)
    inverse = lax.rsqrt(spread + EPSILON)
    return (widened - center) * inverse, inverse


def normalize(values):
    return statistics(values.astype(jnp.float32))[0].astype(jnp.bfloat16)


def normalize_grad(values, upstream):
    scaled, inverse = statistics(values.astype(jnp.float32))
    incoming = upstream.astype(jnp.float32)
    return inverse * (
        incoming
        - jnp.mean(incoming, axis=-1, keepdims=True)
        - scaled * jnp.mean(incoming * scaled, axis=-1, keepdims=True)
    )


def attention_state(normed, weight, live):
    length, features = normed.shape
    projected = jnp.dot(
        normed, weight[:, : 3 * features], preferred_element_type=jnp.float32
    ).astype(jnp.bfloat16)
    projected = projected.reshape(length, 3, HEADS, features // HEADS)
    queries, key_rows, value_rows = projected[:, 0], projected[:, 1], projected[:, 2]
    scaling = 1.0 / math.sqrt(features // HEADS)
    scores = (
        jnp.einsum("lhd,mhd->hlm", queries, key_rows, preferred_element_type=jnp.float32) * scaling
    )
    allowed = jnp.logical_or(live[None, None, :], jnp.eye(length, dtype=bool)[None])
    scores = jnp.where(allowed, scores, NEGATIVE)
    expanded = jnp.exp(scores - jnp.max(scores, axis=-1, keepdims=True))
    probabilities = expanded / jnp.sum(expanded, axis=-1, keepdims=True)
    attended = jnp.einsum(
        "hlm,mhd->lhd",
        probabilities.astype(jnp.bfloat16),
        value_rows,
        preferred_element_type=jnp.float32,
    ).astype(jnp.bfloat16)
    return queries, key_rows, value_rows, probabilities, attended.reshape(length, features)


def attention_grad(state, normed, upstream, weight):
    queries, key_rows, value_rows, probabilities, attended = state
    length, features = normed.shape
    scaling = 1.0 / math.sqrt(features // HEADS)
    last = (((1,), (1,)), ((), ()))
    first = (((0,), (0,)), ((), ()))
    grad_attended = lax.dot_general(
        upstream, weight[:, 3 * features :], last, preferred_element_type=jnp.float32
    ).astype(jnp.bfloat16)
    grad_heads = grad_attended.reshape(length, HEADS, features // HEADS)
    low = probabilities.astype(jnp.bfloat16)
    grad_values = jnp.einsum(
        "hlm,lhd->mhd", low, grad_heads, preferred_element_type=jnp.float32
    ).astype(jnp.bfloat16)
    grad_probs = jnp.einsum(
        "lhd,mhd->hlm", grad_heads, value_rows, preferred_element_type=jnp.float32
    )
    grad_scores = (
        probabilities
        * (grad_probs - jnp.sum(probabilities * grad_probs, axis=-1, keepdims=True))
        * scaling
    ).astype(jnp.bfloat16)
    grad_queries = jnp.einsum(
        "hlm,mhd->lhd", grad_scores, key_rows, preferred_element_type=jnp.float32
    ).astype(jnp.bfloat16)
    grad_keys = jnp.einsum(
        "hlm,lhd->mhd", grad_scores, queries, preferred_element_type=jnp.float32
    ).astype(jnp.bfloat16)
    grad_project = jnp.concatenate(
        [part.reshape(length, features) for part in (grad_queries, grad_keys, grad_values)], axis=1
    )
    grad_normed = lax.dot_general(
        grad_project, weight[:, : 3 * features], last, preferred_element_type=jnp.float32
    ).astype(jnp.bfloat16)
    term = jnp.concatenate(
        [
            lax.dot_general(grad_project, normed, first, preferred_element_type=jnp.float32).astype(
                jnp.bfloat16
            ),
            lax.dot_general(upstream, attended, first, preferred_element_type=jnp.float32).astype(
                jnp.bfloat16
            ),
        ],
        axis=0,
    )
    return grad_normed, term


def add(*parts):
    total = parts[0].astype(jnp.float32)
    for part in parts[1:]:
        total = total + part.astype(jnp.float32)
    return total.astype(jnp.bfloat16)


def pick(array, index, axis):
    return lax.dynamic_index_in_dim(array, index, axis, keepdims=False)


def reduce_columns(term):
    features = term.shape[1]
    swap = [(0, 1), (1, 0)]
    onward = [(i, (i + 1) % 4) for i in range(4)]
    back = [(i, (i + 3) % 4) for i in range(4)]
    share = term.shape[0] // 256
    core, y, xl = lax.axis_index("core"), lax.axis_index("y"), lax.axis_index("xl")
    blocks = term.reshape(2, 8, 2, 4, 2 * share, features)
    held = add(
        pick(blocks, core, 2), lax.ppermute(pick(blocks, 1 - core, 2), "core", swap)
    )
    far = pick(held, (y + 2) % 4, 2)
    from_left = lax.ppermute(far[0], "y", onward)
    from_right = lax.ppermute(far[1], "y", back)
    near_right = pick(held, (y + 1) % 4, 2)
    near_left = pick(held, (y + 3) % 4, 2)
    to_right = jnp.stack([add(near_right[0], from_left), near_right[1]])
    to_left = jnp.stack([near_left[0], add(near_left[1], from_right)])
    mine = add(
        pick(held, y, 2), lax.ppermute(to_right, "y", onward), lax.ppermute(to_left, "y", back)
    )
    mine = add(pick(mine, xl, 0), lax.ppermute(pick(mine, 1 - xl, 0), "xl", swap))
    pieces = mine.reshape(16, share, features)
    arrived = lax.all_to_all(pieces, ("z", "xh"), split_axis=0, concat_axis=0, tiled=True)
    return jnp.sum(arrived.astype(jnp.float32), axis=0).T


def local(tokens, cotangent, mask, w_offset, w_midpoint):
    off_place = lax.axis_index(OFF)
    mid_place = lax.axis_index(MID)
    rows_dev, cols_dev, features = tokens.shape
    everyone = OFF + MID
    live = mask == 1
    column_live = pick(live, mid_place * cols_dev + off_place, 1)
    row_live = pick(live, off_place * rows_dev + mid_place, 0)
    row_live = row_live.reshape(8, 32).T.reshape(256)

    def exchange(rows):
        return lax.all_to_all(rows, everyone, split_axis=0, concat_axis=0, tiled=True)

    column_tokens = lax.all_to_all(
        jnp.swapaxes(tokens, 0, 1), OFF, split_axis=0, concat_axis=0, tiled=True
    ).reshape(256, features)
    row_up = lax.all_to_all(cotangent, MID, split_axis=0, concat_axis=0, tiled=True)
    row_up = jnp.swapaxes(row_up.reshape(8, 32, features), 0, 1).reshape(256, features)

    column_normed = normalize(column_tokens)
    offset_state = attention_state(column_normed, w_offset, column_live)
    offset_out = jnp.dot(
        offset_state[4], w_offset[:, 3 * features :], preferred_element_type=jnp.float32
    ).astype(jnp.bfloat16)
    middle = exchange(add(column_tokens, offset_out))
    row_normed = normalize(middle)
    mid_state = attention_state(row_normed, w_midpoint, row_live)
    row_grad, term_mid = attention_grad(mid_state, row_normed, row_up, w_midpoint)
    upstream = (row_up.astype(jnp.float32) + normalize_grad(middle, row_grad)).astype(jnp.bfloat16)
    column_up = exchange(upstream)
    grad_mid_weights = reduce_columns(term_mid)
    column_grad, term_off = attention_grad(offset_state, column_normed, column_up, w_offset)
    column_out = (
        column_up.astype(jnp.float32) + normalize_grad(column_tokens, column_grad)
    ).astype(jnp.bfloat16)
    grad_tokens = jnp.swapaxes(
        lax.all_to_all(
            column_out.reshape(32, 8, features), OFF, split_axis=0, concat_axis=0, tiled=True
        ),
        0,
        1,
    )
    grad_off_weights = reduce_columns(term_off)
    return grad_tokens, grad_off_weights, grad_mid_weights


def solution(mesh):
    fine = Mesh(mesh.devices.reshape(2, 8, 2, 4, 2), OFF + MID)
    placed = (P(OFF, MID, None), P(OFF, MID, None), P(), P(), P())
    return jax.shard_map(
        local,
        mesh=fine,
        in_specs=placed,
        out_specs=(P(OFF, MID, None), P(None, OFF + MID), P(None, OFF + MID)),
        check_vma=False,
    )
```

```python
import math

import jax
import jax.numpy as jnp
from jax import lax
from jax.experimental import pallas as pl
from jax.experimental.pallas import tpu as pltpu
from jax.sharding import Mesh
from jax.sharding import PartitionSpec as P

HEADS = 12
WIDTH = 64
SCALE = 0.125
EPSILON = 1e-05
NEGATIVE = -1e30
OFF = ("xl", "z", "core")
MID = ("y", "xh")


NT = (((1,), (1,)), ((), ()))
VMEM_LIMIT = 48 * 1024 * 1024


def dot(left, right):
    return jnp.dot(left, right, preferred_element_type=jnp.float32)


def dot_nt(left, right):
    return lax.dot_general(left, right, NT, preferred_element_type=jnp.float32)


def low(value):
    return value.astype(jnp.bfloat16)


def statistics(values):
    widened = values.astype(jnp.float32)
    center = jnp.mean(widened, axis=-1, keepdims=True)
    shifted = widened - center
    inverse = lax.rsqrt(jnp.mean(shifted * shifted, axis=-1, keepdims=True) + EPSILON)
    return shifted * inverse, inverse


def layer_grad(values, incoming):
    scaled, inverse = statistics(values)
    incoming = incoming.astype(jnp.float32)
    return inverse * (
        incoming
        - jnp.mean(incoming, axis=-1, keepdims=True)
        - scaled * jnp.mean(incoming * scaled, axis=-1, keepdims=True)
    )


def key_bias(live):
    length = live.shape[0]
    keys = lax.broadcasted_iota(jnp.int32, (length, length), 0)
    queries = lax.broadcasted_iota(jnp.int32, (length, length), 1)
    allowed = jnp.logical_or(live == 1, keys == queries)
    return jnp.where(allowed, 0.0, NEGATIVE)


def padded(array, head):
    rows = array[head * WIDTH : (head + 1) * WIDTH]
    blank = jnp.zeros_like(rows)
    return jnp.concatenate([rows, blank] if head % 2 == 0 else [blank, rows], axis=0)


def pair(head):
    start = (head // 2) * 2 * WIDTH
    return slice(start, start + 2 * WIDTH)


def own(head):
    return slice(head * WIDTH, (head + 1) * WIDTH)


def softmax_keys(scores):
    expanded = jnp.exp(scores - jnp.max(scores, axis=0, keepdims=True))
    return expanded * (1.0 / jnp.sum(expanded, axis=0, keepdims=True))


def forward_kernel(
    tokens_ref, live_ref, weight_t_ref, weight_ref, out_ref, q_ref, k_ref, vt_ref, a_ref, p_ref, bias_ref
):
    features = tokens_ref.shape[1]
    normed = low(statistics(tokens_ref[...])[0])
    q_ref[...] = low(dot_nt(weight_t_ref[:features], normed)) * SCALE
    k_ref[...] = low(dot(normed, weight_ref[:, features : 2 * features]))
    vt_ref[...] = low(dot_nt(weight_t_ref[2 * features : 3 * features], normed))
    bias_ref[...] = key_bias(live_ref[...])
    for head in range(HEADS):
        scores = dot(k_ref[:, pair(head)], padded(q_ref, head)) + bias_ref[...]
        p = low(softmax_keys(scores))
        p_ref[head] = p
        a_ref[own(head)] = low(dot(vt_ref[own(head)], p))
    out = low(dot(a_ref[...].T, weight_ref[:, 3 * features :]))
    out_ref[...] = low(tokens_ref[...].astype(jnp.float32) + out.astype(jnp.float32))


def residual_kernel(tokens_ref, weight_t_ref, weight_ref, normed_ref, kt_ref, v_ref):
    features = tokens_ref.shape[1]
    normed = low(statistics(tokens_ref[...])[0])
    normed_ref[...] = normed
    kt_ref[...] = low(dot_nt(weight_t_ref[features : 2 * features], normed))
    v_ref[...] = low(dot(normed, weight_ref[:, 2 * features : 3 * features]))


def upstream_kernel(up_ref, weight_ref, da_ref):
    features = up_ref.shape[1]
    da_ref[...] = low(dot_nt(weight_ref[:, 3 * features :], up_ref[...]))


def head_grad(head, p, p_low, q_ref, kt_ref, v_ref, da_ref, d_ref):
    features = da_ref.shape[0]
    dp = dot(v_ref[:, pair(head)], padded(da_ref, head))
    ds = low(p * (dp - jnp.sum(p * dp, axis=0, keepdims=True)))
    d_ref[own(head)] = low(dot(kt_ref[own(head)], ds) * SCALE)
    d_ref[features + head * WIDTH : features + (head + 1) * WIDTH] = low(dot_nt(q_ref[own(head)], ds))
    d_ref[2 * features + head * WIDTH : 2 * features + (head + 1) * WIDTH] = low(
        dot_nt(da_ref[own(head)], p_low)
    )


def middle_kernel(
    tokens_ref, up_ref, live_ref, da_ref, weight_t_ref, weight_ref,
    out_ref, normed_ref, a_ref, d_ref,
    q_ref, k_ref, kt_ref, v_ref, vt_ref, bias_ref,
):
    features = tokens_ref.shape[1]
    normed = low(statistics(tokens_ref[...])[0])
    normed_ref[...] = normed
    q_ref[...] = low(dot_nt(weight_t_ref[:features], normed)) * SCALE
    k_ref[...] = low(dot(normed, weight_ref[:, features : 2 * features]))
    kt_ref[...] = low(dot_nt(weight_t_ref[features : 2 * features], normed))
    v_ref[...] = low(dot(normed, weight_ref[:, 2 * features : 3 * features]))
    vt_ref[...] = low(dot_nt(weight_t_ref[2 * features : 3 * features], normed))
    bias_ref[...] = key_bias(live_ref[...])
    for head in range(HEADS):
        scores = dot(k_ref[:, pair(head)], padded(q_ref, head)) + bias_ref[...]
        p = softmax_keys(scores)
        p_low = low(p)
        a_ref[own(head)] = low(dot(vt_ref[own(head)], p_low))
        head_grad(head, p, p_low, q_ref, kt_ref, v_ref, da_ref, d_ref)
    dh = low(dot(weight_ref[:, : 3 * features], d_ref[...])).T
    out_ref[...] = low(up_ref[...].astype(jnp.float32) + layer_grad(tokens_ref[...], dh))


def backward_kernel(up_ref, weight_ref, q_ref, kt_ref, v_ref, p_ref, d_ref, da_ref):
    features = up_ref.shape[1]
    da_ref[...] = low(dot_nt(weight_ref[:, 3 * features :], up_ref[...]))
    for head in range(HEADS):
        p_low = p_ref[head]
        head_grad(head, p_low.astype(jnp.float32), p_low, q_ref, kt_ref, v_ref, da_ref, d_ref)


def finish_kernel(tokens_ref, up_ref, d_ref, weight_ref, out_ref):
    features = tokens_ref.shape[1]
    dh = low(dot(weight_ref[:, : 3 * features], d_ref[...])).T
    out_ref[...] = low(up_ref[...].astype(jnp.float32) + layer_grad(tokens_ref[...], dh))


def weights_kernel(core_ref, normed_ref, up_ref, a_ref, d_ref, keep_ref, send_ref, upt_ref):
    features = normed_ref.shape[1]
    upt_ref[...] = up_ref[...].T
    groups, group = keep_ref.shape[:2]
    first = 3 * features // (2 * group)
    core = core_ref[0]
    for out_ref, which in ((keep_ref, core), (send_ref, 1 - core)):
        for step in range(groups):
            if step < first:
                start = pl.multiple_of((2 * step + which) * group, group)
                out_ref[step] = low(dot(d_ref[pl.ds(start, group), :], normed_ref[...]))
            else:
                start = pl.multiple_of((2 * (step - first) + which) * group, group)
                out_ref[step] = low(dot_nt(upt_ref[pl.ds(start, group), :], a_ref[...]))


def shape(*sizes):
    return jax.ShapeDtypeStruct(sizes, jnp.bfloat16)


def call(kernel, outs, *args, scratch=(), flops=0, smem=0, name=None):
    space = [pl.BlockSpec(memory_space=pltpu.SMEM)] * smem
    space += [pl.BlockSpec(memory_space=pltpu.VMEM)] * (len(args) - smem)
    moved = sum(math.prod(a.shape) * 2 for a in (*args, *outs))
    return pl.pallas_call(
        kernel,
        out_shape=outs,
        in_specs=space,
        out_specs=[pl.BlockSpec(memory_space=pltpu.VMEM)] * len(outs),
        scratch_shapes=[pltpu.VMEM(s, t) for s, t in scratch],
        compiler_params=pltpu.CompilerParams(vmem_limit_bytes=VMEM_LIMIT),
        cost_estimate=pl.CostEstimate(flops=int(flops), bytes_accessed=moved, transcendentals=0),
        name=name,
    )(*args)


def offset_forward(tokens, live, weight_t, weight):
    length, features = tokens.shape
    flat, turned = shape(length, features), shape(features, length)
    return call(
        forward_kernel,
        [flat, turned, flat, turned, turned, shape(HEADS, length, length)],
        tokens, live, weight_t, weight,
        scratch=[((length, length), jnp.float32)],
        flops=4e9, name="offset_forward",
    )


def offset_residuals(tokens, weight_t, weight):
    length, features = tokens.shape
    return call(
        residual_kernel,
        [shape(length, features), shape(features, length), shape(length, features)],
        tokens, weight_t, weight, flops=1e9, name="offset_residuals",
    )


def cotangent_heads(up, weight):
    length, features = up.shape
    return call(upstream_kernel, [shape(features, length)], up, weight, flops=5e8, name="cotangent_heads")[0]


def midpoint_both(tokens, up, live, da, weight_t, weight):
    length, features = tokens.shape
    flat, turned = shape(length, features), shape(features, length)
    bf = jnp.bfloat16
    return call(
        middle_kernel,
        [flat, flat, turned, shape(3 * features, length)],
        tokens, up, live, da, weight_t, weight,
        scratch=[
            (turned.shape, bf), (flat.shape, bf), (turned.shape, bf), (flat.shape, bf), (turned.shape, bf),
            ((length, length), jnp.float32),
        ],
        flops=1e10, name="midpoint_both",
    )


def offset_backward(up, weight, q, kt, v, p):
    length, features = up.shape
    return call(
        backward_kernel, [shape(3 * features, length)], up, weight, q, kt, v, p,
        scratch=[((features, length), jnp.bfloat16)], flops=5e9, name="offset_backward",
    )[0]


def offset_finish(tokens, up, d, weight):
    return call(
        finish_kernel, [shape(*tokens.shape)], tokens, up, d, weight, flops=2e9, name="offset_finish"
    )[0]


def weight_terms(core, normed, up, a, d):
    length, features = normed.shape
    half = shape(16, features // 8, features)
    return call(
        weights_kernel, [half, half], core, normed, up, a, d,
        scratch=[((features, length), jnp.bfloat16)], smem=1, flops=2e9, name="weight_terms",
    )


def add(*parts):
    total = parts[0].astype(jnp.float32)
    for part in parts[1:]:
        total = total + part.astype(jnp.float32)
    return total.astype(jnp.bfloat16)


def pick(array, index, axis):
    return lax.dynamic_index_in_dim(array, index, axis, keepdims=False)


def reduce_columns(keep, send):
    groups, group, features = keep.shape
    swap = [(0, 1), (1, 0)]
    onward = [(i, (i + 1) % 4) for i in range(4)]
    back = [(i, (i + 3) % 4) for i in range(4)]
    y, xl = lax.axis_index("y"), lax.axis_index("xl")
    shape = (2, groups // 2, 4, group // 4, features)
    came = lax.ppermute(send, "core", swap)
    held = add(keep, came).reshape(shape)
    far = pick(held, (y + 2) % 4, 2)
    from_left = lax.ppermute(far[0], "y", onward)
    from_right = lax.ppermute(far[1], "y", back)
    near_right = pick(held, (y + 1) % 4, 2)
    near_left = pick(held, (y + 3) % 4, 2)
    to_right = jnp.stack([add(near_right[0], from_left), near_right[1]])
    to_left = jnp.stack([near_left[0], add(near_left[1], from_right)])
    mine = add(
        pick(held, y, 2), lax.ppermute(to_right, "y", onward), lax.ppermute(to_left, "y", back)
    )
    mine = add(pick(mine, xl, 0), lax.ppermute(pick(mine, 1 - xl, 0), "xl", swap))
    pieces = mine.reshape(groups, group // 8, features)
    arrived = lax.all_to_all(pieces, ("z", "xh"), split_axis=0, concat_axis=0, tiled=True)
    return jnp.sum(arrived.astype(jnp.float32), axis=0).T


def local(tokens, cotangent, mask, w_offset, w_midpoint):
    off_place = lax.axis_index(OFF)
    mid_place = lax.axis_index(MID)
    core = lax.axis_index("core").reshape(1).astype(jnp.int32)
    rows_dev, cols_dev, features = tokens.shape
    everyone = OFF + MID
    column_live = pick(mask, mid_place * cols_dev + off_place, 1).reshape(256, 1)
    row_live = pick(mask, off_place * rows_dev + mid_place, 0)
    row_live = row_live.reshape(8, 32).T.reshape(256, 1)

    def exchange(rows):
        return lax.all_to_all(rows, everyone, split_axis=0, concat_axis=0, tiled=True)

    column_tokens = lax.all_to_all(
        jnp.swapaxes(tokens, 0, 1), OFF, split_axis=0, concat_axis=0, tiled=True
    ).reshape(256, features)
    row_up = lax.all_to_all(cotangent, MID, split_axis=0, concat_axis=0, tiled=True)
    row_up = jnp.swapaxes(row_up.reshape(8, 32, features), 0, 1).reshape(256, features)
    w_offset_t = w_offset[:, : 3 * features].T
    w_midpoint_t = w_midpoint[:, : 3 * features].T

    column_middle, q, k, vt, a, p = offset_forward(
        column_tokens, column_live, w_offset_t, w_offset
    )
    middle = exchange(column_middle)
    column_normed, kt, v = offset_residuals(column_tokens, w_offset_t, w_offset)
    da_mid = cotangent_heads(row_up, w_midpoint)
    upstream, row_normed, a_mid, d_mid = midpoint_both(
        middle, row_up, row_live, da_mid, w_midpoint_t, w_midpoint
    )
    column_up = exchange(upstream)
    grad_mid_weights = reduce_columns(*weight_terms(core, row_normed, row_up, a_mid, d_mid))
    d_off = offset_backward(column_up, w_offset, q, kt, v, p)
    keep, send = weight_terms(core, column_normed, column_up, a, d_off)
    column_out = offset_finish(column_tokens, column_up, d_off, w_offset)
    grad_tokens = jnp.swapaxes(
        lax.all_to_all(
            column_out.reshape(32, 8, features), OFF, split_axis=0, concat_axis=0, tiled=True
        ),
        0,
        1,
    )
    grad_off_weights = reduce_columns(keep, send)
    return grad_tokens, grad_off_weights, grad_mid_weights


def solution(mesh):
    fine = Mesh(mesh.devices.reshape(2, 8, 2, 4, 2), OFF + MID)
    placed = (P(OFF, MID, None), P(OFF, MID, None), P(), P(), P())
    return jax.shard_map(
        local,
        mesh=fine,
        in_specs=placed,
        out_specs=(P(OFF, MID, None), P(None, OFF + MID), P(None, OFF + MID)),
        check_vma=False,
    )
```

```python
import math

import jax
import jax.numpy as jnp
from jax import lax
from jax.experimental import pallas as pl
from jax.experimental.pallas import tpu as pltpu
from jax.sharding import Mesh
from jax.sharding import PartitionSpec as P

HEADS = 12
WIDTH = 64
SCALE = 0.125
EPSILON = 1e-05
NEGATIVE = -1e30
OFF = ("xl", "z", "core")
MID = ("y", "xh")


NT = (((1,), (1,)), ((), ()))
VMEM_LIMIT = 48 * 1024 * 1024


def dot(left, right):
    return jnp.dot(left, right, preferred_element_type=jnp.float32)


def dot_nt(left, right):
    return lax.dot_general(left, right, NT, preferred_element_type=jnp.float32)


def low(value):
    return value.astype(jnp.bfloat16)


def statistics(values):
    widened = values.astype(jnp.float32)
    center = jnp.mean(widened, axis=-1, keepdims=True)
    shifted = widened - center
    inverse = lax.rsqrt(jnp.mean(shifted * shifted, axis=-1, keepdims=True) + EPSILON)
    return shifted * inverse, inverse


def layer_grad(values, incoming):
    scaled, inverse = statistics(values)
    incoming = incoming.astype(jnp.float32)
    return inverse * (
        incoming
        - jnp.mean(incoming, axis=-1, keepdims=True)
        - scaled * jnp.mean(incoming * scaled, axis=-1, keepdims=True)
    )


def key_bias(live):
    length = live.shape[0]
    keys = lax.broadcasted_iota(jnp.int32, (length, length), 0)
    queries = lax.broadcasted_iota(jnp.int32, (length, length), 1)
    allowed = jnp.logical_or(live == 1, keys == queries)
    return jnp.where(allowed, 0.0, NEGATIVE)


def padded(array, head):
    rows = array[head * WIDTH : (head + 1) * WIDTH]
    blank = jnp.zeros_like(rows)
    return jnp.concatenate([rows, blank] if head % 2 == 0 else [blank, rows], axis=0)


def pair(head):
    start = (head // 2) * 2 * WIDTH
    return slice(start, start + 2 * WIDTH)


def own(head):
    return slice(head * WIDTH, (head + 1) * WIDTH)


def softmax_keys(scores):
    expanded = jnp.exp(scores - jnp.max(scores, axis=0, keepdims=True))
    return expanded * (1.0 / jnp.sum(expanded, axis=0, keepdims=True))


def forward_kernel(
    tokens_ref, live_ref, weight_t_ref, weight_ref, out_ref, q_ref, k_ref, vt_ref, a_ref, p_ref, bias_ref
):
    features = tokens_ref.shape[1]
    normed = low(statistics(tokens_ref[...])[0])
    q_ref[...] = low(dot_nt(weight_t_ref[:features], normed)) * SCALE
    k_ref[...] = low(dot(normed, weight_ref[:, features : 2 * features]))
    vt_ref[...] = low(dot_nt(weight_t_ref[2 * features : 3 * features], normed))
    bias_ref[...] = key_bias(live_ref[...])
    for head in range(HEADS):
        scores = dot(k_ref[:, pair(head)], padded(q_ref, head)) + bias_ref[...]
        p = low(softmax_keys(scores))
        p_ref[head] = p
        a_ref[own(head)] = low(dot(vt_ref[own(head)], p))
    out = low(dot(a_ref[...].T, weight_ref[:, 3 * features :]))
    out_ref[...] = low(tokens_ref[...].astype(jnp.float32) + out.astype(jnp.float32))


def residual_kernel(tokens_ref, weight_t_ref, weight_ref, normed_ref, kt_ref, v_ref):
    features = tokens_ref.shape[1]
    normed = low(statistics(tokens_ref[...])[0])
    normed_ref[...] = normed
    kt_ref[...] = low(dot_nt(weight_t_ref[features : 2 * features], normed))
    v_ref[...] = low(dot(normed, weight_ref[:, 2 * features : 3 * features]))


def upstream_kernel(up_ref, weight_ref, da_ref):
    features = up_ref.shape[1]
    da_ref[...] = low(dot_nt(weight_ref[:, 3 * features :], up_ref[...]))


def head_grad(head, p, p_low, q_ref, kt_ref, v_ref, da_ref, d_ref):
    features = da_ref.shape[0]
    dp = dot(v_ref[:, pair(head)], padded(da_ref, head))
    ds = low(p * (dp - jnp.sum(p * dp, axis=0, keepdims=True)))
    d_ref[own(head)] = low(dot(kt_ref[own(head)], ds) * SCALE)
    d_ref[features + head * WIDTH : features + (head + 1) * WIDTH] = low(dot_nt(q_ref[own(head)], ds))
    d_ref[2 * features + head * WIDTH : 2 * features + (head + 1) * WIDTH] = low(
        dot_nt(da_ref[own(head)], p_low)
    )


def middle_kernel(
    tokens_ref, up_ref, live_ref, da_ref, weight_t_ref, weight_ref,
    out_ref, normed_ref, a_ref, d_ref,
    q_ref, k_ref, kt_ref, v_ref, vt_ref, bias_ref,
):
    features = tokens_ref.shape[1]
    normed = low(statistics(tokens_ref[...])[0])
    normed_ref[...] = normed
    q_ref[...] = low(dot_nt(weight_t_ref[:features], normed)) * SCALE
    k_ref[...] = low(dot(normed, weight_ref[:, features : 2 * features]))
    kt_ref[...] = low(dot_nt(weight_t_ref[features : 2 * features], normed))
    v_ref[...] = low(dot(normed, weight_ref[:, 2 * features : 3 * features]))
    vt_ref[...] = low(dot_nt(weight_t_ref[2 * features : 3 * features], normed))
    bias_ref[...] = key_bias(live_ref[...])
    for head in range(HEADS):
        scores = dot(k_ref[:, pair(head)], padded(q_ref, head)) + bias_ref[...]
        p = softmax_keys(scores)
        p_low = low(p)
        a_ref[own(head)] = low(dot(vt_ref[own(head)], p_low))
        head_grad(head, p, p_low, q_ref, kt_ref, v_ref, da_ref, d_ref)
    dh = low(dot(weight_ref[:, : 3 * features], d_ref[...])).T
    out_ref[...] = low(up_ref[...].astype(jnp.float32) + layer_grad(tokens_ref[...], dh))


def backward_kernel(up_ref, weight_ref, q_ref, kt_ref, v_ref, p_ref, d_ref, da_ref):
    features = up_ref.shape[1]
    da_ref[...] = low(dot_nt(weight_ref[:, 3 * features :], up_ref[...]))
    for head in range(HEADS):
        p_low = p_ref[head]
        head_grad(head, p_low.astype(jnp.float32), p_low, q_ref, kt_ref, v_ref, da_ref, d_ref)


def finish_kernel(tokens_ref, up_ref, d_ref, weight_ref, out_ref):
    features = tokens_ref.shape[1]
    dh = low(dot(weight_ref[:, : 3 * features], d_ref[...])).T
    out_ref[...] = low(up_ref[...].astype(jnp.float32) + layer_grad(tokens_ref[...], dh))


def weights_kernel(core_ref, normed_ref, up_ref, a_ref, d_ref, keep_ref, send_ref, upt_ref):
    features = normed_ref.shape[1]
    upt_ref[...] = up_ref[...].T
    groups, group = keep_ref.shape[:2]
    first = 3 * features // (2 * group)
    core = core_ref[0]
    for out_ref, which in ((keep_ref, core), (send_ref, 1 - core)):
        for step in range(groups):
            if step < first:
                start = pl.multiple_of((2 * step + which) * group, group)
                out_ref[step] = low(dot(d_ref[pl.ds(start, group), :], normed_ref[...]))
            else:
                start = pl.multiple_of((2 * (step - first) + which) * group, group)
                out_ref[step] = low(dot_nt(upt_ref[pl.ds(start, group), :], a_ref[...]))


def shape(*sizes):
    return jax.ShapeDtypeStruct(sizes, jnp.bfloat16)


def call(kernel, outs, *args, scratch=(), flops=0, smem=0, name=None):
    space = [pl.BlockSpec(memory_space=pltpu.SMEM)] * smem
    space += [pl.BlockSpec(memory_space=pltpu.VMEM)] * (len(args) - smem)
    moved = sum(math.prod(a.shape) * 2 for a in (*args, *outs))
    return pl.pallas_call(
        kernel,
        out_shape=outs,
        in_specs=space,
        out_specs=[pl.BlockSpec(memory_space=pltpu.VMEM)] * len(outs),
        scratch_shapes=[pltpu.VMEM(s, t) for s, t in scratch],
        compiler_params=pltpu.CompilerParams(vmem_limit_bytes=VMEM_LIMIT),
        cost_estimate=pl.CostEstimate(flops=int(flops), bytes_accessed=moved, transcendentals=0),
        name=name,
    )(*args)


def offset_forward(tokens, live, weight_t, weight):
    length, features = tokens.shape
    flat, turned = shape(length, features), shape(features, length)
    return call(
        forward_kernel,
        [flat, turned, flat, turned, turned, shape(HEADS, length, length)],
        tokens, live, weight_t, weight,
        scratch=[((length, length), jnp.float32)],
        flops=4e9, name="offset_forward",
    )


def offset_residuals(tokens, weight_t, weight):
    length, features = tokens.shape
    return call(
        residual_kernel,
        [shape(length, features), shape(features, length), shape(length, features)],
        tokens, weight_t, weight, flops=1e9, name="offset_residuals",
    )


def cotangent_heads(up, weight):
    length, features = up.shape
    return call(upstream_kernel, [shape(features, length)], up, weight, flops=5e8, name="cotangent_heads")[0]


def midpoint_both(tokens, up, live, da, weight_t, weight):
    length, features = tokens.shape
    flat, turned = shape(length, features), shape(features, length)
    bf = jnp.bfloat16
    return call(
        middle_kernel,
        [flat, flat, turned, shape(3 * features, length)],
        tokens, up, live, da, weight_t, weight,
        scratch=[
            (turned.shape, bf), (flat.shape, bf), (turned.shape, bf), (flat.shape, bf), (turned.shape, bf),
            ((length, length), jnp.float32),
        ],
        flops=1e10, name="midpoint_both",
    )


def offset_backward(up, weight, q, kt, v, p):
    length, features = up.shape
    return call(
        backward_kernel, [shape(3 * features, length)], up, weight, q, kt, v, p,
        scratch=[((features, length), jnp.bfloat16)], flops=5e9, name="offset_backward",
    )[0]


def offset_finish(tokens, up, d, weight):
    return call(
        finish_kernel, [shape(*tokens.shape)], tokens, up, d, weight, flops=2e9, name="offset_finish"
    )[0]


def weight_terms(core, normed, up, a, d):
    length, features = normed.shape
    half = shape(16, features // 8, features)
    return call(
        weights_kernel, [half, half], core, normed, up, a, d,
        scratch=[((features, length), jnp.bfloat16)], smem=1, flops=2e9, name="weight_terms",
    )


def add(*parts):
    total = parts[0].astype(jnp.float32)
    for part in parts[1:]:
        total = total + part.astype(jnp.float32)
    return total.astype(jnp.bfloat16)


def pick(array, index, axis):
    return lax.dynamic_index_in_dim(array, index, axis, keepdims=False)


SWAP = [(0, 1), (1, 0)]
ONWARD = [(i, (i + 1) % 4) for i in range(4)]
BACK = [(i, (i + 3) % 4) for i in range(4)]


def tie(*arrays):
    return lax.optimization_barrier(arrays)


def core_sum(keep, send):
    groups, group, features = keep.shape
    came = lax.ppermute(send, "core", SWAP)
    return add(keep, came).reshape(2, groups // 2, 4, group // 4, features)


def ring_first(held):
    y = lax.axis_index("y")
    far = pick(held, (y + 2) % 4, 2)
    right = pick(held, (y + 1) % 4, 2)
    left = pick(held, (y + 3) % 4, 2)
    return (
        lax.ppermute(far[0], "y", ONWARD),
        lax.ppermute(far[1], "y", BACK),
        lax.ppermute(right[1], "y", ONWARD),
        lax.ppermute(left[0], "y", BACK),
    )


def ring_second(held, came):
    y = lax.axis_index("y")
    right = pick(held, (y + 1) % 4, 2)
    left = pick(held, (y + 3) % 4, 2)
    own = pick(held, y, 2)
    first = lax.ppermute(add(right[0], came[0]), "y", ONWARD)
    second = lax.ppermute(add(left[1], came[1]), "y", BACK)
    return add(own[0], came[3], first), add(own[1], came[2], second)


def pair_sum(first, second):
    upper = lax.axis_index("xl") == 1
    keep, send = jnp.where(upper, second, first), jnp.where(upper, first, second)
    return add(keep, lax.ppermute(send, "xl", SWAP))


def last_sum(*halves):
    z, wide, features = halves[0].shape
    pieces = jnp.concatenate([half.reshape(2 * z, wide // 2, features) for half in halves], axis=1)
    arrived = lax.all_to_all(pieces, ("z", "xh"), split_axis=0, concat_axis=0, tiled=True)
    total = jnp.sum(arrived.astype(jnp.float32), axis=0).T
    return jnp.split(total, len(halves), axis=1)


def to_rows(cotangent):
    y, xh = lax.axis_index("y"), lax.axis_index("xh")
    came = [(2 * y + xh, pick(cotangent, 2 * y + xh, 0))]
    for step in range(4):
        for turn in range(2):
            if step == turn == 0:
                continue
            perm = [
                (2 * i + j, 2 * ((i + step) % 4) + (j ^ turn)) for i in range(4) for j in range(2)
            ]
            target = 2 * ((y + step) % 4) + (xh + turn) % 2
            source = 2 * ((y + 4 - step) % 4) + (xh + turn) % 2
            came.append((source, lax.ppermute(pick(cotangent, target, 0), MID, perm)))
    return came


def assemble(came, like):
    blocks = jnp.zeros_like(like)
    for source, block in came:
        blocks = lax.dynamic_update_slice_in_dim(blocks, block[None], source, 0)
    (blocks,) = tie(blocks)
    mids, columns, features = blocks.shape
    return jnp.swapaxes(blocks, 0, 1).reshape(mids * columns, features)


def local(tokens, cotangent, mask, w_offset, w_midpoint):
    off_place = lax.axis_index(OFF)
    mid_place = lax.axis_index(MID)
    core = lax.axis_index("core").reshape(1).astype(jnp.int32)
    rows_dev, cols_dev, features = tokens.shape
    everyone = OFF + MID
    column_live = pick(mask, mid_place * cols_dev + off_place, 1).reshape(256, 1)
    row_live = pick(mask, off_place * rows_dev + mid_place, 0)
    row_live = row_live.reshape(8, 32).T.reshape(256, 1)

    def exchange(rows):
        return lax.all_to_all(rows, everyone, split_axis=0, concat_axis=0, tiled=True)

    column_tokens = lax.all_to_all(
        jnp.swapaxes(tokens, 0, 1), OFF, split_axis=0, concat_axis=0, tiled=True
    ).reshape(256, features)
    sources, came = zip(*to_rows(cotangent))
    column_tokens, *came = tie(column_tokens, *came)
    row_up = assemble(zip(sources, came), cotangent)
    w_offset_t = w_offset[:, : 3 * features].T
    w_midpoint_t = w_midpoint[:, : 3 * features].T

    column_middle, q, k, vt, a, p = offset_forward(
        column_tokens, column_live, w_offset_t, w_offset
    )
    middle = exchange(column_middle)
    column_normed, kt, v = offset_residuals(column_tokens, w_offset_t, w_offset)
    da_mid = cotangent_heads(row_up, w_midpoint)
    upstream, row_normed, a_mid, d_mid = midpoint_both(
        middle, row_up, row_live, da_mid, w_midpoint_t, w_midpoint
    )
    column_up = exchange(upstream)
    mid_held = core_sum(*weight_terms(core, row_normed, row_up, a_mid, d_mid))
    mid_ring = ring_first(mid_held)
    column_up, mid_held = tie(column_up, mid_held)
    d_off = offset_backward(column_up, w_offset, q, kt, v, p)
    d_off, *mid_ring = tie(d_off, *mid_ring)
    mid_pair = ring_second(mid_held, mid_ring)
    keep, send = weight_terms(core, column_normed, column_up, a, d_off)
    send, *mid_pair = tie(send, *mid_pair)
    mid_half = pair_sum(*mid_pair)
    held = core_sum(keep, send)
    column_out = offset_finish(column_tokens, column_up, d_off, w_offset)
    grad_tokens = jnp.swapaxes(
        lax.all_to_all(
            column_out.reshape(32, 8, features), OFF, split_axis=0, concat_axis=0, tiled=True
        ),
        0,
        1,
    )
    off_half = pair_sum(*ring_second(held, ring_first(held)))
    grad_off_weights, grad_mid_weights = last_sum(off_half, mid_half)
    return grad_tokens, grad_off_weights, grad_mid_weights


def solution(mesh):
    fine = Mesh(mesh.devices.reshape(2, 8, 2, 4, 2), OFF + MID)
    placed = (P(OFF, MID, None), P(OFF, MID, None), P(), P(), P())
    return jax.shard_map(
        local,
        mesh=fine,
        in_specs=placed,
        out_specs=(P(OFF, MID, None), P(None, OFF + MID), P(None, OFF + MID)),
        check_vma=False,
    )
```

```python
import math

import jax
import jax.numpy as jnp
from jax import lax
from jax.experimental import pallas as pl
from jax.experimental.pallas import tpu as pltpu
from jax.sharding import Mesh
from jax.sharding import PartitionSpec as P

HEADS = 12
WIDTH = 64
SCALE = 0.125
EPSILON = 1e-05
NEGATIVE = -1e30
OFF = ("xl", "z", "core")
MID = ("y", "xh")


NT = (((1,), (1,)), ((), ()))
VMEM_LIMIT = 48 * 1024 * 1024


def dot(left, right):
    return jnp.dot(left, right, preferred_element_type=jnp.float32)


def dot_nt(left, right):
    return lax.dot_general(left, right, NT, preferred_element_type=jnp.float32)


def low(value):
    return value.astype(jnp.bfloat16)


def statistics(values):
    widened = values.astype(jnp.float32)
    center = jnp.mean(widened, axis=-1, keepdims=True)
    shifted = widened - center
    inverse = lax.rsqrt(jnp.mean(shifted * shifted, axis=-1, keepdims=True) + EPSILON)
    return shifted * inverse, inverse


def layer_grad(values, incoming):
    scaled, inverse = statistics(values)
    incoming = incoming.astype(jnp.float32)
    return inverse * (
        incoming
        - jnp.mean(incoming, axis=-1, keepdims=True)
        - scaled * jnp.mean(incoming * scaled, axis=-1, keepdims=True)
    )


def key_bias(live):
    length = live.shape[0]
    keys = lax.broadcasted_iota(jnp.int32, (length, length), 0)
    queries = lax.broadcasted_iota(jnp.int32, (length, length), 1)
    allowed = jnp.logical_or(live == 1, keys == queries)
    return jnp.where(allowed, 0.0, NEGATIVE)


def padded(array, head):
    rows = array[head * WIDTH : (head + 1) * WIDTH]
    blank = jnp.zeros_like(rows)
    return jnp.concatenate([rows, blank] if head % 2 == 0 else [blank, rows], axis=0)


def pair(head):
    start = (head // 2) * 2 * WIDTH
    return slice(start, start + 2 * WIDTH)


def own(head):
    return slice(head * WIDTH, (head + 1) * WIDTH)


def softmax_keys(scores):
    expanded = jnp.exp(scores - jnp.max(scores, axis=0, keepdims=True))
    return expanded * (1.0 / jnp.sum(expanded, axis=0, keepdims=True))


def fetch(weight_hbm, weight_ref, sems, *parts):
    features = weight_hbm.shape[0]
    copies = {}
    for place, part in enumerate(parts):
        columns = slice(part * features, (part + 1) * features)
        copies[part] = pltpu.make_async_copy(
            weight_hbm.at[:, columns],
            weight_ref.at[:, place * features : (place + 1) * features],
            sems.at[place],
        )
        copies[part].start()
    return copies


def columns(weight_ref, place):
    features = weight_ref.shape[0]
    return weight_ref[:, place * features : (place + 1) * features]


def encode(rows, wide_ref, out_ref):
    chunks = rows.shape[1] // 128
    for c in range(chunks):
        wide_ref[pl.ds(c, rows.shape[0], stride=chunks), :] = rows[:, c * 128 : (c + 1) * 128]
    out_ref[...] = low(wide_ref[...])


def decode(in_ref, wide_ref, rows_ref):
    length, features = rows_ref.shape
    chunks = features // 128
    wide_ref[...] = in_ref[...].astype(jnp.float32)
    for c in range(chunks):
        rows_ref[:, c * 128 : (c + 1) * 128] = low(wide_ref[pl.ds(c, length, stride=chunks), :])


def encode_midpoints(rows, wide_ref, out_ref):
    chunks = rows.shape[1] // 128
    for m in range(8):
        for c in range(chunks):
            wide_ref[pl.ds(m * chunks + c, 32, stride=8 * chunks), :] = rows[
                m * 32 : (m + 1) * 32, c * 128 : (c + 1) * 128
            ]
    out_ref[...] = low(wide_ref[...])


def decode_midpoints(in_ref, wide_ref, rows_ref):
    chunks = rows_ref.shape[1] // 128
    wide_ref[...] = in_ref[...].astype(jnp.float32)
    for m in range(8):
        for c in range(chunks):
            rows_ref[m * 32 : (m + 1) * 32, c * 128 : (c + 1) * 128] = low(
                wide_ref[pl.ds(m * chunks + c, 32, stride=8 * chunks), :]
            )


def forward_kernel(
    tokens_ref, live_ref, weight_hbm, out_ref, q_hbm, a_hbm, p_hbm,
    weight_ref, q_ref, k_ref, v_ref, a_ref, p_ref, bias_ref, wide_ref, sems, out_sems,
):
    copies = fetch(weight_hbm, weight_ref, sems, 1, 0, 2, 3)
    bias_ref[...] = key_bias(live_ref[...])
    normed = low(statistics(tokens_ref[...])[0])
    copies[1].wait()
    k_ref[...] = low(dot(normed, columns(weight_ref, 0)))
    copies[0].wait()
    q_ref[...] = (low(dot(normed, columns(weight_ref, 1))) * SCALE).T
    copies[2].wait()
    v_ref[...] = low(dot(normed, columns(weight_ref, 2))).T
    sent = [pltpu.make_async_copy(q_ref, q_hbm, out_sems.at[HEADS])]
    sent[0].start()
    for head in range(HEADS):
        scores = dot(k_ref[:, pair(head)], padded(q_ref, head)) + bias_ref[...]
        p = low(softmax_keys(scores))
        p_ref[head] = p
        sent.append(pltpu.make_async_copy(p_ref.at[head], p_hbm.at[head], out_sems.at[head]))
        sent[-1].start()
        a_ref[own(head)] = low(dot(v_ref[own(head)], p))
    sent.append(pltpu.make_async_copy(a_ref, a_hbm, out_sems.at[HEADS + 1]))
    sent[-1].start()
    copies[3].wait()
    out = low(dot(a_ref[...].T, columns(weight_ref, 3)))
    encode(tokens_ref[...].astype(jnp.float32) + out.astype(jnp.float32), wide_ref, out_ref)
    for copy in sent:
        copy.wait()


def residual_kernel(tokens_ref, weight_hbm, normed_ref, kt_ref, v_ref, weight_ref, sems):
    copies = fetch(weight_hbm, weight_ref, sems, 1, 2)
    normed = low(statistics(tokens_ref[...])[0])
    normed_ref[...] = normed
    copies[1].wait()
    kt_ref[...] = low(dot(normed, columns(weight_ref, 0))).T
    copies[2].wait()
    v_ref[...] = low(dot(normed, columns(weight_ref, 1)))


def cotangent_kernel(place_ref, *refs):
    *blocks, weight_hbm, up_ref, da_ref, weight_ref, sems = refs
    copies = fetch(weight_hbm, weight_ref, sems, 3)
    for i, block in enumerate(blocks):
        size = block.shape[0]
        up_ref[pl.ds(pl.multiple_of(place_ref[i] * size, size), size), :] = block[...]
    copies[3].wait()
    da_ref[...] = low(dot_nt(weight_ref[...], up_ref[...]))


def head_grad(head, p, p_low, q_ref, kt_ref, v_ref, da_ref, d_ref):
    features = da_ref.shape[0]
    dp = dot(v_ref[:, pair(head)], padded(da_ref, head))
    ds = low(p * (dp - jnp.sum(p * dp, axis=0, keepdims=True)))
    d_ref[own(head)] = low(dot(kt_ref[own(head)], ds) * SCALE)
    d_ref[features + head * WIDTH : features + (head + 1) * WIDTH] = low(dot_nt(q_ref[own(head)], ds))
    d_ref[2 * features + head * WIDTH : 2 * features + (head + 1) * WIDTH] = low(
        dot_nt(da_ref[own(head)], p_low)
    )


def middle_kernel(
    tokens_ref, up_ref, live_ref, da_ref, weight_hbm,
    out_ref, normed_ref, a_ref, d_ref,
    weight_ref, rows_ref, q_ref, k_ref, kt_ref, v_ref, vt_ref, bias_ref, wide_ref, sems,
):
    features = rows_ref.shape[1]
    copies = fetch(weight_hbm, weight_ref, sems, 0, 1, 2)
    bias_ref[...] = key_bias(live_ref[...])
    decode_midpoints(tokens_ref, wide_ref, rows_ref)
    normed = low(statistics(rows_ref[...])[0])
    normed_ref[...] = normed
    copies[0].wait()
    q_ref[...] = (low(dot(normed, columns(weight_ref, 0))) * SCALE).T
    copies[1].wait()
    k_ref[...] = low(dot(normed, columns(weight_ref, 1)))
    kt_ref[...] = k_ref[...].T
    copies[2].wait()
    v_ref[...] = low(dot(normed, columns(weight_ref, 2)))
    vt_ref[...] = v_ref[...].T
    for head in range(HEADS):
        scores = dot(k_ref[:, pair(head)], padded(q_ref, head)) + bias_ref[...]
        p = softmax_keys(scores)
        p_low = low(p)
        a_ref[own(head)] = low(dot(vt_ref[own(head)], p_low))
        head_grad(head, p, p_low, q_ref, kt_ref, v_ref, da_ref, d_ref)
    dh = low(dot(weight_ref[...], d_ref[...])).T
    encode_midpoints(
        up_ref[...].astype(jnp.float32) + layer_grad(rows_ref[...], dh), wide_ref, out_ref
    )


def backward_kernel(
    up_ref, weight_hbm, q_ref, kt_ref, v_ref, p_ref, d_ref, rows_ref, weight_ref, da_ref, wide_ref, sems
):
    copies = fetch(weight_hbm, weight_ref, sems, 3)
    decode(up_ref, wide_ref, rows_ref)
    copies[3].wait()
    da_ref[...] = low(dot_nt(weight_ref[...], rows_ref[...]))
    for head in range(HEADS):
        p_low = p_ref[head]
        head_grad(head, p_low.astype(jnp.float32), p_low, q_ref, kt_ref, v_ref, da_ref, d_ref)


def finish_kernel(tokens_ref, up_ref, d_ref, weight_hbm, out_ref, weight_ref, sems):
    features = tokens_ref.shape[1]
    copies = fetch(weight_hbm, weight_ref, sems, 0, 1, 2)
    total = None
    for part in range(3):
        copies[part].wait()
        term = dot(columns(weight_ref, part), d_ref[part * features : (part + 1) * features])
        total = term if total is None else total + term
    out_ref[...] = low(up_ref[...].astype(jnp.float32) + layer_grad(tokens_ref[...], low(total).T))


def weights_kernel(
    core_ref, normed_ref, up_ref, a_ref, d_ref, keep_hbm, send_hbm, upt_ref, keep_ref, send_ref, sems
):
    features = normed_ref.shape[1]
    groups, group = keep_ref.shape[:2]
    first = 3 * features // (2 * group)
    core = core_ref[0]
    sent = []
    upt_ref[...] = up_ref[...].T
    for place, (out_ref, out_hbm, which) in enumerate(
        ((send_ref, send_hbm, 1 - core), (keep_ref, keep_hbm, core))
    ):
        for step in range(groups):
            if step < first:
                start = pl.multiple_of((2 * step + which) * group, group)
                out_ref[step] = low(dot(d_ref[pl.ds(start, group), :], normed_ref[...]))
            else:
                start = pl.multiple_of((2 * (step - first) + which) * group, group)
                out_ref[step] = low(dot_nt(upt_ref[pl.ds(start, group), :], a_ref[...]))
            if step % 4 == 3:
                part = slice(step - 3, step + 1)
                sent.append(
                    pltpu.make_async_copy(
                        out_ref.at[part], out_hbm.at[part], sems.at[place * groups // 4 + step // 4]
                    )
                )
                sent[-1].start()
    for copy in sent:
        copy.wait()


BF = jnp.bfloat16
F32 = jnp.float32
HBM, VMEM = "hbm", "vmem"
PLACES = {
    HBM: pl.BlockSpec(memory_space=pltpu.HBM),
    VMEM: pl.BlockSpec(memory_space=pltpu.VMEM),
    "smem": pl.BlockSpec(memory_space=pltpu.SMEM),
}


def call(name, kernel, outs, args, scratch, sems, flops):
    moved = sum(math.prod(a.shape) * 2 for _, a in args) + sum(math.prod(s) * 2 for _, s in outs)
    return pl.pallas_call(
        kernel,
        out_shape=[jax.ShapeDtypeStruct(s, BF) for _, s in outs],
        in_specs=[PLACES[place] for place, _ in args],
        out_specs=[PLACES[place] for place, _ in outs],
        scratch_shapes=[pltpu.VMEM(s, t) for s, t in scratch]
        + [pltpu.SemaphoreType.DMA((n,)) for n in sems],
        compiler_params=pltpu.CompilerParams(vmem_limit_bytes=VMEM_LIMIT),
        cost_estimate=pl.CostEstimate(flops=int(flops), bytes_accessed=moved, transcendentals=0),
        name=name,
    )(*[a for _, a in args])


def offset_forward(tokens, live, weight):
    length, features = tokens.shape
    flat, turned, wide = (length, features), (features, length), (length * features // 128, 128)
    return call(
        "offset_forward",
        forward_kernel,
        [(VMEM, wide), (HBM, turned), (HBM, turned), (HBM, (HEADS, length, length))],
        [(VMEM, tokens), (VMEM, live), (HBM, weight)],
        [
            (weight.shape, BF), (turned, BF), (flat, BF), (turned, BF), (turned, BF),
            ((HEADS, length, length), BF), ((length, length), F32), (wide, F32),
        ],
        [4, HEADS + 2],
        4e9,
    )


def offset_residuals(tokens, weight):
    length, features = tokens.shape
    flat, turned = (length, features), (features, length)
    return call(
        "offset_residuals", residual_kernel, [(VMEM, flat), (VMEM, turned), (VMEM, flat)],
        [(VMEM, tokens), (HBM, weight)], [((features, 2 * features), BF)], [2], 1e9,
    )


def cotangent_heads(places, blocks, weight):
    features = blocks[0].shape[1]
    length = sum(block.shape[0] for block in blocks)
    return call(
        "cotangent_heads", cotangent_kernel, [(VMEM, (length, features)), (VMEM, (features, length))],
        [("smem", places), *[(VMEM, block) for block in blocks], (HBM, weight)],
        [((features, features), BF)], [1], 5e8,
    )


def midpoint_both(tokens, up, live, da, weight):
    length, features = up.shape
    flat, turned = (length, features), (features, length)
    return call(
        "midpoint_both", middle_kernel,
        [(VMEM, tokens.shape), (VMEM, flat), (VMEM, turned), (VMEM, (3 * features, length))],
        [(VMEM, tokens), (VMEM, up), (VMEM, live), (VMEM, da), (HBM, weight)],
        [
            ((features, 3 * features), BF), (flat, BF), (turned, BF), (flat, BF), (turned, BF), (flat, BF),
            (turned, BF), ((length, length), F32), (tokens.shape, F32),
        ],
        [3], 1e10,
    )


def offset_backward(up, weight, q, kt, v, p):
    features, length = q.shape
    return call(
        "offset_backward", backward_kernel,
        [(VMEM, (3 * features, length)), (VMEM, (length, features))],
        [(VMEM, up), (HBM, weight), (VMEM, q), (VMEM, kt), (VMEM, v), (VMEM, p)],
        [((features, features), BF), ((features, length), BF), (up.shape, F32)], [1], 5e9,
    )


def offset_finish(tokens, up, d, weight):
    features = tokens.shape[1]
    return call(
        "offset_finish", finish_kernel, [(VMEM, tokens.shape)],
        [(VMEM, tokens), (VMEM, up), (VMEM, d), (HBM, weight)],
        [((features, 3 * features), BF)], [3], 2e9,
    )[0]


def weight_terms(core, normed, up, a, d):
    length, features = normed.shape
    half = (16, features // 8, features)
    return call(
        "weight_terms", weights_kernel, [(HBM, half), (HBM, half)],
        [("smem", core), (VMEM, normed), (VMEM, up), (VMEM, a), (VMEM, d)],
        [((features, length), BF), (half, BF), (half, BF)], [8], 2e9,
    )


def add(*parts):
    total = parts[0].astype(jnp.float32)
    for part in parts[1:]:
        total = total + part.astype(jnp.float32)
    return total.astype(jnp.bfloat16)


def pick(array, index, axis):
    return lax.dynamic_index_in_dim(array, index, axis, keepdims=False)


SWAP = [(0, 1), (1, 0)]
ONWARD = [(i, (i + 1) % 4) for i in range(4)]
BACK = [(i, (i + 3) % 4) for i in range(4)]


def tie(*arrays):
    return lax.optimization_barrier(arrays)


def core_sum(keep, send):
    groups, group, features = keep.shape
    came = lax.ppermute(send, "core", SWAP)
    return add(keep, came).reshape(2, groups // 2, 4, group // 4, features)


def ring_first(held):
    y = lax.axis_index("y")
    far = pick(held, (y + 2) % 4, 2)
    right = pick(held, (y + 1) % 4, 2)
    left = pick(held, (y + 3) % 4, 2)
    return (
        lax.ppermute(far[0], "y", ONWARD),
        lax.ppermute(far[1], "y", BACK),
        lax.ppermute(right[1], "y", ONWARD),
        lax.ppermute(left[0], "y", BACK),
    )


def ring_second(held, came):
    y = lax.axis_index("y")
    right = pick(held, (y + 1) % 4, 2)
    left = pick(held, (y + 3) % 4, 2)
    own = pick(held, y, 2)
    first = lax.ppermute(add(right[0], came[0]), "y", ONWARD)
    second = lax.ppermute(add(left[1], came[1]), "y", BACK)
    return add(own[0], came[3], first), add(own[1], came[2], second)


def pair_sum(first, second):
    upper = lax.axis_index("xl") == 1
    keep, send = jnp.where(upper, second, first), jnp.where(upper, first, second)
    return add(keep, lax.ppermute(send, "xl", SWAP))


def last_sum(*halves):
    z, wide, features = halves[0].shape
    pieces = jnp.concatenate([half.reshape(2 * z, wide // 2, features) for half in halves], axis=1)
    arrived = lax.all_to_all(pieces, ("z", "xh"), split_axis=0, concat_axis=0, tiled=True)
    total = jnp.sum(arrived.astype(jnp.float32), axis=0).T
    return jnp.split(total, len(halves), axis=1)


def to_rows(cotangent):
    y, xh = lax.axis_index("y"), lax.axis_index("xh")
    came = [(2 * y + xh, pick(cotangent, 2 * y + xh, 0))]
    for step in range(4):
        for turn in range(2):
            if step == turn == 0:
                continue
            perm = [
                (2 * i + j, 2 * ((i + step) % 4) + (j ^ turn)) for i in range(4) for j in range(2)
            ]
            target = 2 * ((y + step) % 4) + (xh + turn) % 2
            source = 2 * ((y + 4 - step) % 4) + (xh + turn) % 2
            came.append((source, lax.ppermute(pick(cotangent, target, 0), MID, perm)))
    return came


def local(tokens, cotangent, mask, w_offset, w_midpoint):
    off_place = lax.axis_index(OFF)
    mid_place = lax.axis_index(MID)
    core = lax.axis_index("core").reshape(1).astype(jnp.int32)
    rows_dev, cols_dev, features = tokens.shape
    length = mask.shape[0]
    column_live = pick(mask, mid_place * cols_dev + off_place, 1).reshape(length, 1)
    row_live = pick(mask, off_place * rows_dev + mid_place, 0).reshape(length, 1)

    def exchange(wide):
        rows = wide.reshape(length, -1, 2, 128)
        rows = lax.all_to_all(rows, OFF + MID, split_axis=0, concat_axis=0, tiled=True)
        return rows.reshape(wide.shape)

    column_tokens = lax.all_to_all(
        jnp.swapaxes(tokens, 0, 1), OFF, split_axis=0, concat_axis=0, tiled=True
    ).reshape(length, features)
    places, blocks = zip(*to_rows(cotangent))
    column_tokens, *blocks = tie(column_tokens, *blocks)

    column_middle, q, a, p = offset_forward(column_tokens, column_live, w_offset)
    middle = exchange(column_middle)
    row_up, da_mid = cotangent_heads(jnp.stack(places).astype(jnp.int32), blocks, w_midpoint)
    column_normed, kt, v = offset_residuals(column_tokens, w_offset)
    row_wide, row_normed, a_mid, d_mid = midpoint_both(middle, row_up, row_live, da_mid, w_midpoint)
    column_wide = exchange(row_wide)
    mid_held = core_sum(*weight_terms(core, row_normed, row_up, a_mid, d_mid))
    mid_ring = ring_first(mid_held)
    column_wide, mid_held = tie(column_wide, mid_held)
    d_off, column_up = offset_backward(column_wide, w_offset, q, kt, v, p)
    d_off, *mid_ring = tie(d_off, *mid_ring)
    mid_pair = ring_second(mid_held, mid_ring)
    keep, send = weight_terms(core, column_normed, column_up, a, d_off)
    send, *mid_pair = tie(send, *mid_pair)
    mid_half = pair_sum(*mid_pair)
    column_out = offset_finish(column_tokens, column_up, d_off, w_offset)
    held = core_sum(keep, send)
    held, column_out, mid_half = tie(held, column_out, mid_half)
    grad_tokens = jnp.swapaxes(
        lax.all_to_all(
            column_out.reshape(cols_dev, rows_dev, features), OFF, split_axis=0, concat_axis=0, tiled=True
        ),
        0,
        1,
    )
    off_half = pair_sum(*ring_second(held, ring_first(held)))
    grad_off_weights, grad_mid_weights = last_sum(off_half, mid_half)
    return grad_tokens, grad_off_weights, grad_mid_weights


def solution(mesh):
    fine = Mesh(mesh.devices.reshape(2, 8, 2, 4, 2), OFF + MID)
    placed = (P(OFF, MID, None), P(OFF, MID, None), P(), P(), P())
    return jax.shard_map(
        local,
        mesh=fine,
        in_specs=placed,
        out_specs=(P(OFF, MID, None), P(None, OFF + MID), P(None, OFF + MID)),
        check_vma=False,
    )
```

```python
import math

import jax
import jax.numpy as jnp
from jax import lax
from jax.experimental import pallas as pl
from jax.experimental.pallas import tpu as pltpu
from jax.sharding import Mesh
from jax.sharding import PartitionSpec as P

HEADS = 12
WIDTH = 64
SCALE = 0.125
EPSILON = 1e-05
NEGATIVE = -1e30
OFF = ("xl", "z", "core")
MID = ("y", "xh")


NT = (((1,), (1,)), ((), ()))
VMEM_LIMIT = 60 * 1024 * 1024


def dot(left, right):
    return jnp.dot(left, right, preferred_element_type=jnp.float32)


def dot_nt(left, right):
    return lax.dot_general(left, right, NT, preferred_element_type=jnp.float32)


def low(value):
    return value.astype(jnp.bfloat16)


def statistics(values):
    widened = values.astype(jnp.float32)
    center = jnp.mean(widened, axis=-1, keepdims=True)
    shifted = widened - center
    inverse = lax.rsqrt(jnp.mean(shifted * shifted, axis=-1, keepdims=True) + EPSILON)
    return shifted * inverse, inverse


def layer_grad(values, incoming):
    scaled, inverse = statistics(values)
    incoming = incoming.astype(jnp.float32)
    return inverse * (
        incoming
        - jnp.mean(incoming, axis=-1, keepdims=True)
        - scaled * jnp.mean(incoming * scaled, axis=-1, keepdims=True)
    )


def key_bias(live):
    length = live.shape[0]
    keys = lax.broadcasted_iota(jnp.int32, (length, length), 0)
    queries = lax.broadcasted_iota(jnp.int32, (length, length), 1)
    allowed = jnp.logical_or(live == 1, keys == queries)
    return jnp.where(allowed, 0.0, NEGATIVE)


def padded(array, head):
    rows = array[head * WIDTH : (head + 1) * WIDTH]
    blank = jnp.zeros_like(rows)
    return jnp.concatenate([rows, blank] if head % 2 == 0 else [blank, rows], axis=0)


def pair(head):
    start = (head // 2) * 2 * WIDTH
    return slice(start, start + 2 * WIDTH)


def own(head):
    return slice(head * WIDTH, (head + 1) * WIDTH)


def softmax_keys(scores):
    expanded = jnp.exp(scores - jnp.max(scores, axis=0, keepdims=True))
    return expanded * (1.0 / jnp.sum(expanded, axis=0, keepdims=True))


def fetch(weight_hbm, weight_ref, sems, *parts):
    features = weight_hbm.shape[0]
    copies = {}
    for place, part in enumerate(parts):
        columns = slice(part * features, (part + 1) * features)
        copies[part] = pltpu.make_async_copy(
            weight_hbm.at[:, columns],
            weight_ref.at[:, place * features : (place + 1) * features],
            sems.at[place],
        )
        copies[part].start()
    return copies


def columns(weight_ref, place):
    features = weight_ref.shape[0]
    return weight_ref[:, place * features : (place + 1) * features]


def encode(rows, wide_ref, out_ref):
    chunks = rows.shape[1] // 128
    for c in range(chunks):
        wide_ref[pl.ds(c, rows.shape[0], stride=chunks), :] = rows[:, c * 128 : (c + 1) * 128]
    out_ref[...] = low(wide_ref[...])


def decode(in_ref, wide_ref, rows_ref):
    length, features = rows_ref.shape
    chunks = features // 128
    wide_ref[...] = in_ref[...].astype(jnp.float32)
    for c in range(chunks):
        rows_ref[:, c * 128 : (c + 1) * 128] = low(wide_ref[pl.ds(c, length, stride=chunks), :])


def encode_midpoints(rows, wide_ref, out_ref):
    chunks = rows.shape[1] // 128
    for m in range(8):
        for c in range(chunks):
            wide_ref[pl.ds(m * chunks + c, 32, stride=8 * chunks), :] = rows[
                m * 32 : (m + 1) * 32, c * 128 : (c + 1) * 128
            ]
    out_ref[...] = low(wide_ref[...])


def decode_midpoints(in_ref, wide_ref, rows_ref):
    chunks = rows_ref.shape[1] // 128
    wide_ref[...] = in_ref[...].astype(jnp.float32)
    for m in range(8):
        for c in range(chunks):
            rows_ref[m * 32 : (m + 1) * 32, c * 128 : (c + 1) * 128] = low(
                wide_ref[pl.ds(m * chunks + c, 32, stride=8 * chunks), :]
            )


def forward_kernel(
    tokens_ref, live_ref, weight_hbm, out_ref, q_hbm, a_hbm, p_hbm,
    weight_ref, q_ref, k_ref, v_ref, a_ref, p_ref, bias_ref, wide_ref, sems, out_sems,
):
    copies = fetch(weight_hbm, weight_ref, sems, 1, 0, 2, 3)
    bias_ref[...] = key_bias(live_ref[...])
    normed = low(statistics(tokens_ref[...])[0])
    copies[1].wait()
    k_ref[...] = low(dot(normed, columns(weight_ref, 0)))
    copies[0].wait()
    q_ref[...] = (low(dot(normed, columns(weight_ref, 1))) * SCALE).T
    copies[2].wait()
    v_ref[...] = low(dot(normed, columns(weight_ref, 2))).T
    sent = [pltpu.make_async_copy(q_ref, q_hbm, out_sems.at[HEADS])]
    sent[0].start()
    for head in range(HEADS):
        scores = dot(k_ref[:, pair(head)], padded(q_ref, head)) + bias_ref[...]
        p = low(softmax_keys(scores))
        p_ref[head] = p
        sent.append(pltpu.make_async_copy(p_ref.at[head], p_hbm.at[head], out_sems.at[head]))
        sent[-1].start()
        a_ref[own(head)] = low(dot(v_ref[own(head)], p))
    sent.append(pltpu.make_async_copy(a_ref, a_hbm, out_sems.at[HEADS + 1]))
    sent[-1].start()
    copies[3].wait()
    out = low(dot(a_ref[...].T, columns(weight_ref, 3)))
    encode(tokens_ref[...].astype(jnp.float32) + out.astype(jnp.float32), wide_ref, out_ref)
    for copy in sent:
        copy.wait()


def residual_kernel(tokens_ref, weight_hbm, normed_ref, kt_ref, v_ref, weight_ref, sems):
    copies = fetch(weight_hbm, weight_ref, sems, 1, 2)
    normed = low(statistics(tokens_ref[...])[0])
    normed_ref[...] = normed
    copies[1].wait()
    kt_ref[...] = low(dot(normed, columns(weight_ref, 0))).T
    copies[2].wait()
    v_ref[...] = low(dot(normed, columns(weight_ref, 1)))


def cotangent_kernel(place_ref, *refs):
    *blocks, weight_hbm, up_ref, upt_ref, da_ref, weight_ref, sems = refs
    copies = fetch(weight_hbm, weight_ref, sems, 3)
    for i, block in enumerate(blocks):
        size = block.shape[0]
        up_ref[pl.ds(pl.multiple_of(place_ref[i] * size, size), size), :] = block[...]
    upt_ref[...] = up_ref[...].T
    copies[3].wait()
    da_ref[...] = low(dot_nt(weight_ref[...], up_ref[...]))


def divide(core, d_ref, upt_ref, keep_ref, send_ref):
    group = 96
    first = d_ref.shape[0] // (2 * group)
    for out_ref, which in ((send_ref, 1 - core), (keep_ref, core)):
        for step in range(out_ref.shape[0] // group):
            source, at = (d_ref, step) if step < first else (upt_ref, step - first)
            start = pl.multiple_of((2 * at + which) * group, group)
            out_ref[step * group : (step + 1) * group] = source[pl.ds(start, group), :]


def head_grad(head, p, p_low, q_ref, kt_ref, v_ref, da_ref, d_ref):
    features = da_ref.shape[0]
    dp = dot(v_ref[:, pair(head)], padded(da_ref, head))
    ds = low(p * (dp - jnp.sum(p * dp, axis=0, keepdims=True)))
    d_ref[own(head)] = low(dot(kt_ref[own(head)], ds) * SCALE)
    d_ref[features + head * WIDTH : features + (head + 1) * WIDTH] = low(dot_nt(q_ref[own(head)], ds))
    d_ref[2 * features + head * WIDTH : 2 * features + (head + 1) * WIDTH] = low(
        dot_nt(da_ref[own(head)], p_low)
    )


def middle_kernel(
    core_ref, tokens_ref, up_ref, upt_ref, live_ref, da_ref, weight_hbm,
    out_ref, normed_ref, a_ref, keep_ref, send_ref,
    weight_ref, rows_ref, q_ref, k_ref, kt_ref, v_ref, vt_ref, d_ref, bias_ref, wide_ref, sems,
):
    copies = fetch(weight_hbm, weight_ref, sems, 0, 1, 2)
    bias_ref[...] = key_bias(live_ref[...])
    decode_midpoints(tokens_ref, wide_ref, rows_ref)
    normed = low(statistics(rows_ref[...])[0])
    normed_ref[...] = normed
    copies[0].wait()
    q_ref[...] = (low(dot(normed, columns(weight_ref, 0))) * SCALE).T
    copies[1].wait()
    k_ref[...] = low(dot(normed, columns(weight_ref, 1)))
    kt_ref[...] = k_ref[...].T
    copies[2].wait()
    v_ref[...] = low(dot(normed, columns(weight_ref, 2)))
    vt_ref[...] = v_ref[...].T
    for head in range(HEADS):
        scores = dot(k_ref[:, pair(head)], padded(q_ref, head)) + bias_ref[...]
        p = softmax_keys(scores)
        p_low = low(p)
        a_ref[own(head)] = low(dot(vt_ref[own(head)], p_low))
        head_grad(head, p, p_low, q_ref, kt_ref, v_ref, da_ref, d_ref)
    dh = low(dot(weight_ref[...], d_ref[...])).T
    divide(core_ref[0], d_ref, upt_ref, keep_ref, send_ref)
    encode_midpoints(
        up_ref[...].astype(jnp.float32) + layer_grad(rows_ref[...], dh), wide_ref, out_ref
    )


def backward_kernel(
    core_ref, up_ref, weight_hbm, q_hbm, kt_hbm, v_hbm, p_hbm,
    d_ref, rows_ref, keep_ref, send_ref,
    weight_ref, q_ref, kt_ref, v_ref, p_ref, da_ref, upt_ref, wide_ref, sems, in_sems,
):
    copies = fetch(weight_hbm, weight_ref, sems, 3)
    moved = [
        pltpu.make_async_copy(source, target, in_sems.at[i])
        for i, (source, target) in enumerate(
            ((v_hbm, v_ref), (p_hbm, p_ref), (kt_hbm, kt_ref), (q_hbm, q_ref))
        )
    ]
    for copy in moved:
        copy.start()
    decode(up_ref, wide_ref, rows_ref)
    copies[3].wait()
    da_ref[...] = low(dot_nt(weight_ref[...], rows_ref[...]))
    upt_ref[...] = rows_ref[...].T
    for copy in moved:
        copy.wait()
    for head in range(HEADS):
        p_low = p_ref[head]
        head_grad(head, p_low.astype(jnp.float32), p_low, q_ref, kt_ref, v_ref, da_ref, d_ref)
    divide(core_ref[0], d_ref, upt_ref, keep_ref, send_ref)


def finish_kernel(tokens_ref, up_ref, d_ref, weight_hbm, out_ref, weight_ref, sems):
    features = tokens_ref.shape[1]
    copies = fetch(weight_hbm, weight_ref, sems, 0, 1, 2)
    total = None
    for part in range(3):
        copies[part].wait()
        term = dot(columns(weight_ref, part), d_ref[part * features : (part + 1) * features])
        total = term if total is None else total + term
    out_ref[...] = low(up_ref[...].astype(jnp.float32) + layer_grad(tokens_ref[...], low(total).T))


def weights_kernel(y_ref, d_ref, d2_ref, normed_ref, normed2_ref, a_ref, a2_ref, *refs):
    *outs, sums_ref = refs
    y, group, share = y_ref[0], 96, 24
    first = 3 * normed_ref.shape[1] // (2 * group)
    for step in range(8):
        rows = slice(step * 2 * group, (step + 1) * 2 * group)
        if 2 * step < first:
            sums = dot(d_ref[rows], normed_ref[...]) + dot(d2_ref[rows], normed2_ref[...])
        else:
            sums = dot_nt(d_ref[rows], a_ref[...]) + dot_nt(d2_ref[rows], a2_ref[...])
        sums_ref[step] = sums
        place = step % 4
        for away in range(4):
            start = pl.multiple_of(lax.rem(y + away, 4) * share, 8)
            pieces = [sums_ref[step, pl.ds(start + i * group, share), :] for i in range(2)]
            outs[2 * away + step // 4][place * 2 * share : (place + 1) * 2 * share] = low(
                jnp.concatenate(pieces, axis=0)
            )


BF = jnp.bfloat16
F32 = jnp.float32
HBM, VMEM = "hbm", "vmem"
PLACES = {
    HBM: pl.BlockSpec(memory_space=pltpu.HBM),
    VMEM: pl.BlockSpec(memory_space=pltpu.VMEM),
    "smem": pl.BlockSpec(memory_space=pltpu.SMEM),
}


def call(name, kernel, outs, args, scratch, sems, flops):
    moved = sum(math.prod(a.shape) * 2 for _, a in args) + sum(math.prod(s) * 2 for _, s in outs)
    return pl.pallas_call(
        kernel,
        out_shape=[jax.ShapeDtypeStruct(s, BF) for _, s in outs],
        in_specs=[PLACES[place] for place, _ in args],
        out_specs=[PLACES[place] for place, _ in outs],
        scratch_shapes=[pltpu.VMEM(s, t) for s, t in scratch]
        + [pltpu.SemaphoreType.DMA((n,)) for n in sems],
        compiler_params=pltpu.CompilerParams(vmem_limit_bytes=VMEM_LIMIT),
        cost_estimate=pl.CostEstimate(flops=int(flops), bytes_accessed=moved, transcendentals=0),
        name=name,
    )(*[a for _, a in args])


def offset_forward(tokens, live, weight):
    length, features = tokens.shape
    flat, turned, wide = (length, features), (features, length), (length * features // 128, 128)
    return call(
        "offset_forward",
        forward_kernel,
        [(VMEM, wide), (HBM, turned), (HBM, turned), (HBM, (HEADS, length, length))],
        [(VMEM, tokens), (VMEM, live), (HBM, weight)],
        [
            (weight.shape, BF), (turned, BF), (flat, BF), (turned, BF), (turned, BF),
            ((HEADS, length, length), BF), ((length, length), F32), (wide, F32),
        ],
        [4, HEADS + 2],
        4e9,
    )


def offset_residuals(tokens, weight):
    length, features = tokens.shape
    flat, turned = (length, features), (features, length)
    return call(
        "offset_residuals", residual_kernel, [(VMEM, flat), (VMEM, turned), (VMEM, flat)],
        [(VMEM, tokens), (HBM, weight)], [((features, 2 * features), BF)], [2], 1e9,
    )


def cotangent_heads(places, blocks, weight):
    features = blocks[0].shape[1]
    length = sum(block.shape[0] for block in blocks)
    flat, turned = (length, features), (features, length)
    return call(
        "cotangent_heads", cotangent_kernel, [(VMEM, flat), (VMEM, turned), (VMEM, turned)],
        [("smem", places), *[(VMEM, block) for block in blocks], (HBM, weight)],
        [((features, features), BF)], [1], 5e8,
    )


def midpoint_both(core, tokens, up, up_t, live, da, weight):
    length, features = up.shape
    flat, turned, half = (length, features), (features, length), (2 * features, length)
    return call(
        "midpoint_both", middle_kernel,
        [(VMEM, tokens.shape), (VMEM, flat), (VMEM, turned), (VMEM, half), (VMEM, half)],
        [("smem", core), (VMEM, tokens), (VMEM, up), (VMEM, up_t), (VMEM, live), (VMEM, da), (HBM, weight)],
        [
            ((features, 3 * features), BF), (flat, BF), (turned, BF), (flat, BF), (turned, BF), (flat, BF),
            (turned, BF), ((3 * features, length), BF), ((length, length), F32), (tokens.shape, F32),
        ],
        [3], 1e10,
    )


def offset_backward(core, up, weight, q, kt, v, p):
    features, length = q.shape
    half = (2 * features, length)
    return call(
        "offset_backward", backward_kernel,
        [(VMEM, (3 * features, length)), (VMEM, (length, features)), (VMEM, half), (VMEM, half)],
        [("smem", core), (VMEM, up), (HBM, weight), (HBM, q), (HBM, kt), (HBM, v), (HBM, p)],
        [
            ((features, features), BF), (q.shape, BF), (kt.shape, BF), (v.shape, BF), (p.shape, BF),
            (q.shape, BF), (q.shape, BF), (up.shape, F32),
        ],
        [1, 4], 5e9,
    )


def offset_finish(tokens, up, d, weight):
    features = tokens.shape[1]
    return call(
        "offset_finish", finish_kernel, [(VMEM, tokens.shape)],
        [(VMEM, tokens), (VMEM, up), (VMEM, d), (HBM, weight)],
        [((features, 3 * features), BF)], [3], 2e9,
    )[0]


def weight_terms(y, *factors):
    features = factors[2].shape[1]
    return call(
        "weight_terms", weights_kernel, [(VMEM, (features // 4, features))] * 8,
        [("smem", y), *[(VMEM, factor) for factor in factors]],
        [((8, features // 4, features), F32)], [], 2.5e9,
    )


def add(*parts):
    total = parts[0].astype(jnp.float32)
    for part in parts[1:]:
        total = total + part.astype(jnp.float32)
    return total.astype(jnp.bfloat16)


def pick(array, index, axis):
    return lax.dynamic_index_in_dim(array, index, axis, keepdims=False)


SWAP = [(0, 1), (1, 0)]
ONWARD = [(i, (i + 1) % 4) for i in range(4)]
BACK = [(i, (i + 3) % 4) for i in range(4)]


def tie(*arrays):
    return lax.optimization_barrier(arrays)


def other_core(array):
    return lax.ppermute(array, "core", SWAP)


def ring_first(blocks):
    own0, own1, right0, right1, far0, far1, left0, left1 = blocks
    return (
        lax.ppermute(far0, "y", ONWARD),
        lax.ppermute(far1, "y", BACK),
        lax.ppermute(right1, "y", ONWARD),
        lax.ppermute(left0, "y", BACK),
    )


def ring_second(blocks, came):
    own0, own1, right0, right1, far0, far1, left0, left1 = blocks
    first = lax.ppermute(add(right0, came[0]), "y", ONWARD)
    second = lax.ppermute(add(left1, came[1]), "y", BACK)
    return add(own0, came[3], first), add(own1, came[2], second)


def pair_sum(first, second):
    upper = lax.axis_index("xl") == 1
    keep, send = jnp.where(upper, second, first), jnp.where(upper, first, second)
    return add(keep, lax.ppermute(send, "xl", SWAP))


def last_swap(block):
    share = block.shape[0] // 2
    xh = lax.axis_index("xh")
    keep = lax.dynamic_slice_in_dim(block, xh * share, share, 0)
    send = lax.dynamic_slice_in_dim(block, (1 - xh) * share, share, 0).astype(jnp.bfloat16)
    return (keep + lax.ppermute(send, "xh", SWAP).astype(jnp.float32)).T


def to_rows(cotangent):
    y, xh = lax.axis_index("y"), lax.axis_index("xh")
    came = [(2 * y + xh, pick(cotangent, 2 * y + xh, 0))]
    for step in range(4):
        for turn in range(2):
            if step == turn == 0:
                continue
            perm = [
                (2 * i + j, 2 * ((i + step) % 4) + (j ^ turn)) for i in range(4) for j in range(2)
            ]
            target = 2 * ((y + step) % 4) + (xh + turn) % 2
            source = 2 * ((y + 4 - step) % 4) + (xh + turn) % 2
            came.append((source, lax.ppermute(pick(cotangent, target, 0), MID, perm)))
    return came


def local(tokens, cotangent, mask, w_offset, w_midpoint):
    off_place = lax.axis_index(OFF)
    mid_place = lax.axis_index(MID)
    core = lax.axis_index("core").reshape(1).astype(jnp.int32)
    y = lax.axis_index("y").reshape(1).astype(jnp.int32)
    rows_dev, cols_dev, features = tokens.shape
    length = mask.shape[0]
    column_live = pick(mask, mid_place * cols_dev + off_place, 1).reshape(length, 1)
    row_live = pick(mask, off_place * rows_dev + mid_place, 0).reshape(length, 1)

    def exchange(wide):
        rows = wide.reshape(length, -1, 2, 128)
        rows = lax.all_to_all(rows, OFF + MID, split_axis=0, concat_axis=0, tiled=True)
        return rows.reshape(wide.shape)

    column_tokens = lax.all_to_all(
        jnp.swapaxes(tokens, 0, 1), OFF, split_axis=0, concat_axis=0, tiled=True
    ).reshape(length, features)
    places, blocks = zip(*to_rows(cotangent))

    column_middle, q, a, p = offset_forward(column_tokens, column_live, w_offset)
    column_middle, *blocks = tie(column_middle, *blocks)
    middle = exchange(column_middle)
    row_up, row_up_t, da_mid = cotangent_heads(
        jnp.stack(places).astype(jnp.int32), blocks, w_midpoint
    )
    column_normed, kt, v = offset_residuals(column_tokens, w_offset)
    normed2, a2 = other_core(column_normed), other_core(a)
    row_wide, row_normed, a_mid, keep, send = midpoint_both(
        core, middle, row_up, row_up_t, row_live, da_mid, w_midpoint
    )
    column_wide = exchange(row_wide)
    mid_blocks = weight_terms(
        y, keep, other_core(send), row_normed, other_core(row_normed), a_mid, other_core(a_mid)
    )
    mid_first = ring_first(mid_blocks)
    column_wide, normed2, a2, *mid_blocks = tie(column_wide, normed2, a2, *mid_blocks)
    d_off, column_up, keep, send = offset_backward(core, column_wide, w_offset, q, kt, v, p)
    came = other_core(send)
    column_out = offset_finish(column_tokens, column_up, d_off, w_offset)
    came, column_out, *mid_first = tie(came, column_out, *mid_first)
    off_blocks = weight_terms(y, keep, came, column_normed, normed2, a, a2)
    mid_pair = ring_second(mid_blocks, mid_first)
    off_first = ring_first(off_blocks)
    *off_first, mid_low, mid_high = tie(*off_first, *mid_pair)
    mid_half = pair_sum(mid_low, mid_high)
    grad_tokens = jnp.swapaxes(
        lax.all_to_all(
            column_out.reshape(cols_dev, rows_dev, features), OFF, split_axis=0, concat_axis=0, tiled=True
        ),
        0,
        1,
    )
    off_low, off_high = ring_second(off_blocks, off_first)
    mid_last = lax.psum_scatter(mid_half, "z", scatter_dimension=0, tiled=True)
    pieces = jnp.concatenate([off_low, off_high], axis=0).reshape(16, -1, features)
    arrived = lax.all_to_all(pieces, ("xl", "z"), split_axis=0, concat_axis=0, tiled=True)
    grad_off_weights = last_swap(jnp.sum(arrived.astype(jnp.float32), axis=0))
    grad_mid_weights = last_swap(mid_last.astype(jnp.float32))
    return grad_tokens, grad_off_weights, grad_mid_weights


def solution(mesh):
    fine = Mesh(mesh.devices.reshape(2, 8, 2, 4, 2), OFF + MID)
    placed = (P(OFF, MID, None), P(OFF, MID, None), P(), P(), P())
    return jax.shard_map(
        local,
        mesh=fine,
        in_specs=placed,
        out_specs=(P(OFF, MID, None), P(None, OFF + MID), P(None, OFF + MID)),
        check_vma=False,
    )
```

```python
import math

import jax
import jax.numpy as jnp
from jax import lax
from jax.experimental import pallas as pl
from jax.experimental.pallas import tpu as pltpu
from jax.sharding import Mesh
from jax.sharding import PartitionSpec as P

HEADS = 12
WIDTH = 64
SCALE = 0.125
EPSILON = 1e-05
NEGATIVE = -1e30
OFF = ("xl", "z", "core")
MID = ("y", "xh")


NT = (((1,), (1,)), ((), ()))
MIB = 1024 * 1024


def dot(left, right):
    return jnp.dot(left, right, preferred_element_type=jnp.float32)


def dot_nt(left, right):
    return lax.dot_general(left, right, NT, preferred_element_type=jnp.float32)


def low(value):
    return value.astype(jnp.bfloat16)


def statistics(values):
    widened = values.astype(jnp.float32)
    center = jnp.mean(widened, axis=-1, keepdims=True)
    shifted = widened - center
    inverse = lax.rsqrt(jnp.mean(shifted * shifted, axis=-1, keepdims=True) + EPSILON)
    return shifted * inverse, inverse


def layer_grad(values, incoming):
    scaled, inverse = statistics(values)
    incoming = incoming.astype(jnp.float32)
    return inverse * (
        incoming
        - jnp.mean(incoming, axis=-1, keepdims=True)
        - scaled * jnp.mean(incoming * scaled, axis=-1, keepdims=True)
    )


def key_bias(live):
    length = live.shape[0]
    keys = lax.broadcasted_iota(jnp.int32, (length, length), 0)
    queries = lax.broadcasted_iota(jnp.int32, (length, length), 1)
    allowed = jnp.logical_or(live == 1, keys == queries)
    return jnp.where(allowed, 0.0, NEGATIVE)


def padded(array, head):
    rows = array[head * WIDTH : (head + 1) * WIDTH]
    blank = jnp.zeros_like(rows)
    return jnp.concatenate([rows, blank] if head % 2 == 0 else [blank, rows], axis=0)


def pair(head):
    start = (head // 2) * 2 * WIDTH
    return slice(start, start + 2 * WIDTH)


def own(head):
    return slice(head * WIDTH, (head + 1) * WIDTH)


def softmax_keys(scores):
    expanded = jnp.exp(scores - jnp.max(scores, axis=0, keepdims=True))
    return expanded * (1.0 / jnp.sum(expanded, axis=0, keepdims=True))


def fetch(weight_hbm, weight_ref, sems, *parts):
    features = weight_hbm.shape[0]
    copies = {}
    for place, part in enumerate(parts):
        columns = slice(part * features, (part + 1) * features)
        copies[part] = pltpu.make_async_copy(
            weight_hbm.at[:, columns],
            weight_ref.at[:, place * features : (place + 1) * features],
            sems.at[place],
        )
        copies[part].start()
    return copies


def columns(weight_ref, place):
    features = weight_ref.shape[0]
    return weight_ref[:, place * features : (place + 1) * features]


def encode(rows, wide_ref, out_ref):
    chunks = rows.shape[1] // 128
    for c in range(chunks):
        wide_ref[pl.ds(c, rows.shape[0], stride=chunks), :] = rows[:, c * 128 : (c + 1) * 128]
    out_ref[...] = low(wide_ref[...])


def decode(in_ref, wide_ref, rows_ref):
    length, features = rows_ref.shape
    chunks = features // 128
    wide_ref[...] = in_ref[...].astype(jnp.float32)
    for c in range(chunks):
        rows_ref[:, c * 128 : (c + 1) * 128] = low(wide_ref[pl.ds(c, length, stride=chunks), :])


def encode_midpoints(rows, wide_ref, out_ref):
    chunks = rows.shape[1] // 128
    for m in range(8):
        for c in range(chunks):
            wide_ref[pl.ds(m * chunks + c, 32, stride=8 * chunks), :] = rows[
                m * 32 : (m + 1) * 32, c * 128 : (c + 1) * 128
            ]
    out_ref[...] = low(wide_ref[...])


def decode_midpoints(in_ref, wide_ref, rows_ref):
    chunks = rows_ref.shape[1] // 128
    wide_ref[...] = in_ref[...].astype(jnp.float32)
    for m in range(8):
        for c in range(chunks):
            rows_ref[m * 32 : (m + 1) * 32, c * 128 : (c + 1) * 128] = low(
                wide_ref[pl.ds(m * chunks + c, 32, stride=8 * chunks), :]
            )


def forward_kernel(
    tokens_ref, live_ref, weight_hbm, out_ref, q_hbm, a_hbm, p_hbm,
    weight_ref, q_ref, k_ref, v_ref, a_ref, p_ref, bias_ref, wide_ref, sems, out_sems,
):
    copies = fetch(weight_hbm, weight_ref, sems, 1, 0, 2, 3)
    bias_ref[...] = key_bias(live_ref[...])
    normed = low(statistics(tokens_ref[...])[0])
    copies[1].wait()
    k_ref[...] = low(dot(normed, columns(weight_ref, 0)))
    copies[0].wait()
    q_ref[...] = (low(dot(normed, columns(weight_ref, 1))) * SCALE).T
    copies[2].wait()
    v_ref[...] = low(dot(normed, columns(weight_ref, 2))).T
    sent = [pltpu.make_async_copy(q_ref, q_hbm, out_sems.at[HEADS])]
    sent[0].start()
    for head in range(HEADS):
        scores = dot(k_ref[:, pair(head)], padded(q_ref, head)) + bias_ref[...]
        p = low(softmax_keys(scores))
        p_ref[head] = p
        sent.append(pltpu.make_async_copy(p_ref.at[head], p_hbm.at[head], out_sems.at[head]))
        sent[-1].start()
        a_ref[own(head)] = low(dot(v_ref[own(head)], p))
    sent.append(pltpu.make_async_copy(a_ref, a_hbm, out_sems.at[HEADS + 1]))
    sent[-1].start()
    copies[3].wait()
    out = low(dot(a_ref[...].T, columns(weight_ref, 3)))
    encode(tokens_ref[...].astype(jnp.float32) + out.astype(jnp.float32), wide_ref, out_ref)
    for copy in sent:
        copy.wait()


def residual_kernel(tokens_ref, weight_hbm, normed_ref, kt_ref, v_ref, weight_ref, sems):
    copies = fetch(weight_hbm, weight_ref, sems, 1, 2)
    normed = low(statistics(tokens_ref[...])[0])
    normed_ref[...] = normed
    copies[1].wait()
    kt_ref[...] = low(dot(normed, columns(weight_ref, 0))).T
    copies[2].wait()
    v_ref[...] = low(dot(normed, columns(weight_ref, 1)))


def cotangent_kernel(place_ref, *refs):
    *blocks, weight_hbm, up_ref, upt_ref, da_ref, weight_ref, sems = refs
    copies = fetch(weight_hbm, weight_ref, sems, 3)
    for i, block in enumerate(blocks):
        size = block.shape[0]
        up_ref[pl.ds(pl.multiple_of(place_ref[i] * size, size), size), :] = block[...]
    upt_ref[...] = up_ref[...].T
    copies[3].wait()
    da_ref[...] = low(dot_nt(weight_ref[...], up_ref[...]))


def divide(core, d_ref, upt_ref, keep_ref, send_ref):
    group = 96
    first = d_ref.shape[0] // (2 * group)
    for out_ref, which in ((send_ref, 1 - core), (keep_ref, core)):
        for step in range(out_ref.shape[0] // group):
            source, at = (d_ref, step) if step < first else (upt_ref, step - first)
            start = pl.multiple_of((2 * at + which) * group, group)
            out_ref[step * group : (step + 1) * group] = source[pl.ds(start, group), :]


def head_grad(head, p, p_low, q_ref, kt_ref, v_ref, da_ref, d_ref):
    features = da_ref.shape[0]
    dp = dot(v_ref[:, pair(head)], padded(da_ref, head))
    ds = low(p * (dp - jnp.sum(p * dp, axis=0, keepdims=True)))
    d_ref[own(head)] = low(dot(kt_ref[own(head)], ds) * SCALE)
    d_ref[features + head * WIDTH : features + (head + 1) * WIDTH] = low(dot_nt(q_ref[own(head)], ds))
    d_ref[2 * features + head * WIDTH : 2 * features + (head + 1) * WIDTH] = low(
        dot_nt(da_ref[own(head)], p_low)
    )


def middle_kernel(
    core_ref, tokens_ref, up_ref, upt_ref, live_ref, da_ref, weight_hbm,
    out_ref, normed_hbm, a_hbm, keep_hbm, send_hbm,
    weight_ref, normed_ref, a_ref, keep_ref, send_ref, rows_ref, q_ref, k_ref, kt_ref, v_ref, vt_ref, d_ref, bias_ref, wide_ref, sems, out_sems,
):
    copies = fetch(weight_hbm, weight_ref, sems, 0, 1, 2)
    bias_ref[...] = key_bias(live_ref[...])
    decode_midpoints(tokens_ref, wide_ref, rows_ref)
    normed = low(statistics(rows_ref[...])[0])
    normed_ref[...] = normed
    sent = [
        pltpu.make_async_copy(source, target, out_sems.at[i])
        for i, (source, target) in enumerate(
            ((normed_ref, normed_hbm), (a_ref, a_hbm), (keep_ref, keep_hbm), (send_ref, send_hbm))
        )
    ]
    sent[0].start()
    copies[0].wait()
    q_ref[...] = (low(dot(normed, columns(weight_ref, 0))) * SCALE).T
    copies[1].wait()
    k_ref[...] = low(dot(normed, columns(weight_ref, 1)))
    kt_ref[...] = k_ref[...].T
    copies[2].wait()
    v_ref[...] = low(dot(normed, columns(weight_ref, 2)))
    vt_ref[...] = v_ref[...].T
    for head in range(HEADS):
        scores = dot(k_ref[:, pair(head)], padded(q_ref, head)) + bias_ref[...]
        p = softmax_keys(scores)
        p_low = low(p)
        a_ref[own(head)] = low(dot(vt_ref[own(head)], p_low))
        head_grad(head, p, p_low, q_ref, kt_ref, v_ref, da_ref, d_ref)
    sent[1].start()
    divide(core_ref[0], d_ref, upt_ref, keep_ref, send_ref)
    sent[2].start()
    sent[3].start()
    dh = low(dot(weight_ref[...], d_ref[...])).T
    encode_midpoints(
        up_ref[...].astype(jnp.float32) + layer_grad(rows_ref[...], dh), wide_ref, out_ref
    )
    for copy in sent:
        copy.wait()


def backward_kernel(
    core_ref, up_ref, weight_hbm, q_hbm, kt_hbm, v_hbm, p_hbm,
    d_ref, rows_ref, keep_ref, send_ref,
    weight_ref, q_ref, kt_ref, v_ref, p_ref, da_ref, upt_ref, wide_ref, sems, in_sems,
):
    copies = fetch(weight_hbm, weight_ref, sems, 3)
    moved = [
        pltpu.make_async_copy(source, target, in_sems.at[i])
        for i, (source, target) in enumerate(
            ((v_hbm, v_ref), (p_hbm, p_ref), (kt_hbm, kt_ref), (q_hbm, q_ref))
        )
    ]
    for copy in moved:
        copy.start()
    decode(up_ref, wide_ref, rows_ref)
    copies[3].wait()
    da_ref[...] = low(dot_nt(weight_ref[...], rows_ref[...]))
    upt_ref[...] = rows_ref[...].T
    for copy in moved:
        copy.wait()
    for head in range(HEADS):
        p_low = p_ref[head]
        head_grad(head, p_low.astype(jnp.float32), p_low, q_ref, kt_ref, v_ref, da_ref, d_ref)
    divide(core_ref[0], d_ref, upt_ref, keep_ref, send_ref)


def finish_kernel(tokens_ref, up_ref, d_ref, weight_hbm, out_ref, weight_ref, sems):
    features = tokens_ref.shape[1]
    copies = fetch(weight_hbm, weight_ref, sems, 0, 1, 2)
    total = None
    for part in range(3):
        copies[part].wait()
        term = dot(columns(weight_ref, part), d_ref[part * features : (part + 1) * features])
        total = term if total is None else total + term
    out_ref[...] = low(up_ref[...].astype(jnp.float32) + layer_grad(tokens_ref[...], low(total).T))


def weights_kernel(y_ref, d_ref, d2_ref, normed_ref, normed2_ref, a_ref, a2_ref, *refs):
    outs_hbm, outs, (sums_ref, sems) = refs[:8], refs[8:16], refs[16:]
    sent = [pltpu.make_async_copy(outs[i], outs_hbm[i], sems.at[i]) for i in range(8)]
    y, group, share = y_ref[0], 96, 24
    first = 3 * normed_ref.shape[1] // (2 * group)
    for step in range(8):
        rows = slice(step * 2 * group, (step + 1) * 2 * group)
        if 2 * step < first:
            sums = dot(d_ref[rows], normed_ref[...]) + dot(d2_ref[rows], normed2_ref[...])
        else:
            sums = dot_nt(d_ref[rows], a_ref[...]) + dot_nt(d2_ref[rows], a2_ref[...])
        sums_ref[step] = sums
        place = step % 4
        for away in range(4):
            start = pl.multiple_of(lax.rem(y + away, 4) * share, 8)
            pieces = [sums_ref[step, pl.ds(start + i * group, share), :] for i in range(2)]
            outs[2 * away + step // 4][place * 2 * share : (place + 1) * 2 * share] = low(
                jnp.concatenate(pieces, axis=0)
            )
            if place == 3:
                sent[2 * away + step // 4].start()
    for copy in sent:
        copy.wait()


BF = jnp.bfloat16
F32 = jnp.float32
HBM, VMEM = "hbm", "vmem"
PLACES = {
    HBM: pl.BlockSpec(memory_space=pltpu.HBM),
    VMEM: pl.BlockSpec(memory_space=pltpu.VMEM),
    "smem": pl.BlockSpec(memory_space=pltpu.SMEM),
}


def call(name, kernel, outs, args, scratch, sems, flops, limit=60):
    moved = sum(math.prod(a.shape) * 2 for _, a in args) + sum(math.prod(s) * 2 for _, s in outs)
    return pl.pallas_call(
        kernel,
        out_shape=[jax.ShapeDtypeStruct(s, BF) for _, s in outs],
        in_specs=[PLACES[place] for place, _ in args],
        out_specs=[PLACES[place] for place, _ in outs],
        scratch_shapes=[pltpu.VMEM(s, t) for s, t in scratch]
        + [pltpu.SemaphoreType.DMA((n,)) for n in sems],
        compiler_params=pltpu.CompilerParams(vmem_limit_bytes=limit * MIB),
        cost_estimate=pl.CostEstimate(flops=int(flops), bytes_accessed=moved, transcendentals=0),
        name=name,
    )(*[a for _, a in args])


def offset_forward(tokens, live, weight):
    length, features = tokens.shape
    flat, turned, wide = (length, features), (features, length), (length * features // 128, 128)
    return call(
        "offset_forward",
        forward_kernel,
        [(VMEM, wide), (HBM, turned), (HBM, turned), (HBM, (HEADS, length, length))],
        [(VMEM, tokens), (VMEM, live), (HBM, weight)],
        [
            (weight.shape, BF), (turned, BF), (flat, BF), (turned, BF), (turned, BF),
            ((HEADS, length, length), BF), ((length, length), F32), (wide, F32),
        ],
        [4, HEADS + 2],
        4e9,
    )


def offset_residuals(tokens, weight):
    length, features = tokens.shape
    flat, turned = (length, features), (features, length)
    return call(
        "offset_residuals", residual_kernel, [(VMEM, flat), (VMEM, turned), (VMEM, flat)],
        [(VMEM, tokens), (HBM, weight)], [((features, 2 * features), BF)], [2], 1e9,
    )


def cotangent_heads(places, blocks, weight):
    features = blocks[0].shape[1]
    length = sum(block.shape[0] for block in blocks)
    flat, turned = (length, features), (features, length)
    return call(
        "cotangent_heads", cotangent_kernel, [(VMEM, flat), (VMEM, turned), (VMEM, turned)],
        [("smem", places), *[(VMEM, block) for block in blocks], (HBM, weight)],
        [((features, features), BF)], [1], 5e8,
    )


def midpoint_both(core, tokens, up, up_t, live, da, weight):
    length, features = up.shape
    flat, turned, half = (length, features), (features, length), (2 * features, length)
    return call(
        "midpoint_both", middle_kernel,
        [(VMEM, tokens.shape), (HBM, flat), (HBM, turned), (HBM, half), (HBM, half)],
        [("smem", core), (VMEM, tokens), (VMEM, up), (VMEM, up_t), (VMEM, live), (VMEM, da), (HBM, weight)],
        [
            ((features, 3 * features), BF), (flat, BF), (turned, BF), (half, BF), (half, BF),
            (flat, BF), (turned, BF), (flat, BF), (turned, BF), (flat, BF), (turned, BF), ((3 * features, length), BF), ((length, length), F32), (tokens.shape, F32),
        ],
        [3, 4], 1e10,
    )


def offset_backward(core, up, weight, q, kt, v, p):
    features, length = q.shape
    half = (2 * features, length)
    return call(
        "offset_backward", backward_kernel,
        [(VMEM, (3 * features, length)), (VMEM, (length, features)), (VMEM, half), (VMEM, half)],
        [("smem", core), (VMEM, up), (HBM, weight), (HBM, q), (HBM, kt), (HBM, v), (HBM, p)],
        [
            ((features, features), BF), (q.shape, BF), (kt.shape, BF), (v.shape, BF), (p.shape, BF),
            (q.shape, BF), (q.shape, BF), (up.shape, F32),
        ],
        [1, 4], 5e9, 48,
    )


def offset_finish(tokens, up, d, weight):
    features = tokens.shape[1]
    return call(
        "offset_finish", finish_kernel, [(VMEM, tokens.shape)],
        [(VMEM, tokens), (VMEM, up), (VMEM, d), (HBM, weight)],
        [((features, 3 * features), BF)], [3], 2e9, 48,
    )[0]


def weight_terms(y, *factors):
    features = factors[2].shape[1]
    return call(
        "weight_terms", weights_kernel, [(HBM, (features // 4, features))] * 8,
        [("smem", y), *[(VMEM, factor) for factor in factors]],
        [((features // 4, features), BF)] * 8 + [((8, features // 4, features), F32)], [8], 2.5e9,
    )


def add(*parts):
    total = parts[0].astype(jnp.float32)
    for part in parts[1:]:
        total = total + part.astype(jnp.float32)
    return total.astype(jnp.bfloat16)


def pick(array, index, axis):
    return lax.dynamic_index_in_dim(array, index, axis, keepdims=False)


SWAP = [(0, 1), (1, 0)]
ONWARD = [(i, (i + 1) % 4) for i in range(4)]
BACK = [(i, (i + 3) % 4) for i in range(4)]


def tie(*arrays):
    return lax.optimization_barrier(arrays)


def other_core(array):
    return lax.ppermute(array, "core", SWAP)


def ring_first(blocks):
    own0, own1, right0, right1, far0, far1, left0, left1 = blocks
    return (
        lax.ppermute(far0, "y", ONWARD),
        lax.ppermute(far1, "y", BACK),
        lax.ppermute(right1, "y", ONWARD),
        lax.ppermute(left0, "y", BACK),
    )


def ring_second(blocks, came):
    own0, own1, right0, right1, far0, far1, left0, left1 = blocks
    first = lax.ppermute(add(right0, came[0]), "y", ONWARD)
    second = lax.ppermute(add(left1, came[1]), "y", BACK)
    return add(own0, came[3], first), add(own1, came[2], second)


def last_sum(*pairs):
    share = pairs[0][0].shape[0] // 16
    features = pairs[0][0].shape[1]
    pieces = [jnp.concatenate(pair, axis=0).reshape(32, share, features) for pair in pairs]
    arrived = lax.all_to_all(
        jnp.concatenate(pieces, axis=1), ("xl", "z", "xh"), split_axis=0, concat_axis=0, tiled=True
    )
    return jnp.split(jnp.sum(arrived.astype(jnp.float32), axis=0).T, len(pairs), axis=1)


def to_rows(cotangent):
    y, xh = lax.axis_index("y"), lax.axis_index("xh")
    came = [(2 * y + xh, pick(cotangent, 2 * y + xh, 0))]
    for step in range(4):
        for turn in range(2):
            if step == turn == 0:
                continue
            perm = [
                (2 * i + j, 2 * ((i + step) % 4) + (j ^ turn)) for i in range(4) for j in range(2)
            ]
            target = 2 * ((y + step) % 4) + (xh + turn) % 2
            source = 2 * ((y + 4 - step) % 4) + (xh + turn) % 2
            came.append((source, lax.ppermute(pick(cotangent, target, 0), MID, perm)))
    return came


def local(tokens, cotangent, mask, w_offset, w_midpoint):
    off_place = lax.axis_index(OFF)
    mid_place = lax.axis_index(MID)
    core = lax.axis_index("core").reshape(1).astype(jnp.int32)
    y = lax.axis_index("y").reshape(1).astype(jnp.int32)
    rows_dev, cols_dev, features = tokens.shape
    length = mask.shape[0]
    column_live = pick(mask, mid_place * cols_dev + off_place, 1).reshape(length, 1)
    row_live = pick(mask, off_place * rows_dev + mid_place, 0).reshape(length, 1)

    def exchange(wide):
        rows = wide.reshape(length, -1, 2, 128)
        rows = lax.all_to_all(rows, OFF + MID, split_axis=0, concat_axis=0, tiled=True)
        return rows.reshape(wide.shape)

    column_tokens = lax.all_to_all(
        jnp.swapaxes(tokens, 0, 1), OFF, split_axis=0, concat_axis=0, tiled=True
    ).reshape(length, features)
    places, blocks = zip(*to_rows(cotangent))

    column_middle, q, a, p = offset_forward(column_tokens, column_live, w_offset)
    column_middle, *blocks = tie(column_middle, *blocks)
    middle = exchange(column_middle)
    row_up, row_up_t, da_mid = cotangent_heads(
        jnp.stack(places).astype(jnp.int32), blocks, w_midpoint
    )
    column_normed, kt, v = offset_residuals(column_tokens, w_offset)
    normed2, a2 = other_core(column_normed), other_core(a)
    row_wide, row_normed, a_mid, keep, send = midpoint_both(
        core, middle, row_up, row_up_t, row_live, da_mid, w_midpoint
    )
    column_wide = exchange(row_wide)
    mid_blocks = weight_terms(
        y, keep, other_core(send), row_normed, other_core(row_normed), a_mid, other_core(a_mid)
    )
    mid_first = ring_first(mid_blocks)
    column_wide, normed2, a2, *mid_blocks = tie(column_wide, normed2, a2, *mid_blocks)
    d_off, column_up, keep, send = offset_backward(core, column_wide, w_offset, q, kt, v, p)
    send, *mid_first = tie(send, *mid_first)
    came = other_core(send)
    mid_pair = ring_second(mid_blocks, mid_first)
    column_out = offset_finish(column_tokens, column_up, d_off, w_offset)
    came, column_out, *mid_pair = tie(came, column_out, *mid_pair)
    off_blocks = weight_terms(y, keep, came, column_normed, normed2, a, a2)
    off_first = ring_first(off_blocks)
    grad_tokens = jnp.swapaxes(
        lax.all_to_all(
            column_out.reshape(cols_dev, rows_dev, features), OFF, split_axis=0, concat_axis=0, tiled=True
        ),
        0,
        1,
    )
    off_pair = ring_second(off_blocks, off_first)
    grad_off_weights, grad_mid_weights = last_sum(off_pair, mid_pair)
    return grad_tokens, grad_off_weights, grad_mid_weights


def solution(mesh):
    fine = Mesh(mesh.devices.reshape(2, 8, 2, 4, 2), OFF + MID)
    placed = (P(OFF, MID, None), P(OFF, MID, None), P(), P(), P())
    return jax.shard_map(
        local,
        mesh=fine,
        in_specs=placed,
        out_specs=(P(OFF, MID, None), P(None, OFF + MID), P(None, OFF + MID)),
        check_vma=False,
    )
```

```python
import math

import jax
import jax.numpy as jnp
from jax import lax
from jax.experimental import pallas as pl
from jax.experimental.pallas import tpu as pltpu
from jax.sharding import Mesh
from jax.sharding import PartitionSpec as P

HEADS = 12
WIDTH = 64
SCALE = 0.125
EPSILON = 1e-05
NEGATIVE = -1e30
OFF = ("xl", "z", "core")
MID = ("y", "xh")


NT = (((1,), (1,)), ((), ()))
MIB = 1024 * 1024


def dot(left, right):
    return jnp.dot(left, right, preferred_element_type=jnp.float32)


def dot_nt(left, right):
    return lax.dot_general(left, right, NT, preferred_element_type=jnp.float32)


def low(value):
    return value.astype(jnp.bfloat16)


def statistics(values):
    widened = values.astype(jnp.float32)
    center = jnp.mean(widened, axis=-1, keepdims=True)
    shifted = widened - center
    inverse = lax.rsqrt(jnp.mean(shifted * shifted, axis=-1, keepdims=True) + EPSILON)
    return shifted * inverse, inverse


def layer_grad(values, incoming):
    scaled, inverse = statistics(values)
    incoming = incoming.astype(jnp.float32)
    return inverse * (
        incoming
        - jnp.mean(incoming, axis=-1, keepdims=True)
        - scaled * jnp.mean(incoming * scaled, axis=-1, keepdims=True)
    )


def key_bias(live):
    length = live.shape[0]
    keys = lax.broadcasted_iota(jnp.int32, (length, length), 0)
    queries = lax.broadcasted_iota(jnp.int32, (length, length), 1)
    allowed = jnp.logical_or(live == 1, keys == queries)
    return jnp.where(allowed, 0.0, NEGATIVE)


def padded(array, head):
    rows = array[head * WIDTH : (head + 1) * WIDTH]
    blank = jnp.zeros_like(rows)
    return jnp.concatenate([rows, blank] if head % 2 == 0 else [blank, rows], axis=0)


def pair(head):
    start = (head // 2) * 2 * WIDTH
    return slice(start, start + 2 * WIDTH)


def own(head):
    return slice(head * WIDTH, (head + 1) * WIDTH)


def softmax_keys(scores):
    expanded = jnp.exp(scores - jnp.max(scores, axis=0, keepdims=True))
    return expanded * (1.0 / jnp.sum(expanded, axis=0, keepdims=True))


def fetch(weight_hbm, weight_ref, sems, *parts):
    features = weight_hbm.shape[0]
    copies = {}
    for place, part in enumerate(parts):
        columns = slice(part * features, (part + 1) * features)
        copies[part] = pltpu.make_async_copy(
            weight_hbm.at[:, columns],
            weight_ref.at[:, place * features : (place + 1) * features],
            sems.at[place],
        )
        copies[part].start()
    return copies


def columns(weight_ref, place):
    features = weight_ref.shape[0]
    return weight_ref[:, place * features : (place + 1) * features]


def encode(rows, wide_ref, out_ref):
    chunks = rows.shape[1] // 128
    for c in range(chunks):
        wide_ref[pl.ds(c, rows.shape[0], stride=chunks), :] = rows[:, c * 128 : (c + 1) * 128]
    out_ref[...] = low(wide_ref[...])


def decode(in_ref, wide_ref, rows_ref):
    length, features = rows_ref.shape
    chunks = features // 128
    wide_ref[...] = in_ref[...].astype(jnp.float32)
    for c in range(chunks):
        rows_ref[:, c * 128 : (c + 1) * 128] = low(wide_ref[pl.ds(c, length, stride=chunks), :])


def encode_midpoints(rows, wide_ref, out_ref):
    chunks = rows.shape[1] // 128
    for m in range(8):
        for c in range(chunks):
            wide_ref[pl.ds(m * chunks + c, 32, stride=8 * chunks), :] = rows[
                m * 32 : (m + 1) * 32, c * 128 : (c + 1) * 128
            ]
    out_ref[...] = low(wide_ref[...])


def decode_midpoints(in_ref, wide_ref, rows_ref):
    chunks = rows_ref.shape[1] // 128
    wide_ref[...] = in_ref[...].astype(jnp.float32)
    for m in range(8):
        for c in range(chunks):
            rows_ref[m * 32 : (m + 1) * 32, c * 128 : (c + 1) * 128] = low(
                wide_ref[pl.ds(m * chunks + c, 32, stride=8 * chunks), :]
            )


def forward_kernel(
    tokens_ref, live_ref, weight_hbm, out_ref, q_hbm, a_hbm, p_hbm,
    weight_ref, q_ref, k_ref, v_ref, a_ref, p_ref, bias_ref, wide_ref, sems, out_sems,
):
    copies = fetch(weight_hbm, weight_ref, sems, 1, 0, 2, 3)
    bias_ref[...] = key_bias(live_ref[...])
    normed = low(statistics(tokens_ref[...])[0])
    copies[1].wait()
    k_ref[...] = low(dot(normed, columns(weight_ref, 0)))
    copies[0].wait()
    q_ref[...] = (low(dot(normed, columns(weight_ref, 1))) * SCALE).T
    copies[2].wait()
    v_ref[...] = low(dot(normed, columns(weight_ref, 2))).T
    sent = [pltpu.make_async_copy(q_ref, q_hbm, out_sems.at[HEADS])]
    sent[0].start()
    for head in range(HEADS):
        scores = dot(k_ref[:, pair(head)], padded(q_ref, head)) + bias_ref[...]
        p = low(softmax_keys(scores))
        p_ref[head] = p
        sent.append(pltpu.make_async_copy(p_ref.at[head], p_hbm.at[head], out_sems.at[head]))
        sent[-1].start()
        a_ref[own(head)] = low(dot(v_ref[own(head)], p))
    sent.append(pltpu.make_async_copy(a_ref, a_hbm, out_sems.at[HEADS + 1]))
    sent[-1].start()
    copies[3].wait()
    out = low(dot(a_ref[...].T, columns(weight_ref, 3)))
    encode(tokens_ref[...].astype(jnp.float32) + out.astype(jnp.float32), wide_ref, out_ref)
    for copy in sent:
        copy.wait()


def residual_kernel(tokens_ref, weight_hbm, normed_ref, kt_ref, v_ref, weight_ref, sems):
    copies = fetch(weight_hbm, weight_ref, sems, 1, 2)
    normed = low(statistics(tokens_ref[...])[0])
    normed_ref[...] = normed
    copies[1].wait()
    kt_ref[...] = low(dot(normed, columns(weight_ref, 0))).T
    copies[2].wait()
    v_ref[...] = low(dot(normed, columns(weight_ref, 1)))


def cotangent_kernel(place_ref, *refs):
    *blocks, weight_hbm, up_ref, upt_ref, da_ref, weight_ref, sems = refs
    copies = fetch(weight_hbm, weight_ref, sems, 3)
    for i, block in enumerate(blocks):
        size = block.shape[0]
        up_ref[pl.ds(pl.multiple_of(place_ref[i] * size, size), size), :] = block[...]
    upt_ref[...] = up_ref[...].T
    copies[3].wait()
    da_ref[...] = low(dot_nt(weight_ref[...], up_ref[...]))


def divide(core, d_ref, upt_ref, keep_ref, send_ref):
    group = 96
    first = d_ref.shape[0] // (2 * group)
    for out_ref, which in ((send_ref, 1 - core), (keep_ref, core)):
        for step in range(out_ref.shape[0] // group):
            source, at = (d_ref, step) if step < first else (upt_ref, step - first)
            start = pl.multiple_of((2 * at + which) * group, group)
            out_ref[step * group : (step + 1) * group] = source[pl.ds(start, group), :]


def head_grad(head, p, p_low, q_ref, kt_ref, v_ref, da_ref, d_ref):
    features = da_ref.shape[0]
    dp = dot(v_ref[:, pair(head)], padded(da_ref, head))
    ds = low(p * (dp - jnp.sum(p * dp, axis=0, keepdims=True)))
    d_ref[own(head)] = low(dot(kt_ref[own(head)], ds) * SCALE)
    d_ref[features + head * WIDTH : features + (head + 1) * WIDTH] = low(dot_nt(q_ref[own(head)], ds))
    d_ref[2 * features + head * WIDTH : 2 * features + (head + 1) * WIDTH] = low(
        dot_nt(da_ref[own(head)], p_low)
    )


def middle_kernel(
    core_ref, tokens_ref, up_ref, upt_ref, live_ref, da_ref, weight_hbm,
    out_ref, normed_hbm, a_hbm, keep_hbm, send_hbm,
    weight_ref, normed_ref, a_ref, keep_ref, send_ref, rows_ref, q_ref, k_ref, kt_ref, v_ref, vt_ref, d_ref, bias_ref, wide_ref, sems, out_sems,
):
    copies = fetch(weight_hbm, weight_ref, sems, 0, 1, 2)
    bias_ref[...] = key_bias(live_ref[...])
    decode_midpoints(tokens_ref, wide_ref, rows_ref)
    normed = low(statistics(rows_ref[...])[0])
    normed_ref[...] = normed
    sent = [
        pltpu.make_async_copy(source, target, out_sems.at[i])
        for i, (source, target) in enumerate(
            ((normed_ref, normed_hbm), (a_ref, a_hbm), (keep_ref, keep_hbm), (send_ref, send_hbm))
        )
    ]
    sent[0].start()
    copies[0].wait()
    q_ref[...] = (low(dot(normed, columns(weight_ref, 0))) * SCALE).T
    copies[1].wait()
    k_ref[...] = low(dot(normed, columns(weight_ref, 1)))
    kt_ref[...] = k_ref[...].T
    copies[2].wait()
    v_ref[...] = low(dot(normed, columns(weight_ref, 2)))
    vt_ref[...] = v_ref[...].T
    for head in range(HEADS):
        scores = dot(k_ref[:, pair(head)], padded(q_ref, head)) + bias_ref[...]
        p = softmax_keys(scores)
        p_low = low(p)
        a_ref[own(head)] = low(dot(vt_ref[own(head)], p_low))
        head_grad(head, p, p_low, q_ref, kt_ref, v_ref, da_ref, d_ref)
    sent[1].start()
    divide(core_ref[0], d_ref, upt_ref, keep_ref, send_ref)
    sent[2].start()
    sent[3].start()
    dh = low(dot(weight_ref[...], d_ref[...])).T
    encode_midpoints(
        up_ref[...].astype(jnp.float32) + layer_grad(rows_ref[...], dh), wide_ref, out_ref
    )
    for copy in sent:
        copy.wait()


def backward_kernel(
    core_ref, up_ref, weight_hbm, q_hbm, kt_hbm, v_hbm, p_hbm,
    d_ref, rows_ref, keep_ref, send_ref,
    weight_ref, q_ref, kt_ref, v_ref, p_ref, da_ref, upt_ref, wide_ref, sems, in_sems,
):
    copies = fetch(weight_hbm, weight_ref, sems, 3)
    moved = [
        pltpu.make_async_copy(source, target, in_sems.at[i])
        for i, (source, target) in enumerate(
            ((v_hbm, v_ref), (p_hbm, p_ref), (kt_hbm, kt_ref), (q_hbm, q_ref))
        )
    ]
    for copy in moved:
        copy.start()
    decode(up_ref, wide_ref, rows_ref)
    copies[3].wait()
    da_ref[...] = low(dot_nt(weight_ref[...], rows_ref[...]))
    upt_ref[...] = rows_ref[...].T
    for copy in moved:
        copy.wait()
    for head in range(HEADS):
        p_low = p_ref[head]
        head_grad(head, p_low.astype(jnp.float32), p_low, q_ref, kt_ref, v_ref, da_ref, d_ref)
    divide(core_ref[0], d_ref, upt_ref, keep_ref, send_ref)


def finish_kernel(tokens_ref, up_ref, d_ref, weight_hbm, out_ref, weight_ref, sems):
    features = tokens_ref.shape[1]
    copies = fetch(weight_hbm, weight_ref, sems, 0, 1, 2)
    total = None
    for part in range(3):
        copies[part].wait()
        term = dot(columns(weight_ref, part), d_ref[part * features : (part + 1) * features])
        total = term if total is None else total + term
    out_ref[...] = low(up_ref[...].astype(jnp.float32) + layer_grad(tokens_ref[...], low(total).T))


def weights_kernel(y_ref, d_ref, d2_ref, normed_ref, normed2_ref, a_ref, a2_ref, *refs):
    outs_hbm, outs, (sums_ref, sems) = refs[:8], refs[8:16], refs[16:]
    sent = [pltpu.make_async_copy(outs[i], outs_hbm[i], sems.at[i]) for i in range(8)]
    y, group, share = y_ref[0], 96, 24
    first = 3 * normed_ref.shape[1] // (2 * group)
    for step in range(8):
        rows = slice(step * 2 * group, (step + 1) * 2 * group)
        if 2 * step < first:
            sums = dot(d_ref[rows], normed_ref[...]) + dot(d2_ref[rows], normed2_ref[...])
        else:
            sums = dot_nt(d_ref[rows], a_ref[...]) + dot_nt(d2_ref[rows], a2_ref[...])
        sums_ref[step] = sums
        place = step % 4
        for away in range(4):
            start = pl.multiple_of(lax.rem(y + away, 4) * share, 8)
            pieces = [sums_ref[step, pl.ds(start + i * group, share), :] for i in range(2)]
            outs[2 * away + step // 4][place * 2 * share : (place + 1) * 2 * share] = low(
                jnp.concatenate(pieces, axis=0)
            )
            if place == 3:
                sent[2 * away + step // 4].start()
    for copy in sent:
        copy.wait()


BF = jnp.bfloat16
F32 = jnp.float32
HBM, VMEM = "hbm", "vmem"
PLACES = {
    HBM: pl.BlockSpec(memory_space=pltpu.HBM),
    VMEM: pl.BlockSpec(memory_space=pltpu.VMEM),
    "smem": pl.BlockSpec(memory_space=pltpu.SMEM),
}


def call(name, kernel, outs, args, scratch, sems, flops, limit=60):
    moved = sum(math.prod(a.shape) * 2 for _, a in args) + sum(math.prod(s) * 2 for _, s in outs)
    return pl.pallas_call(
        kernel,
        out_shape=[jax.ShapeDtypeStruct(s, BF) for _, s in outs],
        in_specs=[PLACES[place] for place, _ in args],
        out_specs=[PLACES[place] for place, _ in outs],
        scratch_shapes=[pltpu.VMEM(s, t) for s, t in scratch]
        + [pltpu.SemaphoreType.DMA((n,)) for n in sems],
        compiler_params=pltpu.CompilerParams(vmem_limit_bytes=limit * MIB),
        cost_estimate=pl.CostEstimate(flops=int(flops), bytes_accessed=moved, transcendentals=0),
        name=name,
    )(*[a for _, a in args])


def offset_forward(tokens, live, weight):
    length, features = tokens.shape
    flat, turned, wide = (length, features), (features, length), (length * features // 128, 128)
    return call(
        "offset_forward",
        forward_kernel,
        [(VMEM, wide), (HBM, turned), (HBM, turned), (HBM, (HEADS, length, length))],
        [(VMEM, tokens), (VMEM, live), (HBM, weight)],
        [
            (weight.shape, BF), (turned, BF), (flat, BF), (turned, BF), (turned, BF),
            ((HEADS, length, length), BF), ((length, length), F32), (wide, F32),
        ],
        [4, HEADS + 2],
        4e9,
    )


def offset_residuals(tokens, weight):
    length, features = tokens.shape
    flat, turned = (length, features), (features, length)
    return call(
        "offset_residuals", residual_kernel, [(VMEM, flat), (VMEM, turned), (VMEM, flat)],
        [(VMEM, tokens), (HBM, weight)], [((features, 2 * features), BF)], [2], 1e9,
    )


def cotangent_heads(places, blocks, weight):
    features = blocks[0].shape[1]
    length = sum(block.shape[0] for block in blocks)
    flat, turned = (length, features), (features, length)
    return call(
        "cotangent_heads", cotangent_kernel, [(VMEM, flat), (VMEM, turned), (VMEM, turned)],
        [("smem", places), *[(VMEM, block) for block in blocks], (HBM, weight)],
        [((features, features), BF)], [1], 5e8,
    )


def midpoint_both(core, tokens, up, up_t, live, da, weight):
    length, features = up.shape
    flat, turned, half = (length, features), (features, length), (2 * features, length)
    return call(
        "midpoint_both", middle_kernel,
        [(VMEM, tokens.shape), (HBM, flat), (HBM, turned), (HBM, half), (HBM, half)],
        [("smem", core), (VMEM, tokens), (VMEM, up), (VMEM, up_t), (VMEM, live), (VMEM, da), (HBM, weight)],
        [
            ((features, 3 * features), BF), (flat, BF), (turned, BF), (half, BF), (half, BF),
            (flat, BF), (turned, BF), (flat, BF), (turned, BF), (flat, BF), (turned, BF), ((3 * features, length), BF), ((length, length), F32), (tokens.shape, F32),
        ],
        [3, 4], 1e10,
    )


def offset_backward(core, up, weight, q, kt, v, p):
    features, length = q.shape
    half = (2 * features, length)
    return call(
        "offset_backward", backward_kernel,
        [(VMEM, (3 * features, length)), (VMEM, (length, features)), (VMEM, half), (VMEM, half)],
        [("smem", core), (VMEM, up), (HBM, weight), (HBM, q), (HBM, kt), (HBM, v), (HBM, p)],
        [
            ((features, features), BF), (q.shape, BF), (kt.shape, BF), (v.shape, BF), (p.shape, BF),
            (q.shape, BF), (q.shape, BF), (up.shape, F32),
        ],
        [1, 4], 5e9, 48,
    )


def offset_finish(tokens, up, d, weight):
    features = tokens.shape[1]
    return call(
        "offset_finish", finish_kernel, [(VMEM, tokens.shape)],
        [(VMEM, tokens), (VMEM, up), (VMEM, d), (HBM, weight)],
        [((features, 3 * features), BF)], [3], 2e9, 48,
    )[0]


def weight_terms(y, *factors):
    features = factors[2].shape[1]
    return call(
        "weight_terms", weights_kernel, [(HBM, (features // 4, features))] * 8,
        [("smem", y), *[(VMEM, factor) for factor in factors]],
        [((features // 4, features), BF)] * 8 + [((8, features // 4, features), F32)], [8], 2.5e9,
    )


def add(*parts):
    total = parts[0].astype(jnp.float32)
    for part in parts[1:]:
        total = total + part.astype(jnp.float32)
    return total.astype(jnp.bfloat16)


def pick(array, index, axis):
    return lax.dynamic_index_in_dim(array, index, axis, keepdims=False)


SWAP = [(0, 1), (1, 0)]
ONWARD = [(i, (i + 1) % 4) for i in range(4)]
BACK = [(i, (i + 3) % 4) for i in range(4)]


def tie(*arrays):
    return lax.optimization_barrier(arrays)


def other_core(array):
    return lax.ppermute(array, "core", SWAP)


def ring_first(blocks):
    own0, own1, right0, right1, far0, far1, left0, left1 = blocks
    return (
        lax.ppermute(far0, "y", ONWARD),
        lax.ppermute(far1, "y", BACK),
        lax.ppermute(right1, "y", ONWARD),
        lax.ppermute(left0, "y", BACK),
    )


def ring_second(blocks, came):
    own0, own1, right0, right1, far0, far1, left0, left1 = blocks
    first = lax.ppermute(add(right0, came[0]), "y", ONWARD)
    second = lax.ppermute(add(left1, came[1]), "y", BACK)
    return add(own0, came[3], first), add(own1, came[2], second)


def last_exchange(first, second):
    blocks = jnp.concatenate([first, second], axis=0)
    pieces = blocks.reshape(32, blocks.shape[0] // 32, blocks.shape[1])
    return lax.all_to_all(pieces, ("xl", "z", "xh"), split_axis=0, concat_axis=0, tiled=True)


def last_sum(arrived):
    return jnp.sum(arrived.astype(jnp.float32), axis=0).T


def to_rows(cotangent):
    y, xh = lax.axis_index("y"), lax.axis_index("xh")
    came = [(2 * y + xh, pick(cotangent, 2 * y + xh, 0))]
    for step in range(4):
        for turn in range(2):
            if step == turn == 0:
                continue
            perm = [
                (2 * i + j, 2 * ((i + step) % 4) + (j ^ turn)) for i in range(4) for j in range(2)
            ]
            target = 2 * ((y + step) % 4) + (xh + turn) % 2
            source = 2 * ((y + 4 - step) % 4) + (xh + turn) % 2
            came.append((source, lax.ppermute(pick(cotangent, target, 0), MID, perm)))
    return came


def local(tokens, cotangent, mask, w_offset, w_midpoint):
    off_place = lax.axis_index(OFF)
    mid_place = lax.axis_index(MID)
    core = lax.axis_index("core").reshape(1).astype(jnp.int32)
    y = lax.axis_index("y").reshape(1).astype(jnp.int32)
    rows_dev, cols_dev, features = tokens.shape
    length = mask.shape[0]
    column_live = pick(mask, mid_place * cols_dev + off_place, 1).reshape(length, 1)
    row_live = pick(mask, off_place * rows_dev + mid_place, 0).reshape(length, 1)

    def exchange(wide):
        rows = wide.reshape(length, -1, 2, 128)
        rows = lax.all_to_all(rows, OFF + MID, split_axis=0, concat_axis=0, tiled=True)
        return rows.reshape(wide.shape)

    column_tokens = lax.all_to_all(
        jnp.swapaxes(tokens, 0, 1), OFF, split_axis=0, concat_axis=0, tiled=True
    ).reshape(length, features)
    places, blocks = zip(*to_rows(cotangent))

    column_middle, q, a, p = offset_forward(column_tokens, column_live, w_offset)
    column_middle, *blocks = tie(column_middle, *blocks)
    middle = exchange(column_middle)
    row_up, row_up_t, da_mid = cotangent_heads(
        jnp.stack(places).astype(jnp.int32), blocks, w_midpoint
    )
    column_normed, kt, v = offset_residuals(column_tokens, w_offset)
    normed2, a2 = other_core(column_normed), other_core(a)
    middle, column_normed, kt, v = tie(middle, column_normed, kt, v)
    row_wide, row_normed, a_mid, keep, send = midpoint_both(
        core, middle, row_up, row_up_t, row_live, da_mid, w_midpoint
    )
    column_wide = exchange(row_wide)
    mid_blocks = weight_terms(
        y, keep, other_core(send), row_normed, other_core(row_normed), a_mid, other_core(a_mid)
    )
    mid_first = ring_first(mid_blocks)
    column_wide, normed2, a2, *mid_blocks = tie(column_wide, normed2, a2, *mid_blocks)
    d_off, column_up, keep, send = offset_backward(core, column_wide, w_offset, q, kt, v, p)
    came = other_core(send)
    d_off, *mid_first = tie(d_off, *mid_first)
    column_out = offset_finish(column_tokens, column_up, d_off, w_offset)
    came, column_out = tie(came, column_out)
    arrived = lax.all_to_all(
        column_out.reshape(cols_dev, rows_dev, features), OFF, split_axis=0, concat_axis=0, tiled=True
    )
    off_blocks = weight_terms(y, keep, came, column_normed, normed2, a, a2)
    off_first = ring_first(off_blocks)
    mid_pair = ring_second(mid_blocks, mid_first)
    *off_first, mid_low, mid_high = tie(*off_first, *mid_pair)
    arrived, mid_low, mid_high = tie(arrived, mid_low, mid_high)
    mid_arrived = last_exchange(mid_low, mid_high)
    off_low, off_high = ring_second(off_blocks, off_first)
    mid_arrived, off_low, off_high = tie(mid_arrived, off_low, off_high)
    grad_off_weights = last_sum(last_exchange(off_low, off_high))
    return jnp.swapaxes(arrived, 0, 1), grad_off_weights, last_sum(mid_arrived)


def solution(mesh):
    fine = Mesh(mesh.devices.reshape(2, 8, 2, 4, 2), OFF + MID)
    placed = (P(OFF, MID, None), P(OFF, MID, None), P(), P(), P())
    return jax.shard_map(
        local,
        mesh=fine,
        in_specs=placed,
        out_specs=(P(OFF, MID, None), P(None, OFF + MID), P(None, OFF + MID)),
        check_vma=False,
    )
```

```python
import math

import jax
import jax.numpy as jnp
from jax import lax
from jax.experimental import pallas as pl
from jax.experimental.pallas import tpu as pltpu
from jax.sharding import Mesh
from jax.sharding import PartitionSpec as P

HEADS = 12
WIDTH = 64
SCALE = 0.125
EPSILON = 1e-05
NEGATIVE = -1e30
OFF = ("xl", "z", "core")
MID = ("y", "xh")


NT = (((1,), (1,)), ((), ()))
MIB = 1024 * 1024


def dot(left, right):
    return jnp.dot(left, right, preferred_element_type=jnp.float32)


def dot_nt(left, right):
    return lax.dot_general(left, right, NT, preferred_element_type=jnp.float32)


def low(value):
    return value.astype(jnp.bfloat16)


def statistics(values):
    widened = values.astype(jnp.float32)
    center = jnp.mean(widened, axis=-1, keepdims=True)
    shifted = widened - center
    inverse = lax.rsqrt(jnp.mean(shifted * shifted, axis=-1, keepdims=True) + EPSILON)
    return shifted * inverse, inverse


def layer_grad(values, incoming):
    scaled, inverse = statistics(values)
    incoming = incoming.astype(jnp.float32)
    return inverse * (
        incoming
        - jnp.mean(incoming, axis=-1, keepdims=True)
        - scaled * jnp.mean(incoming * scaled, axis=-1, keepdims=True)
    )


def key_bias(live):
    length = live.shape[0]
    keys = lax.broadcasted_iota(jnp.int32, (length, length), 0)
    queries = lax.broadcasted_iota(jnp.int32, (length, length), 1)
    allowed = jnp.logical_or(live == 1, keys == queries)
    return jnp.where(allowed, 0.0, NEGATIVE)


def padded(array, head):
    rows = array[head * WIDTH : (head + 1) * WIDTH]
    blank = jnp.zeros_like(rows)
    return jnp.concatenate([rows, blank] if head % 2 == 0 else [blank, rows], axis=0)


def pair(head):
    start = (head // 2) * 2 * WIDTH
    return slice(start, start + 2 * WIDTH)


def own(head):
    return slice(head * WIDTH, (head + 1) * WIDTH)


def softmax_keys(scores):
    expanded = jnp.exp(scores - jnp.max(scores, axis=0, keepdims=True))
    return expanded * (1.0 / jnp.sum(expanded, axis=0, keepdims=True))


def fetch(weight_hbm, weight_ref, sems, *parts):
    features = weight_hbm.shape[0]
    copies = {}
    for place, part in enumerate(parts):
        columns = slice(part * features, (part + 1) * features)
        copies[part] = pltpu.make_async_copy(
            weight_hbm.at[:, columns],
            weight_ref.at[:, place * features : (place + 1) * features],
            sems.at[place],
        )
        copies[part].start()
    return copies


def columns(weight_ref, place):
    features = weight_ref.shape[0]
    return weight_ref[:, place * features : (place + 1) * features]


def encode(rows, wide_ref, out_ref):
    chunks = rows.shape[1] // 128
    for c in range(chunks):
        wide_ref[pl.ds(c, rows.shape[0], stride=chunks), :] = rows[:, c * 128 : (c + 1) * 128]
    out_ref[...] = low(wide_ref[...])


def decode(in_ref, wide_ref, rows_ref):
    length, features = rows_ref.shape
    chunks = features // 128
    wide_ref[...] = in_ref[...].astype(jnp.float32)
    for c in range(chunks):
        rows_ref[:, c * 128 : (c + 1) * 128] = low(wide_ref[pl.ds(c, length, stride=chunks), :])


def encode_midpoints(rows, wide_ref, out_ref):
    chunks = rows.shape[1] // 128
    for m in range(8):
        for c in range(chunks):
            wide_ref[pl.ds(m * chunks + c, 32, stride=8 * chunks), :] = rows[
                m * 32 : (m + 1) * 32, c * 128 : (c + 1) * 128
            ]
    out_ref[...] = low(wide_ref[...])


def decode_midpoints(in_ref, wide_ref, rows_ref):
    chunks = rows_ref.shape[1] // 128
    wide_ref[...] = in_ref[...].astype(jnp.float32)
    for m in range(8):
        for c in range(chunks):
            rows_ref[m * 32 : (m + 1) * 32, c * 128 : (c + 1) * 128] = low(
                wide_ref[pl.ds(m * chunks + c, 32, stride=8 * chunks), :]
            )


def forward_kernel(
    tokens_ref, live_ref, weight_hbm, out_ref, q_hbm, a_hbm, p_hbm,
    weight_ref, q_ref, k_ref, v_ref, a_ref, p_ref, bias_ref, wide_ref, sems, out_sems,
):
    copies = fetch(weight_hbm, weight_ref, sems, 1, 0, 2, 3)
    bias_ref[...] = key_bias(live_ref[...])
    normed = low(statistics(tokens_ref[...])[0])
    copies[1].wait()
    k_ref[...] = low(dot(normed, columns(weight_ref, 0)))
    copies[0].wait()
    q_ref[...] = (low(dot(normed, columns(weight_ref, 1))) * SCALE).T
    copies[2].wait()
    v_ref[...] = low(dot(normed, columns(weight_ref, 2))).T
    sent = [pltpu.make_async_copy(q_ref, q_hbm, out_sems.at[HEADS])]
    sent[0].start()
    for head in range(HEADS):
        scores = dot(k_ref[:, pair(head)], padded(q_ref, head)) + bias_ref[...]
        p = low(softmax_keys(scores))
        p_ref[head] = p
        sent.append(pltpu.make_async_copy(p_ref.at[head], p_hbm.at[head], out_sems.at[head]))
        sent[-1].start()
        a_ref[own(head)] = low(dot(v_ref[own(head)], p))
    sent.append(pltpu.make_async_copy(a_ref, a_hbm, out_sems.at[HEADS + 1]))
    sent[-1].start()
    copies[3].wait()
    out = low(dot(a_ref[...].T, columns(weight_ref, 3)))
    encode(tokens_ref[...].astype(jnp.float32) + out.astype(jnp.float32), wide_ref, out_ref)
    for copy in sent:
        copy.wait()


def residual_kernel(tokens_ref, weight_hbm, normed_ref, kt_ref, v_ref, weight_ref, sems):
    copies = fetch(weight_hbm, weight_ref, sems, 1, 2)
    normed = low(statistics(tokens_ref[...])[0])
    normed_ref[...] = normed
    copies[1].wait()
    kt_ref[...] = low(dot(normed, columns(weight_ref, 0))).T
    copies[2].wait()
    v_ref[...] = low(dot(normed, columns(weight_ref, 1)))


def cotangent_kernel(place_ref, *refs):
    *blocks, weight_hbm, up_ref, upt_ref, da_ref, weight_ref, sems = refs
    copies = fetch(weight_hbm, weight_ref, sems, 3)
    for i, block in enumerate(blocks):
        size = block.shape[0]
        up_ref[pl.ds(pl.multiple_of(place_ref[i] * size, size), size), :] = block[...]
    upt_ref[...] = up_ref[...].T
    copies[3].wait()
    da_ref[...] = low(dot_nt(weight_ref[...], up_ref[...]))


def divide(core, d_ref, upt_ref, keep_ref, send_ref):
    group = 96
    first = d_ref.shape[0] // (2 * group)
    for out_ref, which in ((send_ref, 1 - core), (keep_ref, core)):
        for step in range(out_ref.shape[0] // group):
            source, at = (d_ref, step) if step < first else (upt_ref, step - first)
            start = pl.multiple_of((2 * at + which) * group, group)
            out_ref[step * group : (step + 1) * group] = source[pl.ds(start, group), :]


def head_grad(head, p, p_low, q_ref, kt_ref, v_ref, da_ref, d_ref):
    features = da_ref.shape[0]
    dp = dot(v_ref[:, pair(head)], padded(da_ref, head))
    ds = low(p * (dp - jnp.sum(p * dp, axis=0, keepdims=True)))
    d_ref[own(head)] = low(dot(kt_ref[own(head)], ds) * SCALE)
    d_ref[features + head * WIDTH : features + (head + 1) * WIDTH] = low(dot_nt(q_ref[own(head)], ds))
    d_ref[2 * features + head * WIDTH : 2 * features + (head + 1) * WIDTH] = low(
        dot_nt(da_ref[own(head)], p_low)
    )


def middle_kernel(
    core_ref, tokens_ref, up_ref, upt_ref, live_ref, da_ref, weight_hbm,
    out_ref, normed_hbm, a_hbm, keep_hbm, send_hbm,
    weight_ref, normed_ref, a_ref, keep_ref, send_ref, rows_ref, q_ref, k_ref, kt_ref, v_ref, vt_ref, d_ref, bias_ref, wide_ref, sems, out_sems,
):
    copies = fetch(weight_hbm, weight_ref, sems, 0, 1, 2)
    bias_ref[...] = key_bias(live_ref[...])
    decode_midpoints(tokens_ref, wide_ref, rows_ref)
    normed = low(statistics(rows_ref[...])[0])
    normed_ref[...] = normed
    sent = [
        pltpu.make_async_copy(source, target, out_sems.at[i])
        for i, (source, target) in enumerate(
            ((normed_ref, normed_hbm), (a_ref, a_hbm), (keep_ref, keep_hbm), (send_ref, send_hbm))
        )
    ]
    sent[0].start()
    copies[0].wait()
    q_ref[...] = (low(dot(normed, columns(weight_ref, 0))) * SCALE).T
    copies[1].wait()
    k_ref[...] = low(dot(normed, columns(weight_ref, 1)))
    kt_ref[...] = k_ref[...].T
    copies[2].wait()
    v_ref[...] = low(dot(normed, columns(weight_ref, 2)))
    vt_ref[...] = v_ref[...].T
    for head in range(HEADS):
        scores = dot(k_ref[:, pair(head)], padded(q_ref, head)) + bias_ref[...]
        p = softmax_keys(scores)
        p_low = low(p)
        a_ref[own(head)] = low(dot(vt_ref[own(head)], p_low))
        head_grad(head, p, p_low, q_ref, kt_ref, v_ref, da_ref, d_ref)
    sent[1].start()
    divide(core_ref[0], d_ref, upt_ref, keep_ref, send_ref)
    sent[2].start()
    sent[3].start()
    dh = low(dot(weight_ref[...], d_ref[...])).T
    encode_midpoints(
        up_ref[...].astype(jnp.float32) + layer_grad(rows_ref[...], dh), wide_ref, out_ref
    )
    for copy in sent:
        copy.wait()


def backward_kernel(
    core_ref, up_ref, weight_hbm, q_hbm, kt_hbm, v_hbm, p_hbm,
    d_ref, rows_ref, keep_ref, send_ref,
    weight_ref, q_ref, kt_ref, v_ref, p_ref, da_ref, upt_ref, wide_ref, sems, in_sems,
):
    copies = fetch(weight_hbm, weight_ref, sems, 3)
    moved = [
        pltpu.make_async_copy(source, target, in_sems.at[i])
        for i, (source, target) in enumerate(
            ((v_hbm, v_ref), (p_hbm, p_ref), (kt_hbm, kt_ref), (q_hbm, q_ref))
        )
    ]
    for copy in moved:
        copy.start()
    decode(up_ref, wide_ref, rows_ref)
    copies[3].wait()
    da_ref[...] = low(dot_nt(weight_ref[...], rows_ref[...]))
    upt_ref[...] = rows_ref[...].T
    for copy in moved:
        copy.wait()
    for head in range(HEADS):
        p_low = p_ref[head]
        head_grad(head, p_low.astype(jnp.float32), p_low, q_ref, kt_ref, v_ref, da_ref, d_ref)
    divide(core_ref[0], d_ref, upt_ref, keep_ref, send_ref)


def finish_kernel(tokens_ref, up_ref, d_ref, weight_hbm, out_ref, weight_ref, sems):
    features = tokens_ref.shape[1]
    copies = fetch(weight_hbm, weight_ref, sems, 0, 1, 2)
    total = None
    for part in range(3):
        copies[part].wait()
        term = dot(columns(weight_ref, part), d_ref[part * features : (part + 1) * features])
        total = term if total is None else total + term
    out_ref[...] = low(up_ref[...].astype(jnp.float32) + layer_grad(tokens_ref[...], low(total).T))


def weights_kernel(y_ref, d_ref, d2_ref, normed_ref, normed2_ref, a_ref, a2_ref, *refs):
    outs_hbm, outs, (sums_ref, sems) = refs[:8], refs[8:16], refs[16:]
    sent = [pltpu.make_async_copy(outs[i], outs_hbm[i], sems.at[i]) for i in range(8)]
    y, group, share = y_ref[0], 96, 24
    first = 3 * normed_ref.shape[1] // (2 * group)
    for step in range(8):
        rows = slice(step * 2 * group, (step + 1) * 2 * group)
        if 2 * step < first:
            sums = dot(d_ref[rows], normed_ref[...]) + dot(d2_ref[rows], normed2_ref[...])
        else:
            sums = dot_nt(d_ref[rows], a_ref[...]) + dot_nt(d2_ref[rows], a2_ref[...])
        sums_ref[step] = sums
        place = step % 4
        for away in range(4):
            start = pl.multiple_of(lax.rem(y + away, 4) * share, 8)
            pieces = [sums_ref[step, pl.ds(start + i * group, share), :] for i in range(2)]
            outs[2 * away + step // 4][place * 2 * share : (place + 1) * 2 * share] = low(
                jnp.concatenate(pieces, axis=0)
            )
            if place == 3:
                sent[2 * away + step // 4].start()
    for copy in sent:
        copy.wait()


BF = jnp.bfloat16
F32 = jnp.float32
HBM, VMEM = "hbm", "vmem"
PLACES = {
    HBM: pl.BlockSpec(memory_space=pltpu.HBM),
    VMEM: pl.BlockSpec(memory_space=pltpu.VMEM),
    "smem": pl.BlockSpec(memory_space=pltpu.SMEM),
}


def call(name, kernel, outs, args, scratch, sems, flops, limit=60):
    moved = sum(math.prod(a.shape) * 2 for _, a in args) + sum(math.prod(s) * 2 for _, s in outs)
    return pl.pallas_call(
        kernel,
        out_shape=[jax.ShapeDtypeStruct(s, BF) for _, s in outs],
        in_specs=[PLACES[place] for place, _ in args],
        out_specs=[PLACES[place] for place, _ in outs],
        scratch_shapes=[pltpu.VMEM(s, t) for s, t in scratch]
        + [pltpu.SemaphoreType.DMA((n,)) for n in sems],
        compiler_params=pltpu.CompilerParams(vmem_limit_bytes=limit * MIB),
        cost_estimate=pl.CostEstimate(flops=int(flops), bytes_accessed=moved, transcendentals=0),
        name=name,
    )(*[a for _, a in args])


def offset_forward(tokens, live, weight):
    length, features = tokens.shape
    flat, turned, wide = (length, features), (features, length), (length * features // 128, 128)
    return call(
        "offset_forward",
        forward_kernel,
        [(VMEM, wide), (HBM, turned), (HBM, turned), (HBM, (HEADS, length, length))],
        [(VMEM, tokens), (VMEM, live), (HBM, weight)],
        [
            (weight.shape, BF), (turned, BF), (flat, BF), (turned, BF), (turned, BF),
            ((HEADS, length, length), BF), ((length, length), F32), (wide, F32),
        ],
        [4, HEADS + 2],
        4e9,
    )


def offset_residuals(tokens, weight):
    length, features = tokens.shape
    flat, turned = (length, features), (features, length)
    return call(
        "offset_residuals", residual_kernel, [(VMEM, flat), (VMEM, turned), (VMEM, flat)],
        [(VMEM, tokens), (HBM, weight)], [((features, 2 * features), BF)], [2], 1e9,
    )


def cotangent_heads(places, blocks, weight):
    features = blocks[0].shape[1]
    length = sum(block.shape[0] for block in blocks)
    flat, turned = (length, features), (features, length)
    return call(
        "cotangent_heads", cotangent_kernel, [(VMEM, flat), (VMEM, turned), (VMEM, turned)],
        [("smem", places), *[(VMEM, block) for block in blocks], (HBM, weight)],
        [((features, features), BF)], [1], 5e8,
    )


def midpoint_both(core, tokens, up, up_t, live, da, weight):
    length, features = up.shape
    flat, turned, half = (length, features), (features, length), (2 * features, length)
    return call(
        "midpoint_both", middle_kernel,
        [(VMEM, tokens.shape), (HBM, flat), (HBM, turned), (HBM, half), (HBM, half)],
        [("smem", core), (VMEM, tokens), (VMEM, up), (VMEM, up_t), (VMEM, live), (VMEM, da), (HBM, weight)],
        [
            ((features, 3 * features), BF), (flat, BF), (turned, BF), (half, BF), (half, BF),
            (flat, BF), (turned, BF), (flat, BF), (turned, BF), (flat, BF), (turned, BF), ((3 * features, length), BF), ((length, length), F32), (tokens.shape, F32),
        ],
        [3, 4], 1e10,
    )


def offset_backward(core, up, weight, q, kt, v, p):
    features, length = q.shape
    half = (2 * features, length)
    return call(
        "offset_backward", backward_kernel,
        [(VMEM, (3 * features, length)), (VMEM, (length, features)), (VMEM, half), (VMEM, half)],
        [("smem", core), (VMEM, up), (HBM, weight), (HBM, q), (HBM, kt), (HBM, v), (HBM, p)],
        [
            ((features, features), BF), (q.shape, BF), (kt.shape, BF), (v.shape, BF), (p.shape, BF),
            (q.shape, BF), (q.shape, BF), (up.shape, F32),
        ],
        [1, 4], 5e9, 48,
    )


def offset_finish(tokens, up, d, weight):
    features = tokens.shape[1]
    return call(
        "offset_finish", finish_kernel, [(VMEM, tokens.shape)],
        [(VMEM, tokens), (VMEM, up), (VMEM, d), (HBM, weight)],
        [((features, 3 * features), BF)], [3], 2e9, 48,
    )[0]


def weight_terms(y, *factors):
    features = factors[2].shape[1]
    return call(
        "weight_terms", weights_kernel, [(HBM, (features // 4, features))] * 8,
        [("smem", y), *[(VMEM, factor) for factor in factors]],
        [((features // 4, features), BF)] * 8 + [((8, features // 4, features), F32)], [8], 2.5e9,
    )


def add(*parts):
    total = parts[0].astype(jnp.float32)
    for part in parts[1:]:
        total = total + part.astype(jnp.float32)
    return total.astype(jnp.bfloat16)


def pick(array, index, axis):
    return lax.dynamic_index_in_dim(array, index, axis, keepdims=False)


SWAP = [(0, 1), (1, 0)]
ONWARD = [(i, (i + 1) % 4) for i in range(4)]
BACK = [(i, (i + 3) % 4) for i in range(4)]


def tie(*arrays):
    return lax.optimization_barrier(arrays)


def other_core(array):
    return lax.ppermute(array, "core", SWAP)


def ring_first(blocks):
    own0, own1, right0, right1, far0, far1, left0, left1 = blocks
    return (
        lax.ppermute(far0, "y", ONWARD),
        lax.ppermute(far1, "y", BACK),
        lax.ppermute(right1, "y", ONWARD),
        lax.ppermute(left0, "y", BACK),
    )


def ring_second(blocks, came):
    own0, own1, right0, right1, far0, far1, left0, left1 = blocks
    first = lax.ppermute(add(right0, came[0]), "y", ONWARD)
    second = lax.ppermute(add(left1, came[1]), "y", BACK)
    return add(own0, came[3], first), add(own1, came[2], second)


def last_sum(*pairs):
    rows, features = pairs[0][0].shape
    pieces = [jnp.concatenate(pair, axis=0).reshape(16, rows // 8, features) for pair in pairs]
    arrived = lax.all_to_all(
        jnp.concatenate(pieces, axis=1), ("xl", "z"), split_axis=0, concat_axis=0, tiled=True
    )
    total = jnp.sum(arrived.astype(jnp.float32), axis=0).reshape(len(pairs), 2, rows // 16, features)
    xh = lax.axis_index("xh")
    came = lax.ppermute(pick(total, 1 - xh, 1).astype(jnp.bfloat16), "xh", SWAP)
    total = pick(total, xh, 1) + came.astype(jnp.float32)
    return [part.T for part in total]


def to_rows(cotangent):
    y, xh = lax.axis_index("y"), lax.axis_index("xh")
    came = [(2 * y + xh, pick(cotangent, 2 * y + xh, 0))]
    for step in range(4):
        for turn in range(2):
            if step == turn == 0:
                continue
            perm = [
                (2 * i + j, 2 * ((i + step) % 4) + (j ^ turn)) for i in range(4) for j in range(2)
            ]
            target = 2 * ((y + step) % 4) + (xh + turn) % 2
            source = 2 * ((y + 4 - step) % 4) + (xh + turn) % 2
            came.append((source, lax.ppermute(pick(cotangent, target, 0), MID, perm)))
    return came


def local(tokens, cotangent, mask, w_offset, w_midpoint):
    off_place = lax.axis_index(OFF)
    mid_place = lax.axis_index(MID)
    core = lax.axis_index("core").reshape(1).astype(jnp.int32)
    y = lax.axis_index("y").reshape(1).astype(jnp.int32)
    rows_dev, cols_dev, features = tokens.shape
    length = mask.shape[0]
    column_live = pick(mask, mid_place * cols_dev + off_place, 1).reshape(length, 1)
    row_live = pick(mask, off_place * rows_dev + mid_place, 0).reshape(length, 1)

    def exchange(wide):
        rows = wide.reshape(length, -1, 2, 128)
        rows = lax.all_to_all(rows, OFF + MID, split_axis=0, concat_axis=0, tiled=True)
        return rows.reshape(wide.shape)

    column_tokens = lax.all_to_all(
        jnp.swapaxes(tokens, 0, 1), OFF, split_axis=0, concat_axis=0, tiled=True
    ).reshape(length, features)
    places, blocks = zip(*to_rows(cotangent))

    column_middle, q, a, p = offset_forward(column_tokens, column_live, w_offset)
    column_middle, *blocks = tie(column_middle, *blocks)
    middle = exchange(column_middle)
    row_up, row_up_t, da_mid = cotangent_heads(
        jnp.stack(places).astype(jnp.int32), blocks, w_midpoint
    )
    column_normed, kt, v = offset_residuals(column_tokens, w_offset)
    normed2, a2 = other_core(column_normed), other_core(a)
    middle, column_normed, kt, v = tie(middle, column_normed, kt, v)
    row_wide, row_normed, a_mid, keep, send = midpoint_both(
        core, middle, row_up, row_up_t, row_live, da_mid, w_midpoint
    )
    column_wide = exchange(row_wide)
    mid_blocks = weight_terms(
        y, keep, other_core(send), row_normed, other_core(row_normed), a_mid, other_core(a_mid)
    )
    mid_first = ring_first(mid_blocks)
    column_wide, normed2, a2, *mid_blocks = tie(column_wide, normed2, a2, *mid_blocks)
    d_off, column_up, keep, send = offset_backward(core, column_wide, w_offset, q, kt, v, p)
    send, *mid_first = tie(send, *mid_first)
    came = other_core(send)
    column_out = offset_finish(column_tokens, column_up, d_off, w_offset)
    came, column_out = tie(came, column_out)
    arrived = lax.all_to_all(
        column_out.reshape(cols_dev, rows_dev, features), OFF, split_axis=0, concat_axis=0, tiled=True
    )
    off_blocks = weight_terms(y, keep, came, column_normed, normed2, a, a2)
    off_first = ring_first(off_blocks)
    mid_pair = ring_second(mid_blocks, mid_first)
    arrived, *off_first = tie(arrived, *off_first)
    off_pair = ring_second(off_blocks, off_first)
    grad_off_weights, grad_mid_weights = last_sum(off_pair, mid_pair)
    return jnp.swapaxes(arrived, 0, 1), grad_off_weights, grad_mid_weights


def solution(mesh):
    fine = Mesh(mesh.devices.reshape(2, 8, 2, 4, 2), OFF + MID)
    placed = (P(OFF, MID, None), P(OFF, MID, None), P(), P(), P())
    return jax.shard_map(
        local,
        mesh=fine,
        in_specs=placed,
        out_specs=(P(OFF, MID, None), P(None, OFF + MID), P(None, OFF + MID)),
        check_vma=False,
    )
```

```python
import math

import jax
import jax.numpy as jnp
from jax import lax
from jax.experimental import pallas as pl
from jax.experimental.pallas import tpu as pltpu
from jax.sharding import Mesh
from jax.sharding import PartitionSpec as P

HEADS = 12
WIDTH = 64
SCALE = 0.125
EPSILON = 1e-05
NEGATIVE = -1e30
OFF = ("xl", "z", "core")
MID = ("y", "xh")


NT = (((1,), (1,)), ((), ()))
MIB = 1024 * 1024


def dot(left, right):
    return jnp.dot(left, right, preferred_element_type=jnp.float32)


def dot_nt(left, right):
    return lax.dot_general(left, right, NT, preferred_element_type=jnp.float32)


def low(value):
    return value.astype(jnp.bfloat16)


def statistics(values):
    widened = values.astype(jnp.float32)
    center = jnp.mean(widened, axis=-1, keepdims=True)
    shifted = widened - center
    inverse = lax.rsqrt(jnp.mean(shifted * shifted, axis=-1, keepdims=True) + EPSILON)
    return shifted * inverse, inverse


def layer_grad(values, incoming):
    scaled, inverse = statistics(values)
    incoming = incoming.astype(jnp.float32)
    return inverse * (
        incoming
        - jnp.mean(incoming, axis=-1, keepdims=True)
        - scaled * jnp.mean(incoming * scaled, axis=-1, keepdims=True)
    )


def key_bias(live):
    length = live.shape[0]
    keys = lax.broadcasted_iota(jnp.int32, (length, length), 0)
    queries = lax.broadcasted_iota(jnp.int32, (length, length), 1)
    allowed = jnp.logical_or(live == 1, keys == queries)
    return jnp.where(allowed, 0.0, NEGATIVE)


def padded(array, head):
    rows = array[head * WIDTH : (head + 1) * WIDTH]
    blank = jnp.zeros_like(rows)
    return jnp.concatenate([rows, blank] if head % 2 == 0 else [blank, rows], axis=0)


def pair(head):
    start = (head // 2) * 2 * WIDTH
    return slice(start, start + 2 * WIDTH)


def own(head):
    return slice(head * WIDTH, (head + 1) * WIDTH)


def softmax_keys(scores):
    expanded = jnp.exp(scores - jnp.max(scores, axis=0, keepdims=True))
    return expanded * (1.0 / jnp.sum(expanded, axis=0, keepdims=True))


def fetch(weight_hbm, weight_ref, sems, *parts):
    features = weight_hbm.shape[0]
    copies = {}
    for place, part in enumerate(parts):
        columns = slice(part * features, (part + 1) * features)
        copies[part] = pltpu.make_async_copy(
            weight_hbm.at[:, columns],
            weight_ref.at[:, place * features : (place + 1) * features],
            sems.at[place],
        )
        copies[part].start()
    return copies


def columns(weight_ref, place):
    features = weight_ref.shape[0]
    return weight_ref[:, place * features : (place + 1) * features]


def encode(rows, wide_ref, out_ref):
    chunks = rows.shape[1] // 128
    for c in range(chunks):
        wide_ref[pl.ds(c, rows.shape[0], stride=chunks), :] = rows[:, c * 128 : (c + 1) * 128]
    out_ref[...] = low(wide_ref[...])


def decode(in_ref, wide_ref, rows_ref):
    length, features = rows_ref.shape
    chunks = features // 128
    wide_ref[...] = in_ref[...].astype(jnp.float32)
    for c in range(chunks):
        rows_ref[:, c * 128 : (c + 1) * 128] = low(wide_ref[pl.ds(c, length, stride=chunks), :])


def encode_midpoints(rows, wide_ref, out_ref):
    chunks = rows.shape[1] // 128
    for m in range(8):
        for c in range(chunks):
            wide_ref[pl.ds(m * chunks + c, 32, stride=8 * chunks), :] = rows[
                m * 32 : (m + 1) * 32, c * 128 : (c + 1) * 128
            ]
    out_ref[...] = low(wide_ref[...])


def decode_midpoints(in_ref, wide_ref, rows_ref):
    chunks = rows_ref.shape[1] // 128
    wide_ref[...] = in_ref[...].astype(jnp.float32)
    for m in range(8):
        for c in range(chunks):
            rows_ref[m * 32 : (m + 1) * 32, c * 128 : (c + 1) * 128] = low(
                wide_ref[pl.ds(m * chunks + c, 32, stride=8 * chunks), :]
            )


def forward_kernel(
    tokens_ref, live_ref, weight_hbm, out_ref, q_hbm, a_hbm, p_hbm,
    weight_ref, q_ref, k_ref, v_ref, a_ref, p_ref, bias_ref, wide_ref, sems, out_sems,
):
    copies = fetch(weight_hbm, weight_ref, sems, 1, 0, 2, 3)
    bias_ref[...] = key_bias(live_ref[...])
    normed = low(statistics(tokens_ref[...])[0])
    copies[1].wait()
    k_ref[...] = low(dot(normed, columns(weight_ref, 0)))
    copies[0].wait()
    q_ref[...] = (low(dot(normed, columns(weight_ref, 1))) * SCALE).T
    copies[2].wait()
    v_ref[...] = low(dot(normed, columns(weight_ref, 2))).T
    sent = [pltpu.make_async_copy(q_ref, q_hbm, out_sems.at[HEADS])]
    sent[0].start()
    for head in range(HEADS):
        scores = dot(k_ref[:, pair(head)], padded(q_ref, head)) + bias_ref[...]
        p = low(softmax_keys(scores))
        p_ref[head] = p
        sent.append(pltpu.make_async_copy(p_ref.at[head], p_hbm.at[head], out_sems.at[head]))
        sent[-1].start()
        a_ref[own(head)] = low(dot(v_ref[own(head)], p))
    sent.append(pltpu.make_async_copy(a_ref, a_hbm, out_sems.at[HEADS + 1]))
    sent[-1].start()
    copies[3].wait()
    out = low(dot(a_ref[...].T, columns(weight_ref, 3)))
    encode(tokens_ref[...].astype(jnp.float32) + out.astype(jnp.float32), wide_ref, out_ref)
    for copy in sent:
        copy.wait()


def residual_kernel(tokens_ref, weight_hbm, normed_ref, kt_ref, v_ref, weight_ref, sems):
    copies = fetch(weight_hbm, weight_ref, sems, 1, 2)
    normed = low(statistics(tokens_ref[...])[0])
    normed_ref[...] = normed
    copies[1].wait()
    kt_ref[...] = low(dot(normed, columns(weight_ref, 0))).T
    copies[2].wait()
    v_ref[...] = low(dot(normed, columns(weight_ref, 1)))


def cotangent_kernel(place_ref, *refs):
    *blocks, weight_hbm, up_ref, upt_ref, da_ref, weight_ref, sems = refs
    copies = fetch(weight_hbm, weight_ref, sems, 3)
    for i, block in enumerate(blocks):
        size = block.shape[0]
        up_ref[pl.ds(pl.multiple_of(place_ref[i] * size, size), size), :] = block[...]
    upt_ref[...] = up_ref[...].T
    copies[3].wait()
    da_ref[...] = low(dot_nt(weight_ref[...], up_ref[...]))


def divide(core, d_ref, upt_ref, keep_ref, send_ref):
    group = 96
    first = d_ref.shape[0] // (2 * group)
    for out_ref, which in ((send_ref, 1 - core), (keep_ref, core)):
        for step in range(out_ref.shape[0] // group):
            source, at = (d_ref, step) if step < first else (upt_ref, step - first)
            start = pl.multiple_of((2 * at + which) * group, group)
            out_ref[step * group : (step + 1) * group] = source[pl.ds(start, group), :]


def head_grad(head, p, p_low, q_ref, kt_ref, v_ref, da_ref, d_ref):
    features = da_ref.shape[0]
    dp = dot(v_ref[:, pair(head)], padded(da_ref, head))
    ds = low(p * (dp - jnp.sum(p * dp, axis=0, keepdims=True)))
    d_ref[own(head)] = low(dot(kt_ref[own(head)], ds) * SCALE)
    d_ref[features + head * WIDTH : features + (head + 1) * WIDTH] = low(dot_nt(q_ref[own(head)], ds))
    d_ref[2 * features + head * WIDTH : 2 * features + (head + 1) * WIDTH] = low(
        dot_nt(da_ref[own(head)], p_low)
    )


def middle_kernel(
    core_ref, tokens_ref, up_ref, upt_ref, live_ref, da_ref, weight_hbm,
    out_ref, normed_hbm, a_hbm, keep_hbm, send_hbm,
    weight_ref, normed_ref, a_ref, keep_ref, send_ref, rows_ref, q_ref, k_ref, kt_ref, v_ref, vt_ref, d_ref, bias_ref, wide_ref, sems, out_sems,
):
    copies = fetch(weight_hbm, weight_ref, sems, 0, 1, 2)
    bias_ref[...] = key_bias(live_ref[...])
    decode_midpoints(tokens_ref, wide_ref, rows_ref)
    normed = low(statistics(rows_ref[...])[0])
    normed_ref[...] = normed
    sent = [
        pltpu.make_async_copy(source, target, out_sems.at[i])
        for i, (source, target) in enumerate(
            ((normed_ref, normed_hbm), (a_ref, a_hbm), (keep_ref, keep_hbm), (send_ref, send_hbm))
        )
    ]
    sent[0].start()
    copies[0].wait()
    q_ref[...] = (low(dot(normed, columns(weight_ref, 0))) * SCALE).T
    copies[1].wait()
    k_ref[...] = low(dot(normed, columns(weight_ref, 1)))
    kt_ref[...] = k_ref[...].T
    copies[2].wait()
    v_ref[...] = low(dot(normed, columns(weight_ref, 2)))
    vt_ref[...] = v_ref[...].T
    for head in range(HEADS):
        scores = dot(k_ref[:, pair(head)], padded(q_ref, head)) + bias_ref[...]
        p = softmax_keys(scores)
        p_low = low(p)
        a_ref[own(head)] = low(dot(vt_ref[own(head)], p_low))
        head_grad(head, p, p_low, q_ref, kt_ref, v_ref, da_ref, d_ref)
    sent[1].start()
    divide(core_ref[0], d_ref, upt_ref, keep_ref, send_ref)
    sent[2].start()
    sent[3].start()
    dh = low(dot(weight_ref[...], d_ref[...])).T
    encode_midpoints(
        up_ref[...].astype(jnp.float32) + layer_grad(rows_ref[...], dh), wide_ref, out_ref
    )
    for copy in sent:
        copy.wait()


def backward_kernel(
    core_ref, up_ref, weight_hbm, q_hbm, kt_hbm, v_hbm, p_hbm,
    d_ref, rows_ref, keep_ref, send_ref,
    weight_ref, q_ref, kt_ref, v_ref, p_ref, da_ref, upt_ref, wide_ref, sems, in_sems,
):
    copies = fetch(weight_hbm, weight_ref, sems, 3)
    moved = [
        pltpu.make_async_copy(source, target, in_sems.at[i])
        for i, (source, target) in enumerate(
            ((v_hbm, v_ref), (p_hbm, p_ref), (kt_hbm, kt_ref), (q_hbm, q_ref))
        )
    ]
    for copy in moved:
        copy.start()
    decode(up_ref, wide_ref, rows_ref)
    copies[3].wait()
    da_ref[...] = low(dot_nt(weight_ref[...], rows_ref[...]))
    upt_ref[...] = rows_ref[...].T
    for copy in moved:
        copy.wait()
    for head in range(HEADS):
        p_low = p_ref[head]
        head_grad(head, p_low.astype(jnp.float32), p_low, q_ref, kt_ref, v_ref, da_ref, d_ref)
    divide(core_ref[0], d_ref, upt_ref, keep_ref, send_ref)


def finish_kernel(tokens_ref, up_ref, d_ref, weight_hbm, out_ref, weight_ref, sems):
    features = tokens_ref.shape[1]
    copies = fetch(weight_hbm, weight_ref, sems, 0, 1, 2)
    total = None
    for part in range(3):
        copies[part].wait()
        term = dot(columns(weight_ref, part), d_ref[part * features : (part + 1) * features])
        total = term if total is None else total + term
    out_ref[...] = low(up_ref[...].astype(jnp.float32) + layer_grad(tokens_ref[...], low(total).T))


def weights_kernel(y_ref, d_ref, d2_ref, normed_ref, normed2_ref, a_ref, a2_ref, *refs):
    outs_hbm, outs, (sums_ref, sems) = refs[:8], refs[8:16], refs[16:]
    sent = [pltpu.make_async_copy(outs[i], outs_hbm[i], sems.at[i]) for i in range(8)]
    y, group, share = y_ref[0], 96, 24
    first = 3 * normed_ref.shape[1] // (2 * group)
    for step in range(8):
        rows = slice(step * 2 * group, (step + 1) * 2 * group)
        if 2 * step < first:
            sums = dot(d_ref[rows], normed_ref[...]) + dot(d2_ref[rows], normed2_ref[...])
        else:
            sums = dot_nt(d_ref[rows], a_ref[...]) + dot_nt(d2_ref[rows], a2_ref[...])
        sums_ref[step] = sums
        place = step % 4
        for away in range(4):
            start = pl.multiple_of(lax.rem(y + away, 4) * share, 8)
            pieces = [sums_ref[step, pl.ds(start + i * group, share), :] for i in range(2)]
            outs[2 * away + step // 4][place * 2 * share : (place + 1) * 2 * share] = low(
                jnp.concatenate(pieces, axis=0)
            )
            if place == 3:
                sent[2 * away + step // 4].start()
    for copy in sent:
        copy.wait()


BF = jnp.bfloat16
F32 = jnp.float32
HBM, VMEM = "hbm", "vmem"
PLACES = {
    HBM: pl.BlockSpec(memory_space=pltpu.HBM),
    VMEM: pl.BlockSpec(memory_space=pltpu.VMEM),
    "smem": pl.BlockSpec(memory_space=pltpu.SMEM),
}


def call(name, kernel, outs, args, scratch, sems, flops, limit=60):
    moved = sum(math.prod(a.shape) * 2 for _, a in args) + sum(math.prod(s) * 2 for _, s in outs)
    return pl.pallas_call(
        kernel,
        out_shape=[jax.ShapeDtypeStruct(s, BF) for _, s in outs],
        in_specs=[PLACES[place] for place, _ in args],
        out_specs=[PLACES[place] for place, _ in outs],
        scratch_shapes=[pltpu.VMEM(s, t) for s, t in scratch]
        + [pltpu.SemaphoreType.DMA((n,)) for n in sems],
        compiler_params=pltpu.CompilerParams(vmem_limit_bytes=limit * MIB),
        cost_estimate=pl.CostEstimate(flops=int(flops), bytes_accessed=moved, transcendentals=0),
        name=name,
    )(*[a for _, a in args])


def offset_forward(tokens, live, weight):
    length, features = tokens.shape
    flat, turned, wide = (length, features), (features, length), (length * features // 128, 128)
    return call(
        "offset_forward",
        forward_kernel,
        [(VMEM, wide), (HBM, turned), (HBM, turned), (HBM, (HEADS, length, length))],
        [(VMEM, tokens), (VMEM, live), (HBM, weight)],
        [
            (weight.shape, BF), (turned, BF), (flat, BF), (turned, BF), (turned, BF),
            ((HEADS, length, length), BF), ((length, length), F32), (wide, F32),
        ],
        [4, HEADS + 2],
        4e9,
    )


def offset_residuals(tokens, weight):
    length, features = tokens.shape
    flat, turned = (length, features), (features, length)
    return call(
        "offset_residuals", residual_kernel, [(VMEM, flat), (VMEM, turned), (VMEM, flat)],
        [(VMEM, tokens), (HBM, weight)], [((features, 2 * features), BF)], [2], 1e9,
    )


def cotangent_heads(places, blocks, weight):
    features = blocks[0].shape[1]
    length = sum(block.shape[0] for block in blocks)
    flat, turned = (length, features), (features, length)
    return call(
        "cotangent_heads", cotangent_kernel, [(VMEM, flat), (VMEM, turned), (VMEM, turned)],
        [("smem", places), *[(VMEM, block) for block in blocks], (HBM, weight)],
        [((features, features), BF)], [1], 5e8,
    )


def midpoint_both(core, tokens, up, up_t, live, da, weight):
    length, features = up.shape
    flat, turned, half = (length, features), (features, length), (2 * features, length)
    return call(
        "midpoint_both", middle_kernel,
        [(VMEM, tokens.shape), (HBM, flat), (HBM, turned), (HBM, half), (HBM, half)],
        [("smem", core), (VMEM, tokens), (VMEM, up), (VMEM, up_t), (VMEM, live), (VMEM, da), (HBM, weight)],
        [
            ((features, 3 * features), BF), (flat, BF), (turned, BF), (half, BF), (half, BF),
            (flat, BF), (turned, BF), (flat, BF), (turned, BF), (flat, BF), (turned, BF), ((3 * features, length), BF), ((length, length), F32), (tokens.shape, F32),
        ],
        [3, 4], 1e10,
    )


def offset_backward(core, up, weight, q, kt, v, p):
    features, length = q.shape
    half = (2 * features, length)
    return call(
        "offset_backward", backward_kernel,
        [(VMEM, (3 * features, length)), (VMEM, (length, features)), (VMEM, half), (VMEM, half)],
        [("smem", core), (VMEM, up), (HBM, weight), (HBM, q), (HBM, kt), (HBM, v), (HBM, p)],
        [
            ((features, features), BF), (q.shape, BF), (kt.shape, BF), (v.shape, BF), (p.shape, BF),
            (q.shape, BF), (q.shape, BF), (up.shape, F32),
        ],
        [1, 4], 5e9, 48,
    )


def offset_finish(tokens, up, d, weight):
    features = tokens.shape[1]
    return call(
        "offset_finish", finish_kernel, [(VMEM, tokens.shape)],
        [(VMEM, tokens), (VMEM, up), (VMEM, d), (HBM, weight)],
        [((features, 3 * features), BF)], [3], 2e9, 48,
    )[0]


def weight_terms(y, *factors):
    features = factors[2].shape[1]
    return call(
        "weight_terms", weights_kernel, [(HBM, (features // 4, features))] * 8,
        [("smem", y), *[(VMEM, factor) for factor in factors]],
        [((features // 4, features), BF)] * 8 + [((8, features // 4, features), F32)], [8], 2.5e9, 60,
    )


def add(*parts):
    total = parts[0].astype(jnp.float32)
    for part in parts[1:]:
        total = total + part.astype(jnp.float32)
    return total.astype(jnp.bfloat16)


def pick(array, index, axis):
    return lax.dynamic_index_in_dim(array, index, axis, keepdims=False)


SWAP = [(0, 1), (1, 0)]
ONWARD = [(i, (i + 1) % 4) for i in range(4)]
BACK = [(i, (i + 3) % 4) for i in range(4)]


def tie(*arrays):
    return lax.optimization_barrier(arrays)


def other_core(array):
    return lax.ppermute(array, "core", SWAP)


def ring_first(blocks):
    own0, own1, right0, right1, far0, far1, left0, left1 = blocks
    return (
        lax.ppermute(far0, "y", ONWARD),
        lax.ppermute(far1, "y", BACK),
        lax.ppermute(right1, "y", ONWARD),
        lax.ppermute(left0, "y", BACK),
    )


def ring_second(blocks, came):
    own0, own1, right0, right1, far0, far1, left0, left1 = blocks
    first = lax.ppermute(add(right0, came[0]), "y", ONWARD)
    second = lax.ppermute(add(left1, came[1]), "y", BACK)
    return add(own0, came[3], first), add(own1, came[2], second)


def last_exchange(first, second):
    rows, features = first.shape
    pieces = jnp.concatenate([first, second], axis=0).reshape(16, rows // 8, features)
    return lax.all_to_all(pieces, ("xl", "z"), split_axis=0, concat_axis=0, tiled=True)


def last_sum(*arrived):
    total = jnp.stack([jnp.sum(part.astype(jnp.float32), axis=0) for part in arrived])
    total = total.reshape(len(arrived), 2, total.shape[1] // 2, total.shape[2])
    xh = lax.axis_index("xh")
    came = lax.ppermute(pick(total, 1 - xh, 1).astype(jnp.bfloat16), "xh", SWAP)
    total = pick(total, xh, 1) + came.astype(jnp.float32)
    return [part.T for part in total]


def to_rows(cotangent):
    y, xh = lax.axis_index("y"), lax.axis_index("xh")
    came = [(2 * y + xh, pick(cotangent, 2 * y + xh, 0))]
    for step in range(4):
        for turn in range(2):
            if step == turn == 0:
                continue
            perm = [
                (2 * i + j, 2 * ((i + step) % 4) + (j ^ turn)) for i in range(4) for j in range(2)
            ]
            target = 2 * ((y + step) % 4) + (xh + turn) % 2
            source = 2 * ((y + 4 - step) % 4) + (xh + turn) % 2
            came.append((source, lax.ppermute(pick(cotangent, target, 0), MID, perm)))
    return came


def local(tokens, cotangent, mask, w_offset, w_midpoint):
    off_place = lax.axis_index(OFF)
    mid_place = lax.axis_index(MID)
    core = lax.axis_index("core").reshape(1).astype(jnp.int32)
    y = lax.axis_index("y").reshape(1).astype(jnp.int32)
    rows_dev, cols_dev, features = tokens.shape
    length = mask.shape[0]
    column_live = pick(mask, mid_place * cols_dev + off_place, 1).reshape(length, 1)
    row_live = pick(mask, off_place * rows_dev + mid_place, 0).reshape(length, 1)

    def exchange(wide):
        rows = wide.reshape(length, -1, 2, 128)
        rows = lax.all_to_all(rows, OFF + MID, split_axis=0, concat_axis=0, tiled=True)
        return rows.reshape(wide.shape)

    column_tokens = lax.all_to_all(
        jnp.swapaxes(tokens, 0, 1), OFF, split_axis=0, concat_axis=0, tiled=True
    ).reshape(length, features)
    places, blocks = zip(*to_rows(cotangent))

    column_middle, q, a, p = offset_forward(column_tokens, column_live, w_offset)
    column_middle, *blocks = tie(column_middle, *blocks)
    middle = exchange(column_middle)
    row_up, row_up_t, da_mid = cotangent_heads(
        jnp.stack(places).astype(jnp.int32), blocks, w_midpoint
    )
    column_normed, kt, v = offset_residuals(column_tokens, w_offset)
    normed2, a2 = other_core(column_normed), other_core(a)
    middle, column_normed, kt, v = tie(middle, column_normed, kt, v)
    row_wide, row_normed, a_mid, keep, send = midpoint_both(
        core, middle, row_up, row_up_t, row_live, da_mid, w_midpoint
    )
    column_wide = exchange(row_wide)
    mid_blocks = weight_terms(
        y, keep, other_core(send), row_normed, other_core(row_normed), a_mid, other_core(a_mid)
    )
    mid_first = ring_first(mid_blocks)
    column_wide, normed2, a2, *mid_blocks = tie(column_wide, normed2, a2, *mid_blocks)
    d_off, column_up, keep, send = offset_backward(core, column_wide, w_offset, q, kt, v, p)
    send, *mid_first = tie(send, *mid_first)
    came = other_core(send)
    column_out = offset_finish(column_tokens, column_up, d_off, w_offset)
    came, column_out = tie(came, column_out)
    arrived = lax.all_to_all(
        column_out.reshape(cols_dev, rows_dev, features), OFF, split_axis=0, concat_axis=0, tiled=True
    )
    off_blocks = weight_terms(y, keep, came, column_normed, normed2, a, a2)
    off_first = ring_first(off_blocks)
    mid_pair = ring_second(mid_blocks, mid_first)
    arrived, mid_low, mid_high, *off_far = tie(arrived, *mid_pair, *off_first[:2])
    off_first = (*off_far, *off_first[2:])
    mid_arrived = last_exchange(mid_low, mid_high)
    off_pair = ring_second(off_blocks, off_first)
    mid_arrived, *off_pair = tie(mid_arrived, *off_pair)
    grad_off_weights, grad_mid_weights = last_sum(last_exchange(*off_pair), mid_arrived)
    return jnp.swapaxes(arrived, 0, 1), grad_off_weights, grad_mid_weights


def solution(mesh):
    fine = Mesh(mesh.devices.reshape(2, 8, 2, 4, 2), OFF + MID)
    placed = (P(OFF, MID, None), P(OFF, MID, None), P(), P(), P())
    return jax.shard_map(
        local,
        mesh=fine,
        in_specs=placed,
        out_specs=(P(OFF, MID, None), P(None, OFF + MID), P(None, OFF + MID)),
        check_vma=False,
    )
```

```python
import math

import jax
import jax.numpy as jnp
from jax import lax
from jax.experimental import pallas as pl
from jax.experimental.pallas import tpu as pltpu
from jax.sharding import Mesh
from jax.sharding import PartitionSpec as P

HEADS = 12
WIDTH = 64
SCALE = 0.125
EPSILON = 1e-05
NEGATIVE = -1e30
OFF = ("xl", "z", "core")
MID = ("y", "xh")


NT = (((1,), (1,)), ((), ()))
MIB = 1024 * 1024


def dot(left, right):
    return jnp.dot(left, right, preferred_element_type=jnp.float32)


def dot_nt(left, right):
    return lax.dot_general(left, right, NT, preferred_element_type=jnp.float32)


def low(value):
    return value.astype(jnp.bfloat16)


def statistics(values):
    widened = values.astype(jnp.float32)
    center = jnp.mean(widened, axis=-1, keepdims=True)
    shifted = widened - center
    inverse = lax.rsqrt(jnp.mean(shifted * shifted, axis=-1, keepdims=True) + EPSILON)
    return shifted * inverse, inverse


def layer_grad(values, incoming):
    scaled, inverse = statistics(values)
    incoming = incoming.astype(jnp.float32)
    return inverse * (
        incoming
        - jnp.mean(incoming, axis=-1, keepdims=True)
        - scaled * jnp.mean(incoming * scaled, axis=-1, keepdims=True)
    )


def key_bias(live):
    length = live.shape[0]
    keys = lax.broadcasted_iota(jnp.int32, (length, length), 0)
    queries = lax.broadcasted_iota(jnp.int32, (length, length), 1)
    allowed = jnp.logical_or(live == 1, keys == queries)
    return jnp.where(allowed, 0.0, NEGATIVE)


def padded(array, head):
    rows = array[head * WIDTH : (head + 1) * WIDTH]
    blank = jnp.zeros_like(rows)
    return jnp.concatenate([rows, blank] if head % 2 == 0 else [blank, rows], axis=0)


def pair(head):
    start = (head // 2) * 2 * WIDTH
    return slice(start, start + 2 * WIDTH)


def own(head):
    return slice(head * WIDTH, (head + 1) * WIDTH)


def softmax_keys(scores):
    expanded = jnp.exp(scores - jnp.max(scores, axis=0, keepdims=True))
    return expanded * (1.0 / jnp.sum(expanded, axis=0, keepdims=True))


def fetch(weight_hbm, weight_ref, sems, *parts):
    features = weight_hbm.shape[0]
    copies = {}
    for place, part in enumerate(parts):
        columns = slice(part * features, (part + 1) * features)
        copies[part] = pltpu.make_async_copy(
            weight_hbm.at[:, columns],
            weight_ref.at[:, place * features : (place + 1) * features],
            sems.at[place],
        )
        copies[part].start()
    return copies


def columns(weight_ref, place):
    features = weight_ref.shape[0]
    return weight_ref[:, place * features : (place + 1) * features]


def encode(rows, wide_ref, out_ref):
    chunks = rows.shape[1] // 128
    for c in range(chunks):
        wide_ref[pl.ds(c, rows.shape[0], stride=chunks), :] = rows[:, c * 128 : (c + 1) * 128]
    out_ref[...] = low(wide_ref[...])


def decode(in_ref, wide_ref, rows_ref):
    length, features = rows_ref.shape
    chunks = features // 128
    wide_ref[...] = in_ref[...].astype(jnp.float32)
    for c in range(chunks):
        rows_ref[:, c * 128 : (c + 1) * 128] = low(wide_ref[pl.ds(c, length, stride=chunks), :])


def encode_midpoints(rows, wide_ref, out_ref):
    chunks = rows.shape[1] // 128
    for m in range(8):
        for c in range(chunks):
            wide_ref[pl.ds(m * chunks + c, 32, stride=8 * chunks), :] = rows[
                m * 32 : (m + 1) * 32, c * 128 : (c + 1) * 128
            ]
    out_ref[...] = low(wide_ref[...])


def decode_midpoints(in_ref, wide_ref, rows_ref):
    chunks = rows_ref.shape[1] // 128
    wide_ref[...] = in_ref[...].astype(jnp.float32)
    for m in range(8):
        for c in range(chunks):
            rows_ref[m * 32 : (m + 1) * 32, c * 128 : (c + 1) * 128] = low(
                wide_ref[pl.ds(m * chunks + c, 32, stride=8 * chunks), :]
            )


def forward_kernel(
    tokens_ref, live_ref, weight_hbm, out_ref, q_hbm, a_hbm, p_hbm,
    weight_ref, q_ref, k_ref, v_ref, a_ref, p_ref, bias_ref, wide_ref, sems, out_sems,
):
    copies = fetch(weight_hbm, weight_ref, sems, 1, 0, 2, 3)
    bias_ref[...] = key_bias(live_ref[...])
    normed = low(statistics(tokens_ref[...])[0])
    copies[1].wait()
    k_ref[...] = low(dot(normed, columns(weight_ref, 0)))
    copies[0].wait()
    q_ref[...] = (low(dot(normed, columns(weight_ref, 1))) * SCALE).T
    copies[2].wait()
    v_ref[...] = low(dot(normed, columns(weight_ref, 2))).T
    sent = [pltpu.make_async_copy(q_ref, q_hbm, out_sems.at[HEADS])]
    sent[0].start()
    for head in range(HEADS):
        scores = dot(k_ref[:, pair(head)], padded(q_ref, head)) + bias_ref[...]
        p = low(softmax_keys(scores))
        p_ref[head] = p
        sent.append(pltpu.make_async_copy(p_ref.at[head], p_hbm.at[head], out_sems.at[head]))
        sent[-1].start()
        a_ref[own(head)] = low(dot(v_ref[own(head)], p))
    sent.append(pltpu.make_async_copy(a_ref, a_hbm, out_sems.at[HEADS + 1]))
    sent[-1].start()
    copies[3].wait()
    out = low(dot(a_ref[...].T, columns(weight_ref, 3)))
    encode(tokens_ref[...].astype(jnp.float32) + out.astype(jnp.float32), wide_ref, out_ref)
    for copy in sent:
        copy.wait()


def residual_kernel(tokens_ref, weight_hbm, normed_ref, kt_ref, v_ref, weight_ref, sems):
    copies = fetch(weight_hbm, weight_ref, sems, 1, 2)
    normed = low(statistics(tokens_ref[...])[0])
    normed_ref[...] = normed
    copies[1].wait()
    kt_ref[...] = low(dot(normed, columns(weight_ref, 0))).T
    copies[2].wait()
    v_ref[...] = low(dot(normed, columns(weight_ref, 1)))


def cotangent_kernel(place_ref, *refs):
    *blocks, weight_hbm, up_ref, upt_ref, da_ref, weight_ref, sems = refs
    copies = fetch(weight_hbm, weight_ref, sems, 3)
    for i, block in enumerate(blocks):
        size = block.shape[0]
        up_ref[pl.ds(pl.multiple_of(place_ref[i] * size, size), size), :] = block[...]
    upt_ref[...] = up_ref[...].T
    copies[3].wait()
    da_ref[...] = low(dot_nt(weight_ref[...], up_ref[...]))


def divide(core, d_ref, upt_ref, keep_ref, send_ref):
    group = 96
    first = d_ref.shape[0] // (2 * group)
    for out_ref, which in ((send_ref, 1 - core), (keep_ref, core)):
        for step in range(out_ref.shape[0] // group):
            source, at = (d_ref, step) if step < first else (upt_ref, step - first)
            start = pl.multiple_of((2 * at + which) * group, group)
            out_ref[step * group : (step + 1) * group] = source[pl.ds(start, group), :]


def head_grad(head, p, p_low, q_ref, kt_ref, v_ref, da_ref, d_ref):
    features = da_ref.shape[0]
    dp = dot(v_ref[:, pair(head)], padded(da_ref, head))
    ds = low(p * (dp - jnp.sum(p * dp, axis=0, keepdims=True)))
    d_ref[own(head)] = low(dot(kt_ref[own(head)], ds) * SCALE)
    d_ref[features + head * WIDTH : features + (head + 1) * WIDTH] = low(dot_nt(q_ref[own(head)], ds))
    d_ref[2 * features + head * WIDTH : 2 * features + (head + 1) * WIDTH] = low(
        dot_nt(da_ref[own(head)], p_low)
    )


def middle_kernel(
    core_ref, tokens_ref, up_ref, upt_ref, live_ref, da_ref, weight_hbm,
    out_ref, normed_hbm, a_hbm, keep_hbm, send_hbm,
    weight_ref, normed_ref, a_ref, keep_ref, send_ref, rows_ref, q_ref, k_ref, kt_ref, v_ref, vt_ref, d_ref, bias_ref, wide_ref, sems, out_sems,
):
    copies = fetch(weight_hbm, weight_ref, sems, 0, 1, 2)
    bias_ref[...] = key_bias(live_ref[...])
    decode_midpoints(tokens_ref, wide_ref, rows_ref)
    normed = low(statistics(rows_ref[...])[0])
    normed_ref[...] = normed
    sent = [
        pltpu.make_async_copy(source, target, out_sems.at[i])
        for i, (source, target) in enumerate(
            ((normed_ref, normed_hbm), (a_ref, a_hbm), (keep_ref, keep_hbm), (send_ref, send_hbm))
        )
    ]
    sent[0].start()
    copies[0].wait()
    q_ref[...] = (low(dot(normed, columns(weight_ref, 0))) * SCALE).T
    copies[1].wait()
    k_ref[...] = low(dot(normed, columns(weight_ref, 1)))
    kt_ref[...] = k_ref[...].T
    copies[2].wait()
    v_ref[...] = low(dot(normed, columns(weight_ref, 2)))
    vt_ref[...] = v_ref[...].T
    for head in range(HEADS):
        scores = dot(k_ref[:, pair(head)], padded(q_ref, head)) + bias_ref[...]
        p = softmax_keys(scores)
        p_low = low(p)
        a_ref[own(head)] = low(dot(vt_ref[own(head)], p_low))
        head_grad(head, p, p_low, q_ref, kt_ref, v_ref, da_ref, d_ref)
    sent[1].start()
    divide(core_ref[0], d_ref, upt_ref, keep_ref, send_ref)
    sent[2].start()
    sent[3].start()
    dh = low(dot(weight_ref[...], d_ref[...])).T
    encode_midpoints(
        up_ref[...].astype(jnp.float32) + layer_grad(rows_ref[...], dh), wide_ref, out_ref
    )
    for copy in sent:
        copy.wait()


def backward_kernel(
    core_ref, up_ref, weight_hbm, q_hbm, kt_hbm, v_hbm, p_hbm,
    d_ref, rows_ref, keep_ref, send_ref,
    weight_ref, q_ref, kt_ref, v_ref, p_ref, da_ref, upt_ref, wide_ref, sems, in_sems,
):
    copies = fetch(weight_hbm, weight_ref, sems, 3)
    moved = [
        pltpu.make_async_copy(source, target, in_sems.at[i])
        for i, (source, target) in enumerate(
            ((v_hbm, v_ref), (p_hbm, p_ref), (kt_hbm, kt_ref), (q_hbm, q_ref))
        )
    ]
    for copy in moved:
        copy.start()
    decode(up_ref, wide_ref, rows_ref)
    copies[3].wait()
    da_ref[...] = low(dot_nt(weight_ref[...], rows_ref[...]))
    upt_ref[...] = rows_ref[...].T
    for copy in moved:
        copy.wait()
    for head in range(HEADS):
        p_low = p_ref[head]
        head_grad(head, p_low.astype(jnp.float32), p_low, q_ref, kt_ref, v_ref, da_ref, d_ref)
    divide(core_ref[0], d_ref, upt_ref, keep_ref, send_ref)


def finish_kernel(tokens_ref, up_ref, d_ref, weight_hbm, out_ref, weight_ref, sems):
    features = tokens_ref.shape[1]
    copies = fetch(weight_hbm, weight_ref, sems, 0, 1, 2)
    total = None
    for part in range(3):
        copies[part].wait()
        term = dot(columns(weight_ref, part), d_ref[part * features : (part + 1) * features])
        total = term if total is None else total + term
    out_ref[...] = low(up_ref[...].astype(jnp.float32) + layer_grad(tokens_ref[...], low(total).T))


def weights_kernel(y_ref, d_ref, d2_ref, normed_ref, normed2_ref, a_ref, a2_ref, *refs):
    outs_hbm, outs, (sums_ref, sems) = refs[:8], refs[8:16], refs[16:]
    sent = [pltpu.make_async_copy(outs[i], outs_hbm[i], sems.at[i]) for i in range(8)]
    y, group, share = y_ref[0], 96, 24
    first = 3 * normed_ref.shape[1] // (2 * group)
    for step in range(8):
        rows = slice(step * 2 * group, (step + 1) * 2 * group)
        if 2 * step < first:
            sums = dot(d_ref[rows], normed_ref[...]) + dot(d2_ref[rows], normed2_ref[...])
        else:
            sums = dot_nt(d_ref[rows], a_ref[...]) + dot_nt(d2_ref[rows], a2_ref[...])
        sums_ref[step] = sums
        place = step % 4
        for away in range(4):
            start = pl.multiple_of(lax.rem(y + away, 4) * share, 8)
            pieces = [sums_ref[step, pl.ds(start + i * group, share), :] for i in range(2)]
            outs[2 * away + step // 4][place * 2 * share : (place + 1) * 2 * share] = low(
                jnp.concatenate(pieces, axis=0)
            )
            if place == 3:
                sent[2 * away + step // 4].start()
    for copy in sent:
        copy.wait()


BF = jnp.bfloat16
F32 = jnp.float32
HBM, VMEM = "hbm", "vmem"
PLACES = {
    HBM: pl.BlockSpec(memory_space=pltpu.HBM),
    VMEM: pl.BlockSpec(memory_space=pltpu.VMEM),
    "smem": pl.BlockSpec(memory_space=pltpu.SMEM),
}


def call(name, kernel, outs, args, scratch, sems, flops, limit=60):
    moved = sum(math.prod(a.shape) * 2 for _, a in args) + sum(math.prod(s) * 2 for _, s in outs)
    return pl.pallas_call(
        kernel,
        out_shape=[jax.ShapeDtypeStruct(s, BF) for _, s in outs],
        in_specs=[PLACES[place] for place, _ in args],
        out_specs=[PLACES[place] for place, _ in outs],
        scratch_shapes=[pltpu.VMEM(s, t) for s, t in scratch]
        + [pltpu.SemaphoreType.DMA((n,)) for n in sems],
        compiler_params=pltpu.CompilerParams(vmem_limit_bytes=limit * MIB),
        cost_estimate=pl.CostEstimate(flops=int(flops), bytes_accessed=moved, transcendentals=0),
        name=name,
    )(*[a for _, a in args])


def offset_forward(tokens, live, weight):
    length, features = tokens.shape
    flat, turned, wide = (length, features), (features, length), (length * features // 128, 128)
    return call(
        "offset_forward",
        forward_kernel,
        [(VMEM, wide), (HBM, turned), (HBM, turned), (HBM, (HEADS, length, length))],
        [(VMEM, tokens), (VMEM, live), (HBM, weight)],
        [
            (weight.shape, BF), (turned, BF), (flat, BF), (turned, BF), (turned, BF),
            ((HEADS, length, length), BF), ((length, length), F32), (wide, F32),
        ],
        [4, HEADS + 2],
        4e9,
    )


def offset_residuals(tokens, weight):
    length, features = tokens.shape
    flat, turned = (length, features), (features, length)
    return call(
        "offset_residuals", residual_kernel, [(VMEM, flat), (VMEM, turned), (VMEM, flat)],
        [(VMEM, tokens), (HBM, weight)], [((features, 2 * features), BF)], [2], 1e9,
    )


def cotangent_heads(places, blocks, weight):
    features = blocks[0].shape[1]
    length = sum(block.shape[0] for block in blocks)
    flat, turned = (length, features), (features, length)
    return call(
        "cotangent_heads", cotangent_kernel, [(VMEM, flat), (VMEM, turned), (VMEM, turned)],
        [("smem", places), *[(VMEM, block) for block in blocks], (HBM, weight)],
        [((features, features), BF)], [1], 5e8,
    )


def midpoint_both(core, tokens, up, up_t, live, da, weight):
    length, features = up.shape
    flat, turned, half = (length, features), (features, length), (2 * features, length)
    return call(
        "midpoint_both", middle_kernel,
        [(VMEM, tokens.shape), (HBM, flat), (HBM, turned), (HBM, half), (HBM, half)],
        [("smem", core), (VMEM, tokens), (VMEM, up), (VMEM, up_t), (VMEM, live), (VMEM, da), (HBM, weight)],
        [
            ((features, 3 * features), BF), (flat, BF), (turned, BF), (half, BF), (half, BF),
            (flat, BF), (turned, BF), (flat, BF), (turned, BF), (flat, BF), (turned, BF), ((3 * features, length), BF), ((length, length), F32), (tokens.shape, F32),
        ],
        [3, 4], 1e10,
    )


def offset_backward(core, up, weight, q, kt, v, p):
    features, length = q.shape
    half = (2 * features, length)
    return call(
        "offset_backward", backward_kernel,
        [(VMEM, (3 * features, length)), (VMEM, (length, features)), (VMEM, half), (VMEM, half)],
        [("smem", core), (VMEM, up), (HBM, weight), (HBM, q), (HBM, kt), (HBM, v), (HBM, p)],
        [
            ((features, features), BF), (q.shape, BF), (kt.shape, BF), (v.shape, BF), (p.shape, BF),
            (q.shape, BF), (q.shape, BF), (up.shape, F32),
        ],
        [1, 4], 5e9, 48,
    )


def offset_finish(tokens, up, d, weight):
    features = tokens.shape[1]
    return call(
        "offset_finish", finish_kernel, [(VMEM, tokens.shape)],
        [(VMEM, tokens), (VMEM, up), (VMEM, d), (HBM, weight)],
        [((features, 3 * features), BF)], [3], 2e9, 48,
    )[0]


def weight_terms(y, *factors):
    features = factors[2].shape[1]
    return call(
        "weight_terms", weights_kernel, [(HBM, (features // 4, features))] * 8,
        [("smem", y), *[(VMEM, factor) for factor in factors]],
        [((features // 4, features), BF)] * 8 + [((8, features // 4, features), F32)], [8], 2.5e9, 60,
    )


def add(*parts):
    total = parts[0].astype(jnp.float32)
    for part in parts[1:]:
        total = total + part.astype(jnp.float32)
    return total.astype(jnp.bfloat16)


def pick(array, index, axis):
    return lax.dynamic_index_in_dim(array, index, axis, keepdims=False)


SWAP = [(0, 1), (1, 0)]
ONWARD = [(i, (i + 1) % 4) for i in range(4)]
BACK = [(i, (i + 3) % 4) for i in range(4)]


def tie(*arrays):
    return lax.optimization_barrier(arrays)


def other_core(array):
    return lax.ppermute(array, "core", SWAP)


def ring_first(blocks):
    own0, own1, right0, right1, far0, far1, left0, left1 = blocks
    return (
        lax.ppermute(far0, "y", ONWARD),
        lax.ppermute(far1, "y", BACK),
        lax.ppermute(right1, "y", ONWARD),
        lax.ppermute(left0, "y", BACK),
    )


def ring_second(blocks, came):
    own0, own1, right0, right1, far0, far1, left0, left1 = blocks
    first = lax.ppermute(add(right0, came[0]), "y", ONWARD)
    second = lax.ppermute(add(left1, came[1]), "y", BACK)
    return add(own0, came[3], first), add(own1, came[2], second)


def last_exchange(first, second):
    rows, features = first.shape
    pieces = jnp.concatenate([first, second], axis=0).reshape(16, rows // 8, features)
    return lax.all_to_all(pieces, ("xl", "z"), split_axis=0, concat_axis=0, tiled=True)


def last_sum(*arrived):
    total = jnp.stack([jnp.sum(part.astype(jnp.float32), axis=0) for part in arrived])
    total = total.reshape(len(arrived), 2, total.shape[1] // 2, total.shape[2])
    xh = lax.axis_index("xh")
    came = lax.ppermute(pick(total, 1 - xh, 1).astype(jnp.bfloat16), "xh", SWAP)
    total = pick(total, xh, 1) + came.astype(jnp.float32)
    return [part.T for part in total]


def swap_half(block, axis, distance):
    size = lax.axis_size(axis)
    side = (lax.axis_index(axis) // distance) % 2
    halves = block.reshape(2, block.shape[0] // 2, block.shape[1])
    came = lax.ppermute(pick(halves, 1 - side, 0), axis, [(i, i ^ distance) for i in range(size)])
    return add(pick(halves, side, 0), came)


def to_rows(cotangent):
    y, xh = lax.axis_index("y"), lax.axis_index("xh")
    came = [(2 * y + xh, pick(cotangent, 2 * y + xh, 0))]
    for step in range(4):
        for turn in range(2):
            if step == turn == 0:
                continue
            perm = [
                (2 * i + j, 2 * ((i + step) % 4) + (j ^ turn)) for i in range(4) for j in range(2)
            ]
            target = 2 * ((y + step) % 4) + (xh + turn) % 2
            source = 2 * ((y + 4 - step) % 4) + (xh + turn) % 2
            came.append((source, lax.ppermute(pick(cotangent, target, 0), MID, perm)))
    return came


def local(tokens, cotangent, mask, w_offset, w_midpoint):
    off_place = lax.axis_index(OFF)
    mid_place = lax.axis_index(MID)
    core = lax.axis_index("core").reshape(1).astype(jnp.int32)
    y = lax.axis_index("y").reshape(1).astype(jnp.int32)
    rows_dev, cols_dev, features = tokens.shape
    length = mask.shape[0]
    column_live = pick(mask, mid_place * cols_dev + off_place, 1).reshape(length, 1)
    row_live = pick(mask, off_place * rows_dev + mid_place, 0).reshape(length, 1)

    def exchange(wide):
        rows = wide.reshape(length, -1, 2, 128)
        rows = lax.all_to_all(rows, OFF + MID, split_axis=0, concat_axis=0, tiled=True)
        return rows.reshape(wide.shape)

    column_tokens = lax.all_to_all(
        jnp.swapaxes(tokens, 0, 1), OFF, split_axis=0, concat_axis=0, tiled=True
    ).reshape(length, features)
    places, blocks = zip(*to_rows(cotangent))

    column_middle, q, a, p = offset_forward(column_tokens, column_live, w_offset)
    column_middle, *blocks = tie(column_middle, *blocks)
    middle = exchange(column_middle)
    row_up, row_up_t, da_mid = cotangent_heads(
        jnp.stack(places).astype(jnp.int32), blocks, w_midpoint
    )
    column_normed, kt, v = offset_residuals(column_tokens, w_offset)
    normed2, a2 = other_core(column_normed), other_core(a)
    middle, column_normed, kt, v = tie(middle, column_normed, kt, v)
    row_wide, row_normed, a_mid, keep, send = midpoint_both(
        core, middle, row_up, row_up_t, row_live, da_mid, w_midpoint
    )
    column_wide = exchange(row_wide)
    mid_blocks = weight_terms(
        y, keep, other_core(send), row_normed, other_core(row_normed), a_mid, other_core(a_mid)
    )
    mid_first = ring_first(mid_blocks)
    column_wide, normed2, a2, *mid_blocks = tie(column_wide, normed2, a2, *mid_blocks)
    d_off, column_up, keep, send = offset_backward(core, column_wide, w_offset, q, kt, v, p)
    send, *mid_first = tie(send, *mid_first)
    came = other_core(send)
    column_out = offset_finish(column_tokens, column_up, d_off, w_offset)
    mid_pair = ring_second(mid_blocks, mid_first)
    came, column_out, *mid_pair = tie(came, column_out, *mid_pair)
    off_blocks = weight_terms(y, keep, came, column_normed, normed2, a, a2)
    off_first = ring_first(off_blocks)
    arrived = lax.all_to_all(
        column_out.reshape(cols_dev, rows_dev, features), OFF, split_axis=0, concat_axis=0, tiled=True
    )
    mid_block = swap_half(jnp.concatenate(mid_pair, axis=0), "xl", 1)
    *off_first, mid_block = tie(*off_first, mid_block)
    mid_block = swap_half(mid_block, "z", 4)
    off_pair = ring_second(off_blocks, off_first)
    *off_pair, mid_block, arrived = tie(*off_pair, mid_block, arrived)
    off_arrived = last_exchange(*off_pair)
    mid_block = swap_half(swap_half(mid_block, "z", 2), "z", 1)
    grad_off_weights, grad_mid_weights = last_sum(off_arrived, mid_block[None])
    return jnp.swapaxes(arrived, 0, 1), grad_off_weights, grad_mid_weights


def solution(mesh):
    fine = Mesh(mesh.devices.reshape(2, 8, 2, 4, 2), OFF + MID)
    placed = (P(OFF, MID, None), P(OFF, MID, None), P(), P(), P())
    return jax.shard_map(
        local,
        mesh=fine,
        in_specs=placed,
        out_specs=(P(OFF, MID, None), P(None, OFF + MID), P(None, OFF + MID)),
        check_vma=False,
    )
```

```python
import math

import jax
import jax.numpy as jnp
from jax import lax
from jax.experimental import pallas as pl
from jax.experimental.pallas import tpu as pltpu
from jax.sharding import Mesh
from jax.sharding import PartitionSpec as P

HEADS = 12
WIDTH = 64
SCALE = 0.125
EPSILON = 1e-05
NEGATIVE = -1e30
OFF = ("xl", "z", "core")
MID = ("y", "xh")


NT = (((1,), (1,)), ((), ()))
MIB = 1024 * 1024


def dot(left, right):
    return jnp.dot(left, right, preferred_element_type=jnp.float32)


def dot_nt(left, right):
    return lax.dot_general(left, right, NT, preferred_element_type=jnp.float32)


def low(value):
    return value.astype(jnp.bfloat16)


def statistics(values):
    widened = values.astype(jnp.float32)
    center = jnp.mean(widened, axis=-1, keepdims=True)
    shifted = widened - center
    inverse = lax.rsqrt(jnp.mean(shifted * shifted, axis=-1, keepdims=True) + EPSILON)
    return shifted * inverse, inverse


def layer_grad(values, incoming):
    scaled, inverse = statistics(values)
    incoming = incoming.astype(jnp.float32)
    return inverse * (
        incoming
        - jnp.mean(incoming, axis=-1, keepdims=True)
        - scaled * jnp.mean(incoming * scaled, axis=-1, keepdims=True)
    )


def key_bias(live):
    length = live.shape[0]
    keys = lax.broadcasted_iota(jnp.int32, (length, length), 0)
    queries = lax.broadcasted_iota(jnp.int32, (length, length), 1)
    allowed = jnp.logical_or(live == 1, keys == queries)
    return jnp.where(allowed, 0.0, NEGATIVE)


def padded(array, head):
    rows = array[head * WIDTH : (head + 1) * WIDTH]
    blank = jnp.zeros_like(rows)
    return jnp.concatenate([rows, blank] if head % 2 == 0 else [blank, rows], axis=0)


def pair(head):
    start = (head // 2) * 2 * WIDTH
    return slice(start, start + 2 * WIDTH)


def own(head):
    return slice(head * WIDTH, (head + 1) * WIDTH)


def softmax_keys(scores):
    expanded = jnp.exp(scores - jnp.max(scores, axis=0, keepdims=True))
    return expanded * (1.0 / jnp.sum(expanded, axis=0, keepdims=True))


def fetch(weight_hbm, weight_ref, sems, *parts):
    features = weight_hbm.shape[0]
    copies = {}
    for place, part in enumerate(parts):
        columns = slice(part * features, (part + 1) * features)
        copies[part] = pltpu.make_async_copy(
            weight_hbm.at[:, columns],
            weight_ref.at[:, place * features : (place + 1) * features],
            sems.at[place],
        )
        copies[part].start()
    return copies


def columns(weight_ref, place):
    features = weight_ref.shape[0]
    return weight_ref[:, place * features : (place + 1) * features]


def encode(rows, wide_ref, out_ref):
    chunks = rows.shape[1] // 128
    for c in range(chunks):
        wide_ref[pl.ds(c, rows.shape[0], stride=chunks), :] = rows[:, c * 128 : (c + 1) * 128]
    out_ref[...] = low(wide_ref[...])


def decode(in_ref, wide_ref, rows_ref):
    length, features = rows_ref.shape
    chunks = features // 128
    wide_ref[...] = in_ref[...].astype(jnp.float32)
    for c in range(chunks):
        rows_ref[:, c * 128 : (c + 1) * 128] = low(wide_ref[pl.ds(c, length, stride=chunks), :])


def encode_midpoints(rows, wide_ref, out_ref):
    chunks = rows.shape[1] // 128
    for m in range(8):
        for c in range(chunks):
            wide_ref[pl.ds(m * chunks + c, 32, stride=8 * chunks), :] = rows[
                m * 32 : (m + 1) * 32, c * 128 : (c + 1) * 128
            ]
    out_ref[...] = low(wide_ref[...])


def decode_midpoints(in_ref, wide_ref, rows_ref):
    chunks = rows_ref.shape[1] // 128
    wide_ref[...] = in_ref[...].astype(jnp.float32)
    for m in range(8):
        for c in range(chunks):
            rows_ref[m * 32 : (m + 1) * 32, c * 128 : (c + 1) * 128] = low(
                wide_ref[pl.ds(m * chunks + c, 32, stride=8 * chunks), :]
            )


def forward_kernel(
    tokens_ref, live_ref, weight_hbm, out_ref, q_hbm, a_hbm, p_hbm,
    weight_ref, q_ref, k_ref, v_ref, a_ref, p_ref, bias_ref, wide_ref, sems, out_sems,
):
    copies = fetch(weight_hbm, weight_ref, sems, 1, 0, 2, 3)
    bias_ref[...] = key_bias(live_ref[...])
    normed = low(statistics(tokens_ref[...])[0])
    copies[1].wait()
    k_ref[...] = low(dot(normed, columns(weight_ref, 0)))
    copies[0].wait()
    q_ref[...] = (low(dot(normed, columns(weight_ref, 1))) * SCALE).T
    copies[2].wait()
    v_ref[...] = low(dot(normed, columns(weight_ref, 2))).T
    sent = [pltpu.make_async_copy(q_ref, q_hbm, out_sems.at[HEADS])]
    sent[0].start()
    for head in range(HEADS):
        scores = dot(k_ref[:, pair(head)], padded(q_ref, head)) + bias_ref[...]
        p = low(softmax_keys(scores))
        p_ref[head] = p
        sent.append(pltpu.make_async_copy(p_ref.at[head], p_hbm.at[head], out_sems.at[head]))
        sent[-1].start()
        a_ref[own(head)] = low(dot(v_ref[own(head)], p))
    sent.append(pltpu.make_async_copy(a_ref, a_hbm, out_sems.at[HEADS + 1]))
    sent[-1].start()
    copies[3].wait()
    out = low(dot(a_ref[...].T, columns(weight_ref, 3)))
    encode(tokens_ref[...].astype(jnp.float32) + out.astype(jnp.float32), wide_ref, out_ref)
    for copy in sent:
        copy.wait()


def residual_kernel(tokens_ref, weight_hbm, normed_ref, kt_ref, v_ref, weight_ref, sems):
    copies = fetch(weight_hbm, weight_ref, sems, 1, 2)
    normed = low(statistics(tokens_ref[...])[0])
    normed_ref[...] = normed
    copies[1].wait()
    kt_ref[...] = low(dot(normed, columns(weight_ref, 0))).T
    copies[2].wait()
    v_ref[...] = low(dot(normed, columns(weight_ref, 1)))


def cotangent_kernel(place_ref, *refs):
    *blocks, weight_hbm, up_ref, upt_ref, da_ref, weight_ref, sems = refs
    copies = fetch(weight_hbm, weight_ref, sems, 3)
    for i, block in enumerate(blocks):
        size = block.shape[0]
        up_ref[pl.ds(pl.multiple_of(place_ref[i] * size, size), size), :] = block[...]
    upt_ref[...] = up_ref[...].T
    copies[3].wait()
    da_ref[...] = low(dot_nt(weight_ref[...], up_ref[...]))


def divide(core, d_ref, upt_ref, keep_ref, send_ref):
    group = 96
    first = d_ref.shape[0] // (2 * group)
    for out_ref, which in ((send_ref, 1 - core), (keep_ref, core)):
        for step in range(out_ref.shape[0] // group):
            source, at = (d_ref, step) if step < first else (upt_ref, step - first)
            start = pl.multiple_of((2 * at + which) * group, group)
            out_ref[step * group : (step + 1) * group] = source[pl.ds(start, group), :]


def head_grad(head, p, p_low, q_ref, kt_ref, v_ref, da_ref, d_ref):
    features = da_ref.shape[0]
    dp = dot(v_ref[:, pair(head)], padded(da_ref, head))
    ds = low(p * (dp - jnp.sum(p * dp, axis=0, keepdims=True)))
    d_ref[own(head)] = low(dot(kt_ref[own(head)], ds) * SCALE)
    d_ref[features + head * WIDTH : features + (head + 1) * WIDTH] = low(dot_nt(q_ref[own(head)], ds))
    d_ref[2 * features + head * WIDTH : 2 * features + (head + 1) * WIDTH] = low(
        dot_nt(da_ref[own(head)], p_low)
    )


def middle_kernel(
    core_ref, tokens_ref, up_ref, upt_ref, live_ref, da_ref, weight_hbm,
    out_ref, normed_hbm, a_hbm, keep_hbm, send_hbm,
    weight_ref, normed_ref, a_ref, keep_ref, send_ref, rows_ref, q_ref, k_ref, kt_ref, v_ref, vt_ref, d_ref, bias_ref, wide_ref, sems, out_sems,
):
    copies = fetch(weight_hbm, weight_ref, sems, 0, 1, 2)
    bias_ref[...] = key_bias(live_ref[...])
    decode_midpoints(tokens_ref, wide_ref, rows_ref)
    normed = low(statistics(rows_ref[...])[0])
    normed_ref[...] = normed
    sent = [
        pltpu.make_async_copy(source, target, out_sems.at[i])
        for i, (source, target) in enumerate(
            ((normed_ref, normed_hbm), (a_ref, a_hbm), (keep_ref, keep_hbm), (send_ref, send_hbm))
        )
    ]
    sent[0].start()
    copies[0].wait()
    q_ref[...] = (low(dot(normed, columns(weight_ref, 0))) * SCALE).T
    copies[1].wait()
    k_ref[...] = low(dot(normed, columns(weight_ref, 1)))
    kt_ref[...] = k_ref[...].T
    copies[2].wait()
    v_ref[...] = low(dot(normed, columns(weight_ref, 2)))
    vt_ref[...] = v_ref[...].T
    for head in range(HEADS):
        scores = dot(k_ref[:, pair(head)], padded(q_ref, head)) + bias_ref[...]
        p = softmax_keys(scores)
        p_low = low(p)
        a_ref[own(head)] = low(dot(vt_ref[own(head)], p_low))
        head_grad(head, p, p_low, q_ref, kt_ref, v_ref, da_ref, d_ref)
    sent[1].start()
    divide(core_ref[0], d_ref, upt_ref, keep_ref, send_ref)
    sent[2].start()
    sent[3].start()
    dh = low(dot(weight_ref[...], d_ref[...])).T
    encode_midpoints(
        up_ref[...].astype(jnp.float32) + layer_grad(rows_ref[...], dh), wide_ref, out_ref
    )
    for copy in sent:
        copy.wait()


def backward_kernel(
    core_ref, up_ref, weight_hbm, q_hbm, kt_hbm, v_hbm, p_hbm,
    d_ref, rows_ref, keep_ref, send_ref,
    weight_ref, q_ref, kt_ref, v_ref, p_ref, da_ref, upt_ref, wide_ref, sems, in_sems,
):
    copies = fetch(weight_hbm, weight_ref, sems, 3)
    moved = [
        pltpu.make_async_copy(source, target, in_sems.at[i])
        for i, (source, target) in enumerate(
            ((v_hbm, v_ref), (p_hbm, p_ref), (kt_hbm, kt_ref), (q_hbm, q_ref))
        )
    ]
    for copy in moved:
        copy.start()
    decode(up_ref, wide_ref, rows_ref)
    copies[3].wait()
    da_ref[...] = low(dot_nt(weight_ref[...], rows_ref[...]))
    upt_ref[...] = rows_ref[...].T
    for copy in moved:
        copy.wait()
    for head in range(HEADS):
        p_low = p_ref[head]
        head_grad(head, p_low.astype(jnp.float32), p_low, q_ref, kt_ref, v_ref, da_ref, d_ref)
    divide(core_ref[0], d_ref, upt_ref, keep_ref, send_ref)


def finish_kernel(tokens_ref, up_ref, d_ref, weight_hbm, out_ref, weight_ref, sems):
    features = tokens_ref.shape[1]
    copies = fetch(weight_hbm, weight_ref, sems, 0, 1, 2)
    total = None
    for part in range(3):
        copies[part].wait()
        term = dot(columns(weight_ref, part), d_ref[part * features : (part + 1) * features])
        total = term if total is None else total + term
    out_ref[...] = low(up_ref[...].astype(jnp.float32) + layer_grad(tokens_ref[...], low(total).T))


def weights_kernel(y_ref, d_ref, d2_ref, normed_ref, normed2_ref, a_ref, a2_ref, *refs):
    outs_hbm, outs, (sums_ref, sems) = refs[:8], refs[8:16], refs[16:]
    sent = [pltpu.make_async_copy(outs[i], outs_hbm[i], sems.at[i]) for i in range(8)]
    y, group, share = y_ref[0], 96, 24
    first = 3 * normed_ref.shape[1] // (2 * group)
    for step in range(8):
        rows = slice(step * 2 * group, (step + 1) * 2 * group)
        if 2 * step < first:
            sums = dot(d_ref[rows], normed_ref[...]) + dot(d2_ref[rows], normed2_ref[...])
        else:
            sums = dot_nt(d_ref[rows], a_ref[...]) + dot_nt(d2_ref[rows], a2_ref[...])
        sums_ref[step] = sums
        place = step % 4
        for away in range(4):
            start = pl.multiple_of(lax.rem(y + away, 4) * share, 8)
            pieces = [sums_ref[step, pl.ds(start + i * group, share), :] for i in range(2)]
            outs[2 * away + step // 4][place * 2 * share : (place + 1) * 2 * share] = low(
                jnp.concatenate(pieces, axis=0)
            )
            if place == 3:
                sent[2 * away + step // 4].start()
    for copy in sent:
        copy.wait()


BF = jnp.bfloat16
F32 = jnp.float32
HBM, VMEM = "hbm", "vmem"
PLACES = {
    HBM: pl.BlockSpec(memory_space=pltpu.HBM),
    VMEM: pl.BlockSpec(memory_space=pltpu.VMEM),
    "smem": pl.BlockSpec(memory_space=pltpu.SMEM),
}


def call(name, kernel, outs, args, scratch, sems, flops, limit=60):
    moved = sum(math.prod(a.shape) * 2 for _, a in args) + sum(math.prod(s) * 2 for _, s in outs)
    return pl.pallas_call(
        kernel,
        out_shape=[jax.ShapeDtypeStruct(s, BF) for _, s in outs],
        in_specs=[PLACES[place] for place, _ in args],
        out_specs=[PLACES[place] for place, _ in outs],
        scratch_shapes=[pltpu.VMEM(s, t) for s, t in scratch]
        + [pltpu.SemaphoreType.DMA((n,)) for n in sems],
        compiler_params=pltpu.CompilerParams(vmem_limit_bytes=limit * MIB),
        cost_estimate=pl.CostEstimate(flops=int(flops), bytes_accessed=moved, transcendentals=0),
        name=name,
    )(*[a for _, a in args])


def offset_forward(tokens, live, weight):
    length, features = tokens.shape
    flat, turned, wide = (length, features), (features, length), (length * features // 128, 128)
    return call(
        "offset_forward",
        forward_kernel,
        [(VMEM, wide), (HBM, turned), (HBM, turned), (HBM, (HEADS, length, length))],
        [(VMEM, tokens), (VMEM, live), (HBM, weight)],
        [
            (weight.shape, BF), (turned, BF), (flat, BF), (turned, BF), (turned, BF),
            ((HEADS, length, length), BF), ((length, length), F32), (wide, F32),
        ],
        [4, HEADS + 2],
        4e9,
    )


def offset_residuals(tokens, weight):
    length, features = tokens.shape
    flat, turned = (length, features), (features, length)
    return call(
        "offset_residuals", residual_kernel, [(VMEM, flat), (VMEM, turned), (VMEM, flat)],
        [(VMEM, tokens), (HBM, weight)], [((features, 2 * features), BF)], [2], 1e9,
    )


def cotangent_heads(places, blocks, weight):
    features = blocks[0].shape[1]
    length = sum(block.shape[0] for block in blocks)
    flat, turned = (length, features), (features, length)
    return call(
        "cotangent_heads", cotangent_kernel, [(VMEM, flat), (VMEM, turned), (VMEM, turned)],
        [("smem", places), *[(VMEM, block) for block in blocks], (HBM, weight)],
        [((features, features), BF)], [1], 5e8,
    )


def midpoint_both(core, tokens, up, up_t, live, da, weight):
    length, features = up.shape
    flat, turned, half = (length, features), (features, length), (2 * features, length)
    return call(
        "midpoint_both", middle_kernel,
        [(VMEM, tokens.shape), (HBM, flat), (HBM, turned), (HBM, half), (HBM, half)],
        [("smem", core), (VMEM, tokens), (VMEM, up), (VMEM, up_t), (VMEM, live), (VMEM, da), (HBM, weight)],
        [
            ((features, 3 * features), BF), (flat, BF), (turned, BF), (half, BF), (half, BF),
            (flat, BF), (turned, BF), (flat, BF), (turned, BF), (flat, BF), (turned, BF), ((3 * features, length), BF), ((length, length), F32), (tokens.shape, F32),
        ],
        [3, 4], 1e10,
    )


def offset_backward(core, up, weight, q, kt, v, p):
    features, length = q.shape
    half = (2 * features, length)
    return call(
        "offset_backward", backward_kernel,
        [(VMEM, (3 * features, length)), (VMEM, (length, features)), (VMEM, half), (VMEM, half)],
        [("smem", core), (VMEM, up), (HBM, weight), (HBM, q), (HBM, kt), (HBM, v), (HBM, p)],
        [
            ((features, features), BF), (q.shape, BF), (kt.shape, BF), (v.shape, BF), (p.shape, BF),
            (q.shape, BF), (q.shape, BF), (up.shape, F32),
        ],
        [1, 4], 5e9, 48,
    )


def offset_finish(tokens, up, d, weight):
    features = tokens.shape[1]
    return call(
        "offset_finish", finish_kernel, [(VMEM, tokens.shape)],
        [(VMEM, tokens), (VMEM, up), (VMEM, d), (HBM, weight)],
        [((features, 3 * features), BF)], [3], 2e9, 48,
    )[0]


def weight_terms(y, *factors):
    features = factors[2].shape[1]
    return call(
        "weight_terms", weights_kernel, [(HBM, (features // 4, features))] * 8,
        [("smem", y), *[(VMEM, factor) for factor in factors]],
        [((features // 4, features), BF)] * 8 + [((8, features // 4, features), F32)], [8], 2.5e9, 60,
    )


def add(*parts):
    total = parts[0].astype(jnp.float32)
    for part in parts[1:]:
        total = total + part.astype(jnp.float32)
    return total.astype(jnp.bfloat16)


def pick(array, index, axis):
    return lax.dynamic_index_in_dim(array, index, axis, keepdims=False)


SWAP = [(0, 1), (1, 0)]
ONWARD = [(i, (i + 1) % 4) for i in range(4)]
BACK = [(i, (i + 3) % 4) for i in range(4)]


def tie(*arrays):
    return lax.optimization_barrier(arrays)


def other_core(array):
    return lax.ppermute(array, "core", SWAP)


def ring_first(blocks):
    own0, own1, right0, right1, far0, far1, left0, left1 = blocks
    return (
        lax.ppermute(far0, "y", ONWARD),
        lax.ppermute(far1, "y", BACK),
        lax.ppermute(right1, "y", ONWARD),
        lax.ppermute(left0, "y", BACK),
    )


def ring_second(blocks, came):
    own0, own1, right0, right1, far0, far1, left0, left1 = blocks
    first = lax.ppermute(add(right0, came[0]), "y", ONWARD)
    second = lax.ppermute(add(left1, came[1]), "y", BACK)
    return add(own0, came[3], first), add(own1, came[2], second)


def last_exchange(first, second):
    rows, features = first.shape
    pieces = jnp.concatenate([first, second], axis=0).reshape(16, rows // 8, features)
    return lax.all_to_all(pieces, ("xl", "z"), split_axis=0, concat_axis=0, tiled=True)


def last_sum(*arrived):
    total = jnp.stack([jnp.sum(part.astype(jnp.float32), axis=0) for part in arrived])
    total = total.reshape(len(arrived), 2, total.shape[1] // 2, total.shape[2])
    xh = lax.axis_index("xh")
    came = lax.ppermute(pick(total, 1 - xh, 1).astype(jnp.bfloat16), "xh", SWAP)
    total = pick(total, xh, 1) + came.astype(jnp.float32)
    return [part.T for part in total]


def swap_half(block, axis, distance, chunks):
    size = lax.axis_size(axis)
    side = (lax.axis_index(axis) // distance) % 2
    rows, features = block.shape
    halves = block.reshape(chunks // 2, 2, rows // chunks, features)
    came = lax.ppermute(pick(halves, 1 - side, 1), axis, [(i, i ^ distance) for i in range(size)])
    return add(pick(halves, side, 1), came).reshape(rows // 2, features)


def to_rows(cotangent):
    y, xh = lax.axis_index("y"), lax.axis_index("xh")
    came = [(2 * y + xh, pick(cotangent, 2 * y + xh, 0))]
    for step in range(4):
        for turn in range(2):
            if step == turn == 0:
                continue
            perm = [
                (2 * i + j, 2 * ((i + step) % 4) + (j ^ turn)) for i in range(4) for j in range(2)
            ]
            target = 2 * ((y + step) % 4) + (xh + turn) % 2
            source = 2 * ((y + 4 - step) % 4) + (xh + turn) % 2
            came.append((source, lax.ppermute(pick(cotangent, target, 0), MID, perm)))
    return came


def local(tokens, cotangent, mask, w_offset, w_midpoint):
    off_place = lax.axis_index(OFF)
    mid_place = lax.axis_index(MID)
    core = lax.axis_index("core").reshape(1).astype(jnp.int32)
    y = lax.axis_index("y").reshape(1).astype(jnp.int32)
    rows_dev, cols_dev, features = tokens.shape
    length = mask.shape[0]
    column_live = pick(mask, mid_place * cols_dev + off_place, 1).reshape(length, 1)
    row_live = pick(mask, off_place * rows_dev + mid_place, 0).reshape(length, 1)

    def exchange(wide):
        rows = wide.reshape(length, -1, 2, 128)
        rows = lax.all_to_all(rows, OFF + MID, split_axis=0, concat_axis=0, tiled=True)
        return rows.reshape(wide.shape)

    column_tokens = lax.all_to_all(
        jnp.swapaxes(tokens, 0, 1), OFF, split_axis=0, concat_axis=0, tiled=True
    ).reshape(length, features)
    places, blocks = zip(*to_rows(cotangent))

    column_middle, q, a, p = offset_forward(column_tokens, column_live, w_offset)
    column_middle, *blocks = tie(column_middle, *blocks)
    middle = exchange(column_middle)
    row_up, row_up_t, da_mid = cotangent_heads(
        jnp.stack(places).astype(jnp.int32), blocks, w_midpoint
    )
    column_normed, kt, v = offset_residuals(column_tokens, w_offset)
    normed2, a2 = other_core(column_normed), other_core(a)
    middle, column_normed, kt, v = tie(middle, column_normed, kt, v)
    row_wide, row_normed, a_mid, keep, send = midpoint_both(
        core, middle, row_up, row_up_t, row_live, da_mid, w_midpoint
    )
    column_wide = exchange(row_wide)
    mid_blocks = weight_terms(
        y, keep, other_core(send), row_normed, other_core(row_normed), a_mid, other_core(a_mid)
    )
    mid_first = ring_first(mid_blocks)
    column_wide, normed2, a2, *mid_blocks = tie(column_wide, normed2, a2, *mid_blocks)
    d_off, column_up, keep, send = offset_backward(core, column_wide, w_offset, q, kt, v, p)
    send, *mid_first = tie(send, *mid_first)
    came = other_core(send)
    column_out = offset_finish(column_tokens, column_up, d_off, w_offset)
    mid_pair = ring_second(mid_blocks, mid_first)
    came, column_out, *mid_pair = tie(came, column_out, *mid_pair)
    off_blocks = weight_terms(y, keep, came, column_normed, normed2, a, a2)
    off_first = ring_first(off_blocks)
    arrived = lax.all_to_all(
        column_out.reshape(cols_dev, rows_dev, features), OFF, split_axis=0, concat_axis=0, tiled=True
    )
    mid_block = swap_half(jnp.concatenate(mid_pair, axis=0), "xl", 1, 2)
    *off_first, mid_block = tie(*off_first, mid_block)
    mid_block = swap_half(mid_block, "z", 1, 8)
    off_pair = ring_second(off_blocks, off_first)
    *off_pair, mid_block, arrived = tie(*off_pair, mid_block, arrived)
    off_arrived = last_exchange(*off_pair)
    mid_block = swap_half(swap_half(mid_block, "z", 2, 4), "z", 4, 2)
    grad_off_weights, grad_mid_weights = last_sum(off_arrived, mid_block[None])
    return jnp.swapaxes(arrived, 0, 1), grad_off_weights, grad_mid_weights


def solution(mesh):
    fine = Mesh(mesh.devices.reshape(2, 8, 2, 4, 2), OFF + MID)
    placed = (P(OFF, MID, None), P(OFF, MID, None), P(), P(), P())
    return jax.shard_map(
        local,
        mesh=fine,
        in_specs=placed,
        out_specs=(P(OFF, MID, None), P(None, OFF + MID), P(None, OFF + MID)),
        check_vma=False,
    )
```
